512 devices in a mesh: wn: 4 (over x_hi, core), sx: 8 (over y), az: 16 (over z, x_lo).
Axes of the slice: x: 4 (x_hi: 2, x_lo: 2; x = x_hi * 2 + x_lo), y: 8, z: 8, core: 2. Of those that a mesh axis runs over, the one named last changes fastest.
Arguments:
- fields: float32 [5, 64, 128, 1024], P(None, 'wn', 'az', 'sx'), as said below
- shock_height: float32 [128, 1024], P('az', 'sx'), may hold values from 0.5 to 1.5
- behind_shock: float32 [5, 128, 1024], P(None, 'az', 'sx'), as said below
Outputs:
- fields_next: float32 [5, 64, 128, 1024], P(None, 'wn', 'az', 'sx')
- height_next: float32 [128, 1024], P('az', 'sx')
The draws below stay inside these ranges and needn't reach their ends.
Inputs may be any that keep to these rules, and one draw needn't show every extreme that they name: `fields`: built from densities in 0.7 to 1.3, pressures in 0.6 to 1.4 and velocity components of magnitude at most 0.3 in each cell. `behind_shock`: built from densities in 0.7 to 1.3, pressures in 0.6 to 1.4 and velocity components of magnitude at most 0.3 at each surface point.
All inputs are finite; a program needn't handle non-finite values.
Results may differ from the reference program's by a relative error of at most 0.00002.
Values sent between devices are 32-bit elements; how exact they have to be, the bound alone decides.
No kernel may reach another device: no remote copies, remote signals or barrier semaphores. Data moves between devices by JAX's collectives and lax.ppermute only.
A program may use at most 64 MiB of HBM per device.

```python
import math
import jax
import jax.numpy as jnp
from jax import lax

NW = 64
NA = 128
NS = 1024


GAMMA = 1.4


def conserved_state(density, axial_speed, normal_speed, around_speed, pressure):
    kinetic = 0.5 * density * (axial_speed ** 2 + normal_speed ** 2 + around_speed ** 2)
    return jnp.stack([density, density * axial_speed, density * normal_speed, density * around_speed, pressure / (GAMMA - 1.0) + kinetic])


def draw_fields(key, part):
    key = jax.random.fold_in(key, 11)
    key_list = jax.random.split(key, 5)
    shape_cells = (NW, NA, NS)
    density = jax.random.uniform(key_list[0], shape_cells, minval=0.7, maxval=1.3)
    axial_speed = jnp.clip(0.1 * jax.random.normal(key_list[1], shape_cells), -0.3, 0.3)
    normal_speed = jnp.clip(0.1 * jax.random.normal(key_list[2], shape_cells), -0.3, 0.3)
    around_speed = jnp.clip(0.1 * jax.random.normal(key_list[3], shape_cells), -0.3, 0.3)
    pressure = jax.random.uniform(key_list[4], shape_cells, minval=0.6, maxval=1.4)
    return conserved_state(density, axial_speed, normal_speed, around_speed, pressure).astype(jnp.float32)


def draw_behind_shock(key, part):
    key = jax.random.fold_in(key, 12)
    key_list = jax.random.split(key, 5)
    shape_cells = (NA, NS)
    density = jax.random.uniform(key_list[0], shape_cells, minval=0.7, maxval=1.3)
    axial_speed = jnp.clip(0.1 * jax.random.normal(key_list[1], shape_cells), -0.3, 0.3)
    normal_speed = jnp.clip(0.1 * jax.random.normal(key_list[2], shape_cells), -0.3, 0.3)
    around_speed = jnp.clip(0.1 * jax.random.normal(key_list[3], shape_cells), -0.3, 0.3)
    pressure = jax.random.uniform(key_list[4], shape_cells, minval=0.6, maxval=1.4)
    return conserved_state(density, axial_speed, normal_speed, around_speed, pressure).astype(jnp.float32)


def draw_shock_height(key, part):
    key = jax.random.fold_in(key, 13)
    key_list = jax.random.split(key, 2)
    axial_pos = (jnp.arange(NS, dtype=jnp.float32) + 0.5) / NS
    around_pos = jnp.arange(NA, dtype=jnp.float32) / NA
    phases = jax.random.uniform(key_list[0], (2,), minval=-math.pi, maxval=math.pi)
    amplitude = min(0.15, 0.04 * NA / NW)
    smooth = 0.85 + 0.3 * axial_pos[None, :]
    smooth = smooth + amplitude * jnp.cos(4.0 * math.pi * around_pos + phases[0])[:, None]
    smooth = smooth + 0.1 * jnp.cos(2.0 * math.pi * axial_pos + phases[1])[None, :]
    rough_size = min(1.5 / NW, 0.09)
    rough = rough_size * jax.random.uniform(key_list[1], (NA, NS), minval=-1.0, maxval=1.0)
    return (smooth + rough).astype(jnp.float32)


def setup_inputs(seed: int = 0) -> dict:
    seeds = jax.random.split(jax.random.key(seed), 4)
    return {
        "fields": draw_fields(jax.random.fold_in(seeds[3], 71), 0),
        "shock_height": draw_shock_height(jax.random.fold_in(seeds[3], 71), 0),
        "behind_shock": draw_behind_shock(jax.random.fold_in(seeds[3], 71), 0),
    }


GAMMA = 1.4
CFL_STEP = 0.08

def differ(values, axis_index, factor):
    length = values.shape[axis_index] - 4

    def shifted(offset):
        return lax.slice_in_dim(values, offset, offset + length, axis=axis_index)
    return (shifted(0) - 8.0 * shifted(1) + 8.0 * shifted(3) - shifted(4)) * (factor / 12.0)

def pressure(conserved):
    kinetic = (conserved[1] ** 2 + conserved[2] ** 2 + conserved[3] ** 2) / conserved[0]
    return (GAMMA - 1.0) * (conserved[4] - 0.5 * kinetic)

def direction_flux(conserved, component):
    velocity = conserved[component] / conserved[0]
    pressure_now = pressure(conserved)
    pieces = [conserved[component]]
    for moment in (1, 2, 3):
        product = conserved[moment] * velocity
        if moment == component:
            product = product + pressure_now
        pieces.append(product)
    pieces.append((conserved[4] + pressure_now) * velocity)
    return jnp.stack(pieces)

def shock_speed(top_row, behind):
    behind_pressure = pressure(behind)
    return (pressure(top_row) - behind_pressure) / jnp.sqrt(GAMMA * behind_pressure * behind[0])

def tendency(normal_slab, axial_slab, around_slab, height, slope_axial, slope_around, speed_now, height_frac, layers):
    axial_term = differ(direction_flux(axial_slab, 1), 3, layers)
    around_term = differ(direction_flux(around_slab, 3), 2, layers)
    normal_axial = differ(direction_flux(normal_slab, 1), 1, layers)
    normal_wall = differ(direction_flux(normal_slab, 2), 1, layers)
    normal_around = differ(direction_flux(normal_slab, 3), 1, layers)
    normal_state = differ(normal_slab, 1, layers)
    inverse = 1.0 / height
    moving = slope_axial * normal_axial + slope_around * normal_around + speed_now * normal_state
    return -axial_term - around_term - inverse * normal_wall + height_frac * inverse * moving

def surface_pad(surface):
    wrapped = jnp.pad(surface, ((2, 2), (0, 0)), mode='wrap')
    return jnp.pad(wrapped, ((0, 0), (2, 2)), mode='edge')

def rate(state, height, speed_now, behind, height_frac):
    layers = state.shape[1]
    mirror = jnp.array([1.0, -1.0, -1.0, -1.0, 1.0], dtype=state.dtype).reshape(5, 1, 1, 1)
    wall_ghost = mirror * state[:, 1::-1]
    shock_ghost = jnp.broadcast_to(behind[:, None], (5, 2) + behind.shape[1:])
    normal_slab = jnp.concatenate([wall_ghost, state, shock_ghost], axis=1)
    axial_slab = jnp.pad(state, ((0, 0), (0, 0), (0, 0), (2, 2)), mode='edge')
    around_slab = jnp.pad(state, ((0, 0), (0, 0), (2, 2), (0, 0)), mode='wrap')
    height_pad = surface_pad(height)
    slope_axial = differ(height_pad[2:-2], 1, layers)
    slope_around = differ(height_pad[:, 2:-2], 0, layers)
    return tendency(normal_slab, axial_slab, around_slab, height, slope_axial, slope_around, speed_now, height_frac, layers)

def reference(fields, shock_height, behind_shock):
    layers = fields.shape[1]
    time_step = CFL_STEP / layers
    height_frac = ((jnp.arange(layers, dtype=jnp.float32) + 0.5) / layers)[None, :, None, None]
    speed_first = shock_speed(fields[:, -1], behind_shock)
    section_one = fields + time_step * rate(fields, shock_height, speed_first, behind_shock, height_frac)
    height_one = shock_height + time_step * speed_first
    speed_second = shock_speed(section_one[:, -1], behind_shock)
    second_rate = rate(section_one, height_one, speed_second, behind_shock, height_frac)
    fields_next = 0.5 * (fields + section_one + time_step * second_rate)
    height_next = 0.5 * (shock_height + height_one + time_step * speed_second)
    return (fields_next, height_next)
```

```python
import functools

import jax
import jax.numpy as jnp
from jax import lax
from jax.experimental import pallas as pl
from jax.experimental.pallas import tpu as pltpu
from jax.sharding import PartitionSpec as P

GAMMA = 1.4
CFL_STEP = 0.08
LAYERS = 64
NL = 16
NP = 86
HALF = 43
SCALE = LAYERS / 12.0
STEP = CFL_STEP / LAYERS
C = CFL_STEP / 12.0
VM = pl.BlockSpec(memory_space=pltpu.VMEM)
F32 = jnp.float32
MIRROR = (1.0, -1.0, -1.0, -1.0, 1.0)


def lane():
    return lax.broadcasted_iota(jnp.int32, (8, 128), 1)


def row():
    return lax.broadcasted_iota(jnp.int32, (8, 128), 0)


def rl(x, shift):
    return pltpu.roll(x, shift % 128, 1) if shift % 128 else x


def rs(x, shift):
    return pltpu.roll(x, shift % 8, 0) if shift % 8 else x


def d_lane(x):
    return (rl(x, 2) - rl(x, -2)) + 8.0 * (rl(x, -1) - rl(x, 1))


def strip_patch(d):
    off = lane() & 15
    return jnp.where((off == 12) | (off == 13), rl(d, 8), d)


def strip_ends(x):
    off = lane() & 15
    return jnp.where((off == 10) | (off == 11), rl(x, 8), x)


def d_ends(x, e):
    ln = lane()
    p1 = rl(jnp.where(ln < 1, e, x), -1)
    p2 = rl(jnp.where(ln < 2, e, x), -2)
    m1 = rl(jnp.where(ln >= 127, e, x), 1)
    m2 = rl(jnp.where(ln >= 126, e, x), 2)
    return (m2 - p2) + 8.0 * (p1 - m1)


def patched(d, patch):
    ln = lane()
    return jnp.where((ln < 2) | (ln >= 126), patch, d)


def ring(x, z, shift):
    keep = row() >= shift if shift > 0 else row() < 8 + shift
    a, b = rs(x, shift), rs(z, shift)
    return jnp.where(keep, a, b), jnp.where(keep, b, a)


def d_ring(x, z):
    m2, m1, p1, p2 = ring(x, z, 2), ring(x, z, 1), ring(x, z, -1), ring(x, z, -2)
    return tuple((m2[i] - p2[i]) + 8.0 * (p1[i] - m1[i]) for i in (0, 1))


def spread(x, group):
    ln = lane()
    x = rl(x, -16 * group)
    x = jnp.where(ln < 16, x, rl(x, 16))
    x = jnp.where(ln < 32, x, rl(x, 32))
    return jnp.where(ln < 64, x, rl(x, 64))


def pressure(q):
    kinetic = (q[1] * q[1] + q[2] * q[2] + q[3] * q[3]) / q[0]
    return (GAMMA - 1.0) * (q[4] - 0.5 * kinetic)


def speed(q, b):
    behind = pressure(b)
    return (pressure(q) - behind) / jnp.sqrt(GAMMA * behind * b[0])


def fluxes(q, want=(1, 2, 3)):
    inv = 1.0 / q[0]
    v = [None, q[1] * inv, q[2] * inv, q[3] * inv]
    q11, q22, q33 = q[1] * v[1], q[2] * v[2], q[3] * v[3]
    p = (GAMMA - 1.0) * (q[4] - 0.5 * (q11 + q22 + q33))
    e = q[4] + p
    out = []
    if 1 in want:
        out.append([q[1], q11 + p, q[2] * v[1], q[3] * v[1], e * v[1]])
    if 2 in want:
        out.append([q[2], q[1] * v[2], q22 + p, q[3] * v[2], e * v[2]])
    if 3 in want:
        out.append([q[3], q[1] * v[3], q[2] * v[3], q33 + p, e * v[3]])
    return out


def moving(f1, f3, q, hx, hz, w):
    return [hx * f1[f] + hz * f3[f] + w * q[f] for f in range(5)]


def slopes(h, hz, hs, hsz):
    ds, dsz = d_lane(hs), d_lane(hsz)
    x = SCALE * patched(d_lane(h), rl(strip_patch(ds), -12))
    xz = SCALE * patched(d_lane(hz), rl(strip_patch(dsz), -12))
    a, az = d_ring(h, hz)
    s, _ = d_ring(hs, hsz)
    return (x, SCALE * a), (xz, SCALE * az), (SCALE * ds, SCALE * s)


def plane_of(q, h, b):
    def get(i):
        if i < 80:
            return q[i // NL, i % NL]
        return h[...] if i == 80 else b[i - 81]

    return get


def pack_rows(q, h, b, up, dn):
    get = plane_of(q, h, b)
    high = row() >= 4
    for i in range(HALF):
        x, y = get(i), rs(get(i + HALF), 4)
        up[i] = jnp.where(high, x, y)
        dn[i] = jnp.where(high, y, x)


def pack_columns(q, h, b, u, d, z, right, left):
    get = plane_of(q, h, b)
    high = row() >= 4
    ln = lane()
    for i in range(HALF):
        x, y = u[i], d[i]
        z[i] = jnp.where(high, x, y)
        z[i + HALF] = rs(jnp.where(high, y, x), 4)
    for v in range(6):
        r_acc = jnp.zeros((8, 128), F32)
        l_acc = jnp.zeros((8, 128), F32)
        slots = (
            [(j, t, v * NL + j + 8 * (t & 1), t >= 2) for j in range(8) for t in range(4)]
            if v < 5
            else [(j, t, 80 + j, t >= 2) for j in range(6) for t in (0, 2)]
        )
        for j, t, i, halo in slots:
            at = 16 * j + 4 * t
            x = rl(z[i] if halo else get(i), at + 4)
            r_acc = jnp.where((ln >= at) & (ln < at + 4), x, r_acc)
            at = (at + 4) % 128
            l_acc = jnp.where((ln >= at) & (ln < at + 4), x, l_acc)
        right[v] = r_acc
        left[v] = rl(l_acc, -4)


def pack_layers(first, last, q, h, b, z, right, left, lh_ref, rh_ref, hi, lo, w, strips):
    ln, rw = lane(), row()
    m = ln & 3
    quad = (ln >> 2) & 3
    for v in range(6):
        lm, rm = left[v], right[v]
        end_l = jnp.where(m == 0, lm, jnp.where(m == 1, rl(lm, 1), jnp.where(m == 2, rl(lm, 2), rl(lm, 3))))
        end_r = jnp.where(m == 3, rm, jnp.where(m == 2, rl(rm, -1), jnp.where(m == 1, rl(rm, -2), rl(rm, -3))))
        lh = jnp.where(first, end_l, lh_ref[v])
        rh = jnp.where(last, end_r, rh_ref[v])
        for t in range(4) if v < 5 else (0, 2):
            parts = [rl(x, 4 * (i - t)) for i, x in enumerate((lh, lm, rm, rh))]
            strips[4 * v + t if v < 5 else 20 + t // 2] = jnp.where(
                quad < 2, jnp.where(quad == 0, parts[0], parts[1]), jnp.where(quad == 2, parts[2], parts[3])
            )
    surf, surf_z = strips[20], strips[21]
    own, bq = [q[f, 15] for f in range(5)], [b[f] for f in range(5)]
    zq, bz = [z[f * NL + 15] for f in range(5)], [z[81 + f] for f in range(5)]
    sq = [strips[4 * f + 1] for f in range(5)]
    w0 = speed(own, bq)
    w0z = speed(zq, bz)
    w0s = spread(speed(sq, [rl(surf, 16 * (6 - f)) for f in range(5)]), 7)
    (hx, hz), _, _ = slopes(h[...], z[80], spread(surf, 0), spread(surf_z, 0))
    (s1,) = fluxes(sq, (1,))
    (z3,) = fluxes(zq, (3,))
    near = []
    for x in ([q[f, 13] for f in range(5)], [q[f, 14] for f in range(5)], own, bq):
        f1, f2, f3 = fluxes(x)
        near.append((f1, f2, f3, moving(f1, f3, x, hx, hz, w0)))
    eta = (LAYERS - 0.5) / LAYERS
    ih = 1.0 / h[...]
    top = []
    for f in range(5):
        dx = patched(d_lane(near[2][0][f]), rl(strip_patch(d_lane(s1[f])), -124))
        da, _ = d_ring(near[2][2][f], z3[f])
        dn, dg = ((near[0][k][f] - 8.0 * near[1][k][f]) + 7.0 * near[3][k][f] for k in (1, 3))
        top.append(own[f] + C * (ih * (eta * dg - dn) - (dx + da)))
    w1 = speed(top, bq)
    speeds = (w0, w0z, w0s, w1)
    for k in range(4):
        w[k] = speeds[k]
        hi[27 + k] = speeds[k]
        lo[27 + k] = speeds[k]
    near_rows = (rw < 2) | (rw >= 6)
    hi_s = strips[4 * 4 + 1]
    lo_s = strips[4 * 4]
    hi[26] = hi_s
    lo[26] = lo_s
    for f in range(5):
        for k in range(4):
            hi[4 * f + k] = q[f, 12 + k]
            lo[4 * f + k] = q[f, k]
        hi[20 + f] = jnp.where(near_rows, z[f * NL + 14], rs(z[f * NL + 15], 4))
        lo[20 + f] = jnp.where(near_rows, z[f * NL], rs(z[f * NL + 1], 4))
        if f < 4:
            inside = (ln >= 32 * f) & (ln < 32 * f + 32)
            hi_s = jnp.where(inside, rl(strips[4 * f + 1], 32 * f + 32), hi_s)
            lo_s = jnp.where(inside, rl(strips[4 * f], 32 * f), lo_s)
    hi[25] = hi_s
    lo[25] = lo_s


def advance(wn, first, last, q, h, b, z, strips, w, below, above, cross, out, h_out, *scratch):
    qx, qz, f1x, f2x, f3x, gx, f1z, f2z, f3z, gz, sx, sz, pt, ptz = scratch
    ln, rw = lane(), row()
    group, off = ln >> 4, ln & 15
    bottom, top = wn == 0, wn == 3
    near_rows = (rw < 2) | (rw >= 6)

    speeds = []
    for k in range(4):
        a = jnp.where(bottom, below[27 + k], cross[k])
        c = jnp.where(top, w[k], above[27 + k])
        speeds.append(jnp.where(wn < 2, a, c))
    w0, w0z, w0s, w1 = speeds

    surf, surf_z = strips[20], strips[21]
    strip_q = []
    for f in range(5):
        sign = MIRROR[f]
        bq, bz = b[f], z[81 + f]
        for k in range(NL):
            qx[f, 4 + k] = q[f, k]
            qz[f, 2 + k] = z[f * NL + k]
        for k in range(4):
            qx[f, k] = jnp.where(bottom, sign * q[f, 3 - k], below[4 * f + k])
            qx[f, 20 + k] = jnp.where(top, bq, above[4 * f + k])
        zb, za = below[20 + f], above[20 + f]
        qz[f, 0] = jnp.where(bottom, sign * z[f * NL + 1], zb)
        qz[f, 1] = jnp.where(bottom, sign * z[f * NL], rs(zb, 4))
        qz[f, 18] = jnp.where(top, bz, za)
        qz[f, 19] = jnp.where(top, bz, rs(za, 4))
        s_lo, s_hi = strips[4 * f], strips[4 * f + 1]
        if f < 4:
            sb, sa = rl(below[25], 96 - 32 * f), rl(above[25], -32 * f)
        else:
            sb, sa = below[26], above[26]
        sb = jnp.where(bottom, sign * jnp.where(group == 7, rl(s_lo, -16), rl(s_lo, 80)), sb)
        sa = jnp.where(top, spread(surf, 1 + f), sa)
        strip_q.append((s_lo, s_hi, jnp.where(ln < 64, sa, sb)))

    h0, h0z = h[...], z[80]
    h0s, h0sz = spread(surf, 0), spread(surf_z, 0)
    (hx, hz), (hxz, hzz), (hxs, hzs) = slopes(h0, h0z, h0s, h0sz)
    ih, ihz, ihs = 1.0 / h0, 1.0 / h0z, 1.0 / h0s
    base = wn * NL

    parts = []
    for v in range(3):
        x = [strip_q[f][v] for f in range(5)]
        f1, f2, f3 = fluxes(x)
        d1 = [d_lane(f1[f]) for f in range(5)]
        for f in range(5):
            pt[f, v] = strip_patch(d1[f])
        parts.append((d1, f2, f3, moving(f1, f3, x, hxs, hzs, w0s)))
    halo3 = []
    for v in range(2):
        x = [strips[4 * f + 2 + v] for f in range(5)]
        z1, z3 = fluxes(x, (1, 3))
        for f in range(5):
            ptz[f, v] = strip_patch(d_lane(z1[f]))
        halo3.append(z3)

    def layer_shift(x, v, k):
        a = rl(x[v], -16 * k)
        c = rl(x[(v + (1 if k > 0 else -1)) % 3], -16 * k)
        return jnp.where(ln < 128 - 16 * k if k > 0 else ln >= -16 * k, a, c)

    strip_s = []
    for v in range(2):
        eta = ((base + 8 * v + group).astype(F32) + 0.5) / LAYERS
        done = []
        for f in range(5):
            dn, dg = (
                (layer_shift(x, v, -2) - layer_shift(x, v, 2)) + 8.0 * (layer_shift(x, v, 1) - layer_shift(x, v, -1))
                for x in ([parts[i][k][f] for i in range(3)] for k in (1, 3))
            )
            da, _ = d_ring(parts[v][2][f], halo3[v][f])
            s = strip_q[f][v] + C * (ihs * (eta * dg - dn) - (parts[v][0][f] + da))
            s = jnp.where(first & ((off == 2) | (off == 3)), jnp.where(off == 3, rl(s, -1), rl(s, -2)), s)
            s = jnp.where(last & ((off == 12) | (off == 13)), jnp.where(off == 12, rl(s, 1), rl(s, 2)), s)
            done.append(s)
        strip_s.append(done)

    def own_flux(l, _):
        x = [qx[f, l] for f in range(5)]
        f1, f2, f3 = fluxes(x)
        g = moving(f1, f3, x, hx, hz, w0)
        for f in range(5):
            f1x[f, l], f2x[f, l], f3x[f, l], gx[f, l] = f1[f], f2[f], f3[f], g[f]
        return 0

    def halo_flux(l, _):
        x = [qz[f, l] for f in range(5)]
        f1, f2, f3 = fluxes(x)
        g = moving(f1, f3, x, hxz, hzz, w0z)
        for f in range(5):
            f1z[f, l], f2z[f, l], f3z[f, l], gz[f, l] = f1[f], f2[f], f3[f], g[f]
        return 0

    lax.fori_loop(0, 24, own_flux, 0, unroll=2)
    lax.fori_loop(0, 20, halo_flux, 0, unroll=2)

    def d_normal(ref, f, l):
        return (ref[f, l - 2] - ref[f, l + 2]) + 8.0 * (ref[f, l + 1] - ref[f, l - 1])

    def eta_of(l):
        return ((base + l).astype(F32) + 0.5) / LAYERS

    def patch_shift(l):
        return 116 - 16 * (l & 7)

    def own_edge(l):
        eta = eta_of(l)
        for f in range(5):
            dx = patched(d_lane(f1x[f, l + 4]), pltpu.roll(pt[f, 2], patch_shift(l), 1))
            da, _ = d_ring(f3x[f, l + 4], f3z[f, l + 2])
            dn, dg = d_normal(f2x, f, l + 4), d_normal(gx, f, l + 4)
            sx[f, l + 2] = qx[f, l + 4] + C * (ih * (eta * dg - dn) - (dx + da))

    def section(l, _):
        eta = eta_of(l)
        half = l >> 3
        shift = patch_shift(l)
        for f in range(5):
            dx = patched(d_lane(f1x[f, l + 4]), pltpu.roll(pt[f, half], shift, 1))
            dxz = patched(d_lane(f1z[f, l + 2]), pltpu.roll(ptz[f, half], shift, 1))
            da, daz = d_ring(f3x[f, l + 4], f3z[f, l + 2])
            dn, dg = d_normal(f2x, f, l + 4), d_normal(gx, f, l + 4)
            sx[f, l + 2] = qx[f, l + 4] + C * (ih * (eta * dg - dn) - (dx + da))
            dn, dg = d_normal(f2z, f, l + 2), d_normal(gz, f, l + 2)
            sz[f, l] = qz[f, l + 2] + C * (ihz * (eta * dg - dn) - (dxz + daz))
        return 0

    lax.fori_loop(0, NL, section, 0)
    for l in (-2, -1, 16, 17):
        own_edge(l)
    for f in range(5):
        for k in range(2):
            sx[f, k] = jnp.where(bottom, MIRROR[f] * sx[f, 3 - k], sx[f, k])
            sx[f, 18 + k] = jnp.where(top, b[f], sx[f, 18 + k])

    h1, h1z, h1s = h0 + STEP * w0, h0z + STEP * w0z, h0s + STEP * w0s
    hx1 = SCALE * d_ends(h1, rl(strip_ends(h1s), -12))
    hz1 = SCALE * d_ring(h1, h1z)[0]
    ih1 = 1.0 / h1
    h_out[...] = 0.5 * (h0 + h1 + STEP * w1)
    for v in range(2):
        (f1,) = fluxes(strip_s[v], (1,))
        for f in range(5):
            pt[f, v] = strip_ends(f1[f])

    def own_flux_two(l, _):
        x = [sx[f, l] for f in range(5)]
        f1, f2, f3 = fluxes(x)
        g = moving(f1, f3, x, hx1, hz1, w1)
        for f in range(5):
            f1x[f, l], f2x[f, l], f3x[f, l], gx[f, l] = f1[f], f2[f], f3[f], g[f]
        return 0

    def halo_flux_two(l, _):
        (f3,) = fluxes([sz[f, l] for f in range(5)], (3,))
        for f in range(5):
            f3z[f, l] = f3[f]
        return 0

    lax.fori_loop(0, 20, own_flux_two, 0, unroll=2)
    lax.fori_loop(0, NL, halo_flux_two, 0, unroll=2)

    def final(l, _):
        eta = eta_of(l)
        half = l >> 3
        shift = patch_shift(l)
        for f in range(5):
            dx = d_ends(f1x[f, l + 2], pltpu.roll(pt[f, half], shift, 1))
            da, _ = d_ring(f3x[f, l + 2], f3z[f, l])
            dn, dg = d_normal(f2x, f, l + 2), d_normal(gx, f, l + 2)
            rate = ih1 * (eta * dg - dn) - (dx + da)
            out[f, l] = 0.5 * (qx[f, l + 4] + sx[f, l + 2] + C * rate)
        return 0

    lax.fori_loop(0, NL, final, 0)


def call(body, ins, outs, scratch=()):
    shapes = tuple(jax.ShapeDtypeStruct(s, F32) for s in outs)
    return pl.pallas_call(
        body,
        out_shape=shapes,
        in_specs=[VM] * len(ins),
        out_specs=tuple([VM] * len(shapes)),
        scratch_shapes=[pltpu.VMEM(s, F32) for s in scratch],
        compiler_params=pltpu.CompilerParams(vmem_limit_bytes=40 * 1024 * 1024),
    )(*ins)


def stage_layers(*refs):
    tile, tiles = lax.axis_index("sx"), lax.axis_size("sx")
    pack_layers(tile == 0, tile == tiles - 1, *refs)


def stage_advance(*refs):
    tile, tiles = lax.axis_index("sx"), lax.axis_size("sx")
    advance(lax.axis_index("wn"), tile == 0, tile == tiles - 1, *refs)


def per_device(fields, height, behind):
    around = lax.axis_size("az")
    tiles = lax.axis_size("sx")
    own = (fields, height, behind)
    up, dn = call(pack_rows, own, [(HALF, 8, 128)] * 2)
    from_low = lax.ppermute(up, "az", [(i, (i + 1) % around) for i in range(around)])
    from_high = lax.ppermute(dn, "az", [((i + 1) % around, i) for i in range(around)])
    halo, right, left = call(
        pack_columns, (*own, from_low, from_high), [(NP, 8, 128), (6, 8, 128), (6, 8, 128)]
    )
    from_left = lax.ppermute(right, "sx", [(i, i + 1) for i in range(tiles - 1)])
    from_right = lax.ppermute(left, "sx", [(i + 1, i) for i in range(tiles - 1)])
    hi, lo, w, strips = call(
        stage_layers,
        (*own, halo, right, left, from_left, from_right),
        [(31, 8, 128), (31, 8, 128), (4, 8, 128), (22, 8, 128)],
    )
    below = lax.ppermute(hi, "wn", [(0, 1), (1, 2), (2, 3), (3, 0)])
    above = lax.ppermute(lo, "wn", [(1, 0), (2, 1), (3, 2)])
    cross = lax.ppermute(w, "wn", [(3, 1)])
    return call(
        stage_advance,
        (*own, halo, strips, w, below, above, cross),
        [(5, NL, 8, 128), (8, 128)],
        [(5, 24, 8, 128), (5, 20, 8, 128)]
        + [(5, 24, 8, 128)] * 4
        + [(5, 20, 8, 128)] * 4
        + [(5, 20, 8, 128), (5, NL, 8, 128), (5, 3, 8, 128), (5, 2, 8, 128)],
    )


def solution(mesh):
    in_specs = (P(None, "wn", "az", "sx"), P("az", "sx"), P(None, "az", "sx"))
    out_specs = (P(None, "wn", "az", "sx"), P("az", "sx"))
    return jax.shard_map(
        per_device, mesh=mesh, in_specs=in_specs, out_specs=out_specs, check_vma=False
    )
```

```python
import functools

import jax
import jax.numpy as jnp
from jax import lax
from jax.experimental import pallas as pl
from jax.experimental.pallas import tpu as pltpu
from jax.sharding import PartitionSpec as P

GAMMA = 1.4
CFL_STEP = 0.08
LAYERS = 64
NL = 16
NP = 86
HALF = 43
UNITS = 11
SCALE = LAYERS / 12.0
STEP = CFL_STEP / LAYERS
C = CFL_STEP / 12.0
VM = pl.BlockSpec(memory_space=pltpu.VMEM)
F32 = jnp.float32
MIRROR = (1.0, -1.0, -1.0, -1.0, 1.0)


def lane():
    return lax.broadcasted_iota(jnp.int32, (8, 128), 1)


def row():
    return lax.broadcasted_iota(jnp.int32, (8, 128), 0)


def rl(x, shift):
    return pltpu.roll(x, shift % 128, 1) if shift % 128 else x


def rs(x, shift):
    return pltpu.roll(x, shift % 8, 0) if shift % 8 else x


def d_lane(x):
    return (rl(x, 2) - rl(x, -2)) + 8.0 * (rl(x, -1) - rl(x, 1))


def strip_patch(d):
    off = lane() & 15
    return jnp.where((off == 12) | (off == 13), rl(d, 8), d)


def strip_ends(x):
    off = lane() & 15
    return jnp.where((off == 10) | (off == 11), rl(x, 8), x)


def d_ends(x, e):
    ln = lane()
    p1 = rl(jnp.where(ln < 1, e, x), -1)
    p2 = rl(jnp.where(ln < 2, e, x), -2)
    m1 = rl(jnp.where(ln >= 127, e, x), 1)
    m2 = rl(jnp.where(ln >= 126, e, x), 2)
    return (m2 - p2) + 8.0 * (p1 - m1)


def patched(d, patch):
    ln = lane()
    return jnp.where((ln < 2) | (ln >= 126), patch, d)


def ring(x, z, shift):
    keep = row() >= shift if shift > 0 else row() < 8 + shift
    a, b = rs(x, shift), rs(z, shift)
    return jnp.where(keep, a, b), jnp.where(keep, b, a)


def d_ring(x, z):
    m2, m1, p1, p2 = ring(x, z, 2), ring(x, z, 1), ring(x, z, -1), ring(x, z, -2)
    return tuple((m2[i] - p2[i]) + 8.0 * (p1[i] - m1[i]) for i in (0, 1))


def spread(x, group):
    ln = lane()
    x = rl(x, -16 * group)
    x = jnp.where(ln < 16, x, rl(x, 16))
    x = jnp.where(ln < 32, x, rl(x, 32))
    return jnp.where(ln < 64, x, rl(x, 64))


def pressure(q):
    kinetic = (q[1] * q[1] + q[2] * q[2] + q[3] * q[3]) / q[0]
    return (GAMMA - 1.0) * (q[4] - 0.5 * kinetic)


def speed(q, b):
    behind = pressure(b)
    return (pressure(q) - behind) / jnp.sqrt(GAMMA * behind * b[0])


def fluxes(q, want=(1, 2, 3)):
    inv = 1.0 / q[0]
    v = [None, q[1] * inv, q[2] * inv, q[3] * inv]
    q11, q22, q33 = q[1] * v[1], q[2] * v[2], q[3] * v[3]
    p = (GAMMA - 1.0) * (q[4] - 0.5 * (q11 + q22 + q33))
    e = q[4] + p
    out = []
    if 1 in want:
        out.append([q[1], q11 + p, q[2] * v[1], q[3] * v[1], e * v[1]])
    if 2 in want:
        out.append([q[2], q[1] * v[2], q22 + p, q[3] * v[2], e * v[2]])
    if 3 in want:
        out.append([q[3], q[1] * v[3], q[2] * v[3], q33 + p, e * v[3]])
    return out


def moving(f1, f3, q, hx, hz, w):
    return [hx * f1[f] + hz * f3[f] + w * q[f] for f in range(5)]


def slopes(h, hz, hs, hsz):
    ds, dsz = d_lane(hs), d_lane(hsz)
    x = SCALE * patched(d_lane(h), rl(strip_patch(ds), -12))
    xz = SCALE * patched(d_lane(hz), rl(strip_patch(dsz), -12))
    a, az = d_ring(h, hz)
    s, _ = d_ring(hs, hsz)
    return (x, SCALE * a), (xz, SCALE * az), (SCALE * ds, SCALE * s)


def plane_of(q, h, b):
    def get(i):
        if i < 80:
            return q[i // NL, i % NL]
        return h[...] if i == 80 else b[i - 81]

    return get


def unit_planes(u):
    return [8 * u + j for j in range(8)] if u < 10 else [80 + j for j in range(6)]


def columns(get, right, left):
    ln = lane()
    for v in range(3):
        r_acc = jnp.zeros((8, 128), F32)
        l_acc = jnp.zeros((8, 128), F32)
        for u in range(4 * v, min(4 * v + 4, UNITS)):
            for j, i in enumerate(unit_planes(u)):
                at = 16 * j + 4 * (u - 4 * v)
                x = rl(get(i), at + 4)
                r_acc = jnp.where((ln >= at) & (ln < at + 4), x, r_acc)
                at = (at + 4) % 128
                l_acc = jnp.where((ln >= at) & (ln < at + 4), x, l_acc)
        right[v] = r_acc
        left[v] = rl(l_acc, -4)


def to_pairs(even, right, left, one, two):
    for v in range(3):
        one[v] = jnp.where(even, right[v], left[v])
        two[v] = jnp.where(even, left[v], right[v])


def build_strips(tile, tiles, right, left, one, two, put):
    m = lane() & 3
    quad = (lane() >> 2) & 3
    even = tile % 2 == 0
    for v in range(3):
        lm, rm = left[v], right[v]
        end_l = jnp.where(m == 0, lm, jnp.where(m == 1, rl(lm, 1), jnp.where(m == 2, rl(lm, 2), rl(lm, 3))))
        end_r = jnp.where(m == 3, rm, jnp.where(m == 2, rl(rm, -1), jnp.where(m == 1, rl(rm, -2), rl(rm, -3))))
        lh = jnp.where(tile == 0, end_l, jnp.where(even, two[v], one[v]))
        rh = jnp.where(tile == tiles - 1, end_r, jnp.where(even, one[v], two[v]))
        for t in range(min(4, UNITS - 4 * v)):
            a, b, c, d = (rl(x, 4 * (i - t)) for i, x in enumerate((lh, lm, rm, rh)))
            put(4 * v + t, jnp.where(quad < 2, jnp.where(quad == 0, a, b), jnp.where(quad == 2, c, d)))


def pack_rows(odd, q_hbm, h_hbm, b_hbm, q, h, b, one, two, sems):
    copies = [
        pltpu.make_async_copy(x, y, sems.at[i]) for i, (x, y) in enumerate(((q_hbm, q), (h_hbm, h), (b_hbm, b)))
    ]
    for c in copies:
        c.start()
    for c in copies:
        c.wait()
    get = plane_of(q, h, b)
    mask = (row() >= 4) ^ odd
    for i in range(HALF):
        x, y = get(i), rs(get(i + HALF), 4)
        one[i] = jnp.where(mask, x, y)
        two[i] = jnp.where(mask, y, x)


def pack_columns(even, q, h, b, right, left, one, two):
    columns(plane_of(q, h, b), right, left)
    to_pairs(even, right, left, one, two)


def pack_second(odd, wn, tile, tiles, q, h, b, a1, a2, right, left, s1, s2, *outs):
    z, strips, w, near, far, z_right, z_left, z_one, z_two, hi, lo = outs
    ln, rw = lane(), row()
    mask = (rw >= 4) ^ odd
    for i in range(HALF):
        x, y = a2[i], a1[i]
        z[i] = jnp.where(mask, x, y)
        z[i + HALF] = rs(jnp.where(mask, y, x), 4)

    def put(u, x):
        strips[u] = x

    build_strips(tile, tiles, right, left, s1, s2, put)
    surf = strips[10]
    own, bq = [q[f, 15] for f in range(5)], [b[f] for f in range(5)]
    zq, bz = [z[f * NL + 15] for f in range(5)], [z[81 + f] for f in range(5)]
    sq = [strips[2 * f + 1] for f in range(5)]
    w0 = speed(own, bq)
    w0z = speed(zq, bz)
    w0s = spread(speed(sq, [rl(surf, 16 * (6 - f)) for f in range(5)]), 7)
    hx = SCALE * patched(d_lane(h[...]), rl(strip_patch(d_lane(surf)), -12))
    hz = SCALE * d_ring(h[...], z[80])[0]
    (f1s,) = fluxes(sq, (1,))
    (f3z,) = fluxes(zq, (3,))
    levels = []
    for x in ([q[f, 13] for f in range(5)], [q[f, 14] for f in range(5)], own, bq):
        f1, f2, f3 = fluxes(x)
        levels.append((f1, f2, f3, moving(f1, f3, x, hx, hz, w0)))
    eta = (LAYERS - 0.5) / LAYERS
    ih = 1.0 / h[...]
    top = []
    for f in range(5):
        dx = patched(d_lane(levels[2][0][f]), rl(strip_patch(d_lane(f1s[f])), -124))
        da, _ = d_ring(levels[2][2][f], f3z[f])
        dn, dg = ((levels[0][k][f] - 8.0 * levels[1][k][f]) + 7.0 * levels[3][k][f] for k in (1, 3))
        top.append(own[f] + C * (ih * (eta * dg - dn) - (dx + da)))
    speeds = (w0, w0z, w0s, speed(top, bq))
    for k in range(4):
        w[k] = speeds[k]
        near[27 + k] = speeds[k]
        far[27 + k] = speeds[k]
    near_rows = (rw < 2) | (rw >= 6)
    hi_s = hi[26] = strips[9]
    lo_s = lo[26] = strips[8]
    for f in range(5):
        for k in range(4):
            hi[4 * f + k] = q[f, 12 + k]
            lo[4 * f + k] = q[f, k]
        hi[20 + f] = jnp.where(near_rows, z[f * NL + 14], rs(z[f * NL + 15], 4))
        lo[20 + f] = jnp.where(near_rows, z[f * NL], rs(z[f * NL + 1], 4))
        if f < 4:
            inside = (ln >= 32 * f) & (ln < 32 * f + 32)
            hi_s = jnp.where(inside, rl(strips[2 * f + 1], 32 * f + 32), hi_s)
            lo_s = jnp.where(inside, rl(strips[2 * f], 32 * f), lo_s)
    hi[25] = hi_s
    lo[25] = lo_s
    for i in range(27):
        near[i] = jnp.where(wn % 2 == 0, hi[i], lo[i])
        far[i] = jnp.where(wn == 1, hi[i], lo[i])
    columns(lambda i: z[i], z_right, z_left)
    to_pairs(tile % 2 == 0, z_right, z_left, z_one, z_two)


def advance(wn, tile, tiles, q, h, b, z, strips, w, near, far, cross, z_right, z_left, z_one, z_two, *rest):
    out, h_out, qx, qz, f1x, f2x, gx, f1z, f2z, gz, f3, sx, sz, pt, ptz, zst = rest
    first, last = tile == 0, tile == tiles - 1

    def put_strip(u, x):
        zst[u] = x

    build_strips(tile, tiles, z_right, z_left, z_one, z_two, put_strip)
    odd = wn % 2 == 1

    def below(i):
        return jnp.where(odd, near[i], far[i])

    def above(i):
        return jnp.where(odd, far[i], near[i])

    ln, rw = lane(), row()
    group, off = ln >> 4, ln & 15
    bottom, top = wn == 0, wn == 3
    near_rows = (rw < 2) | (rw >= 6)

    speeds = []
    for k in range(4):
        a = jnp.where(bottom, far[27 + k], cross[k])
        c = jnp.where(top, w[k], near[27 + k])
        speeds.append(jnp.where(wn < 2, a, c))
    w0, w0z, w0s, w1 = speeds

    surf, surf_z = strips[10], zst[10]
    strip_q = []
    for f in range(5):
        sign = MIRROR[f]
        bq, bz = b[f], z[81 + f]
        for k in range(NL):
            qx[f, 4 + k] = q[f, k]
            qz[f, 2 + k] = z[f * NL + k]
        for k in range(4):
            qx[f, k] = jnp.where(bottom, sign * q[f, 3 - k], below(4 * f + k))
            qx[f, 20 + k] = jnp.where(top, bq, above(4 * f + k))
        zb, za = below(20 + f), above(20 + f)
        qz[f, 0] = jnp.where(bottom, sign * z[f * NL + 1], zb)
        qz[f, 1] = jnp.where(bottom, sign * z[f * NL], rs(zb, 4))
        qz[f, 18] = jnp.where(top, bz, za)
        qz[f, 19] = jnp.where(top, bz, rs(za, 4))
        s_lo, s_hi = strips[2 * f], strips[2 * f + 1]
        if f < 4:
            sb, sa = rl(below(25), 96 - 32 * f), rl(above(25), -32 * f)
        else:
            sb, sa = below(26), above(26)
        sb = jnp.where(bottom, sign * jnp.where(group == 7, rl(s_lo, -16), rl(s_lo, 80)), sb)
        sa = jnp.where(top, spread(surf, 1 + f), sa)
        strip_q.append((s_lo, s_hi, jnp.where(ln < 64, sa, sb)))

    h0, h0z = h[...], z[80]
    h0s, h0sz = spread(surf, 0), spread(surf_z, 0)
    (hx, hz), (hxz, hzz), (hxs, hzs) = slopes(h0, h0z, h0s, h0sz)
    ih, ihz, ihs = 1.0 / h0, 1.0 / h0z, 1.0 / h0s
    base = wn * NL

    parts = []
    for v in range(3):
        x = [strip_q[f][v] for f in range(5)]
        a1, a2, a3 = fluxes(x)
        d1 = [d_lane(a1[f]) for f in range(5)]
        for f in range(5):
            pt[f, v] = strip_patch(d1[f])
        parts.append((d1, a2, a3, moving(a1, a3, x, hxs, hzs, w0s)))
    halo3 = []
    for v in range(2):
        x = [zst[2 * f + v] for f in range(5)]
        z1, z3 = fluxes(x, (1, 3))
        for f in range(5):
            ptz[f, v] = strip_patch(d_lane(z1[f]))
        halo3.append(z3)

    def layer_shift(x, v, k):
        a = rl(x[v], -16 * k)
        c = rl(x[(v + (1 if k > 0 else -1)) % 3], -16 * k)
        return jnp.where(ln < 128 - 16 * k if k > 0 else ln >= -16 * k, a, c)

    strip_s = []
    for v in range(2):
        eta = ((base + 8 * v + group).astype(F32) + 0.5) / LAYERS
        done = []
        for f in range(5):
            dn, dg = (
                (layer_shift(x, v, -2) - layer_shift(x, v, 2)) + 8.0 * (layer_shift(x, v, 1) - layer_shift(x, v, -1))
                for x in ([parts[i][k][f] for i in range(3)] for k in (1, 3))
            )
            da, _ = d_ring(parts[v][2][f], halo3[v][f])
            s = strip_q[f][v] + C * (ihs * (eta * dg - dn) - (parts[v][0][f] + da))
            s = jnp.where(first & ((off == 2) | (off == 3)), jnp.where(off == 3, rl(s, -1), rl(s, -2)), s)
            s = jnp.where(last & ((off == 12) | (off == 13)), jnp.where(off == 12, rl(s, 1), rl(s, 2)), s)
            done.append(s)
        strip_s.append(done)

    def d_rows(ref, f, l, at):
        m2, m1, p1, p2 = (ref[f, l, pl.ds(at + k, 8)] for k in (-2, -1, 1, 2))
        return (m2 - p2) + 8.0 * (p1 - m1)

    def d_around(f, l):
        return d_rows(f3, f, l, 16)

    def d_around_halo(f, l):
        return jnp.where(rw < 4, d_rows(f3, f, l, 24), d_rows(f3, f, l, 8))

    def put_halo(f, l, x):
        f3[f, l, 24:32] = x
        f3[f, l, 8:16] = x

    def own_flux(l, _):
        x = [qx[f, l] for f in range(5)]
        a1, a2, a3 = fluxes(x)
        g = moving(a1, a3, x, hx, hz, w0)
        for f in range(5):
            f1x[f, l], f2x[f, l], gx[f, l] = a1[f], a2[f], g[f]
            f3[f, l, 16:24] = a3[f]
        return 0

    def halo_flux(l, _):
        x = [qz[f, l] for f in range(5)]
        a1, a2, a3 = fluxes(x)
        g = moving(a1, a3, x, hxz, hzz, w0z)
        for f in range(5):
            f1z[f, l], f2z[f, l], gz[f, l] = a1[f], a2[f], g[f]
            put_halo(f, l + 2, a3[f])
        return 0

    lax.fori_loop(0, 24, own_flux, 0, unroll=8)
    lax.fori_loop(0, 20, halo_flux, 0, unroll=10)

    def d_normal(ref, f, l):
        return (ref[f, l - 2] - ref[f, l + 2]) + 8.0 * (ref[f, l + 1] - ref[f, l - 1])

    def eta_of(l):
        return ((base + l).astype(F32) + 0.5) / LAYERS

    def patch_shift(l):
        return 116 - 16 * (l & 7)

    def own_edge(l):
        eta = eta_of(l)
        for f in range(5):
            dx = patched(d_lane(f1x[f, l + 4]), pltpu.roll(pt[f, 2], patch_shift(l), 1))
            da = d_around(f, l + 4)
            dn, dg = d_normal(f2x, f, l + 4), d_normal(gx, f, l + 4)
            sx[f, l + 2] = qx[f, l + 4] + C * (ih * (eta * dg - dn) - (dx + da))

    def section(l, _):
        eta = eta_of(l)
        half = l >> 3
        shift = patch_shift(l)
        for f in range(5):
            dx = patched(d_lane(f1x[f, l + 4]), pltpu.roll(pt[f, half], shift, 1))
            dxz = patched(d_lane(f1z[f, l + 2]), pltpu.roll(ptz[f, half], shift, 1))
            da, daz = d_around(f, l + 4), d_around_halo(f, l + 4)
            dn, dg = d_normal(f2x, f, l + 4), d_normal(gx, f, l + 4)
            sx[f, l + 2] = qx[f, l + 4] + C * (ih * (eta * dg - dn) - (dx + da))
            dn, dg = d_normal(f2z, f, l + 2), d_normal(gz, f, l + 2)
            sz[f, l] = qz[f, l + 2] + C * (ihz * (eta * dg - dn) - (dxz + daz))
        return 0

    lax.fori_loop(0, NL, section, 0, unroll=8)
    for l in (-2, -1, 16, 17):
        own_edge(l)
    for f in range(5):
        for k in range(2):
            sx[f, k] = jnp.where(bottom, MIRROR[f] * sx[f, 3 - k], sx[f, k])
            sx[f, 18 + k] = jnp.where(top, b[f], sx[f, 18 + k])

    h1, h1z, h1s = h0 + STEP * w0, h0z + STEP * w0z, h0s + STEP * w0s
    hx1 = SCALE * d_ends(h1, rl(strip_ends(h1s), -12))
    hz1 = SCALE * d_ring(h1, h1z)[0]
    ih1 = 1.0 / h1
    h_out[...] = 0.5 * (h0 + h1 + STEP * w1)
    for v in range(2):
        (a1,) = fluxes(strip_s[v], (1,))
        for f in range(5):
            pt[f, v] = strip_ends(a1[f])

    def own_flux_two(l, _):
        x = [sx[f, l] for f in range(5)]
        a1, a2, a3 = fluxes(x)
        g = moving(a1, a3, x, hx1, hz1, w1)
        for f in range(5):
            f1x[f, l], f2x[f, l], gx[f, l] = a1[f], a2[f], g[f]
            f3[f, l, 16:24] = a3[f]
        return 0

    def halo_flux_two(l, _):
        (a3,) = fluxes([sz[f, l] for f in range(5)], (3,))
        for f in range(5):
            put_halo(f, l + 2, a3[f])
        return 0

    lax.fori_loop(0, 20, own_flux_two, 0, unroll=10)
    lax.fori_loop(0, NL, halo_flux_two, 0, unroll=8)

    def final(l, _):
        eta = eta_of(l)
        half = l >> 3
        shift = patch_shift(l)
        for f in range(5):
            dx = d_ends(f1x[f, l + 2], pltpu.roll(pt[f, half], shift, 1))
            da = d_around(f, l + 2)
            dn, dg = d_normal(f2x, f, l + 2), d_normal(gx, f, l + 2)
            rate = ih1 * (eta * dg - dn) - (dx + da)
            out[f, l] = 0.5 * (qx[f, l + 4] + sx[f, l + 2] + C * rate)
        return 0

    lax.fori_loop(0, NL, final, 0, unroll=8)


def call(body, ins, outs, scratch=(), sems=0, space=VM):
    shapes = tuple(jax.ShapeDtypeStruct(s, F32) for s in outs)
    return pl.pallas_call(
        body,
        out_shape=shapes,
        in_specs=[space] * len(ins),
        out_specs=tuple([VM] * len(shapes)),
        scratch_shapes=[pltpu.VMEM(s, F32) for s in scratch] + [pltpu.SemaphoreType.DMA((sems,))] * (sems > 0),
        compiler_params=pltpu.CompilerParams(vmem_limit_bytes=40 * 1024 * 1024),
    )(*ins)


def where_am_i():
    return lax.axis_index("sx"), lax.axis_size("sx")


def stage_rows(*refs):
    pack_rows(lax.axis_index("az") % 2 == 1, *refs)


def stage_columns(*refs):
    pack_columns(lax.axis_index("sx") % 2 == 0, *refs)


def stage_second(*refs):
    pack_second(lax.axis_index("az") % 2 == 1, lax.axis_index("wn"), *where_am_i(), *refs)


def stage_advance(*refs):
    advance(lax.axis_index("wn"), *where_am_i(), *refs)


def swaps(size, start, wrap):
    pairs = [(i, (i + 1) % size) for i in range(start, size if wrap else size - 1, 2)]
    return pairs + [(j, i) for i, j in pairs]


def per_device(fields, height, behind):
    around = lax.axis_size("az")
    tiles = lax.axis_size("sx")
    plane = (8, 128)
    *own, one, two = call(
        stage_rows,
        [pltpu.with_memory_space_constraint(x, pltpu.HBM) for x in (fields, height, behind)],
        [fields.shape, height.shape, behind.shape] + [(HALF, *plane)] * 2,
        sems=3,
        space=pl.BlockSpec(memory_space=pltpu.HBM),
    )
    a2 = lax.ppermute(two, "az", swaps(around, 1, True))
    a1 = lax.ppermute(one, "az", swaps(around, 0, True))
    right, left, one, two = call(stage_columns, own, [(3, *plane)] * 4)
    s2 = lax.ppermute(two, "sx", swaps(tiles, 1, False))
    s1 = lax.ppermute(one, "sx", swaps(tiles, 0, False))
    halo, strips, w, near, far, z_right, z_left, one, two = call(
        stage_second,
        (*own, a1, a2, right, left, s1, s2),
        [(NP, *plane), (UNITS, *plane), (4, *plane)] + [(31, *plane)] * 2 + [(3, *plane)] * 4,
        [(27, *plane)] * 2,
    )
    cross = lax.ppermute(w, "wn", [(3, 1)])
    far = lax.ppermute(far, "wn", [(1, 2), (2, 1), (3, 0)])
    s2 = lax.ppermute(two, "sx", swaps(tiles, 1, False))
    s1 = lax.ppermute(one, "sx", swaps(tiles, 0, False))
    near = lax.ppermute(near, "wn", [(0, 1), (1, 0), (2, 3), (3, 2)])
    return call(
        stage_advance,
        (*own, halo, strips, w, near, far, cross, z_right, z_left, s1, s2),
        [(5, NL, 8, 128), (8, 128)],
        [(5, 24, 8, 128), (5, 20, 8, 128)]
        + [(5, 24, 8, 128)] * 3
        + [(5, 20, 8, 128)] * 3
        + [(5, 24, 40, 128)]
        + [(5, 20, 8, 128), (5, NL, 8, 128), (5, 3, 8, 128), (5, 2, 8, 128), (UNITS, 8, 128)],
    )


def solution(mesh):
    in_specs = (P(None, "wn", "az", "sx"), P("az", "sx"), P(None, "az", "sx"))
    out_specs = (P(None, "wn", "az", "sx"), P("az", "sx"))
    return jax.shard_map(
        per_device, mesh=mesh, in_specs=in_specs, out_specs=out_specs, check_vma=False
    )
```

```python
import functools

import jax
import jax.numpy as jnp
from jax import lax
from jax.experimental import pallas as pl
from jax.experimental.pallas import tpu as pltpu
from jax.sharding import PartitionSpec as P

GAMMA = 1.4
CFL_STEP = 0.08
LAYERS = 64
NL = 16
NP = 86
HALF = 43
UNITS = 11
SCALE = LAYERS / 12.0
STEP = CFL_STEP / LAYERS
C = CFL_STEP / 12.0
VM = pl.BlockSpec(memory_space=pltpu.VMEM)
F32 = jnp.float32
MIRROR = (1.0, -1.0, -1.0, -1.0, 1.0)


def lane():
    return lax.broadcasted_iota(jnp.int32, (8, 128), 1)


def row():
    return lax.broadcasted_iota(jnp.int32, (8, 128), 0)


def rl(x, shift):
    return pltpu.roll(x, shift % 128, 1) if shift % 128 else x


def rs(x, shift):
    return pltpu.roll(x, shift % 8, 0) if shift % 8 else x


def d_lane(x):
    return (rl(x, 2) - rl(x, -2)) + 8.0 * (rl(x, -1) - rl(x, 1))


def strip_patch(d):
    off = lane() & 15
    return jnp.where((off == 12) | (off == 13), rl(d, 8), d)


def strip_ends(x):
    off = lane() & 15
    return jnp.where((off == 10) | (off == 11), rl(x, 8), x)


def d_ends(x, e):
    ln = lane()
    p1 = rl(jnp.where(ln < 1, e, x), -1)
    p2 = rl(jnp.where(ln < 2, e, x), -2)
    m1 = rl(jnp.where(ln >= 127, e, x), 1)
    m2 = rl(jnp.where(ln >= 126, e, x), 2)
    return (m2 - p2) + 8.0 * (p1 - m1)


def patched(d, patch):
    ln = lane()
    return jnp.where((ln < 2) | (ln >= 126), patch, d)


def ring(x, z, shift):
    keep = row() >= shift if shift > 0 else row() < 8 + shift
    a, b = rs(x, shift), rs(z, shift)
    return jnp.where(keep, a, b), jnp.where(keep, b, a)


def d_ring(x, z):
    m2, m1, p1, p2 = ring(x, z, 2), ring(x, z, 1), ring(x, z, -1), ring(x, z, -2)
    return tuple((m2[i] - p2[i]) + 8.0 * (p1[i] - m1[i]) for i in (0, 1))


def spread(x, group):
    ln = lane()
    x = rl(x, -16 * group)
    x = jnp.where(ln < 16, x, rl(x, 16))
    x = jnp.where(ln < 32, x, rl(x, 32))
    return jnp.where(ln < 64, x, rl(x, 64))


def pressure(q):
    kinetic = (q[1] * q[1] + q[2] * q[2] + q[3] * q[3]) / q[0]
    return (GAMMA - 1.0) * (q[4] - 0.5 * kinetic)


def speed(q, b):
    behind = pressure(b)
    return (pressure(q) - behind) / jnp.sqrt(GAMMA * behind * b[0])


def fluxes(q, want=(1, 2, 3), move=None):
    inv = 1.0 / q[0]
    v1, v2, v3 = q[1] * inv, q[2] * inv, q[3] * inv
    q11, q22, q33 = q[1] * v1, q[2] * v2, q[3] * v3
    p = (GAMMA - 1.0) * (q[4] - 0.5 * (q11 + q22 + q33))
    e = q[4] + p
    q12, q13, q23 = q[1] * v2, q[1] * v3, q[2] * v3
    out = []
    if 1 in want:
        out.append([q[1], q11 + p, q12, q13, e * v1])
    if 2 in want:
        out.append([q[2], q12, q22 + p, q23, e * v2])
    if 3 in want:
        out.append([q[3], q13, q23, q33 + p, e * v3])
    if move is not None:
        hx, hz, w = move
        s = hx * v1 + hz * v3
        t = s + w
        out.append([q[0] * t, q[1] * t + p * hx, q[2] * t, q[3] * t + p * hz, q[4] * t + p * s])
    return out


def slopes(h, hz, hs, hsz):
    ds, dsz = d_lane(hs), d_lane(hsz)
    x = SCALE * patched(d_lane(h), rl(strip_patch(ds), -12))
    xz = SCALE * patched(d_lane(hz), rl(strip_patch(dsz), -12))
    a, az = d_ring(h, hz)
    s, _ = d_ring(hs, hsz)
    return (x, SCALE * a), (xz, SCALE * az), (SCALE * ds, SCALE * s)


def plane_of(q, h, b):
    def get(i):
        if i < 80:
            return q[i // NL, i % NL]
        return h[...] if i == 80 else b[i - 81]

    return get


def unit_planes(u):
    return [8 * u + j for j in range(8)] if u < 10 else [80 + j for j in range(6)]


def columns(get, right, left):
    ln = lane()
    for v in range(3):
        r_acc = jnp.zeros((8, 128), F32)
        l_acc = jnp.zeros((8, 128), F32)
        for u in range(4 * v, min(4 * v + 4, UNITS)):
            for j, i in enumerate(unit_planes(u)):
                at = 16 * j + 4 * (u - 4 * v)
                x = rl(get(i), at + 4)
                r_acc = jnp.where((ln >= at) & (ln < at + 4), x, r_acc)
                at = (at + 4) % 128
                l_acc = jnp.where((ln >= at) & (ln < at + 4), x, l_acc)
        right[v] = r_acc
        left[v] = rl(l_acc, -4)


def to_pairs(even, right, left, one, two):
    for v in range(3):
        one[v] = jnp.where(even, right[v], left[v])
        two[v] = jnp.where(even, left[v], right[v])


def build_strips(tile, tiles, right, left, one, two, put):
    m = lane() & 3
    quad = (lane() >> 2) & 3
    even = tile % 2 == 0
    for v in range(3):
        lm, rm = left[v], right[v]
        end_l = jnp.where(m == 0, lm, jnp.where(m == 1, rl(lm, 1), jnp.where(m == 2, rl(lm, 2), rl(lm, 3))))
        end_r = jnp.where(m == 3, rm, jnp.where(m == 2, rl(rm, -1), jnp.where(m == 1, rl(rm, -2), rl(rm, -3))))
        lh = jnp.where(tile == 0, end_l, jnp.where(even, two[v], one[v]))
        rh = jnp.where(tile == tiles - 1, end_r, jnp.where(even, one[v], two[v]))
        for t in range(min(4, UNITS - 4 * v)):
            a, b, c, d = (rl(x, 4 * (i - t)) for i, x in enumerate((lh, lm, rm, rh)))
            put(4 * v + t, jnp.where(quad < 2, jnp.where(quad == 0, a, b), jnp.where(quad == 2, c, d)))


def pack_rows(odd, q_hbm, h_hbm, b_hbm, q, h, b, one, two, sems):
    copies = [
        pltpu.make_async_copy(x, y, sems.at[i]) for i, (x, y) in enumerate(((q_hbm, q), (h_hbm, h), (b_hbm, b)))
    ]
    for c in copies:
        c.start()
    for c in copies:
        c.wait()
    get = plane_of(q, h, b)
    mask = (row() >= 4) ^ odd
    for i in range(HALF):
        x, y = get(i), rs(get(i + HALF), 4)
        one[i] = jnp.where(mask, x, y)
        two[i] = jnp.where(mask, y, x)


def pack_columns(even, q, h, b, right, left, one, two):
    columns(plane_of(q, h, b), right, left)
    to_pairs(even, right, left, one, two)


def pack_second(odd, wn, tile, tiles, q, h, b, a1, a2, right, left, s1, s2, *outs):
    z, strips, w, near, far, z_right, z_left, z_one, z_two, hi, lo = outs
    ln, rw = lane(), row()
    mask = (rw >= 4) ^ odd
    for i in range(HALF):
        x, y = a2[i], a1[i]
        z[i] = jnp.where(mask, x, y)
        z[i + HALF] = rs(jnp.where(mask, y, x), 4)

    def put(u, x):
        strips[u] = x

    build_strips(tile, tiles, right, left, s1, s2, put)
    surf = strips[10]
    own, bq = [q[f, 15] for f in range(5)], [b[f] for f in range(5)]
    zq, bz = [z[f * NL + 15] for f in range(5)], [z[81 + f] for f in range(5)]
    sq = [strips[2 * f + 1] for f in range(5)]
    w0 = speed(own, bq)
    w0z = speed(zq, bz)
    w0s = spread(speed(sq, [rl(surf, 16 * (6 - f)) for f in range(5)]), 7)
    hx = SCALE * patched(d_lane(h[...]), rl(strip_patch(d_lane(surf)), -12))
    hz = SCALE * d_ring(h[...], z[80])[0]
    (f1s,) = fluxes(sq, (1,))
    (f3z,) = fluxes(zq, (3,))
    levels = []
    for x in ([q[f, 13] for f in range(5)], [q[f, 14] for f in range(5)], own, bq):
        levels.append(fluxes(x, move=(hx, hz, w0)))
    eta = (LAYERS - 0.5) / LAYERS
    ih = 1.0 / h[...]
    top = []
    for f in range(5):
        dx = patched(d_lane(levels[2][0][f]), rl(strip_patch(d_lane(f1s[f])), -124))
        da, _ = d_ring(levels[2][2][f], f3z[f])
        dn, dg = ((levels[0][k][f] - 8.0 * levels[1][k][f]) + 7.0 * levels[3][k][f] for k in (1, 3))
        top.append(own[f] + C * (ih * (eta * dg - dn) - (dx + da)))
    speeds = (w0, w0z, w0s, speed(top, bq))
    for k in range(4):
        w[k] = speeds[k]
        far[27 + k] = speeds[k]
    near_rows = (rw < 2) | (rw >= 6)
    hi_s = hi[26] = strips[9]
    lo_s = lo[26] = strips[8]
    for f in range(5):
        for k in range(4):
            hi[4 * f + k] = q[f, 12 + k]
            lo[4 * f + k] = q[f, k]
        hi[20 + f] = jnp.where(near_rows, z[f * NL + 14], rs(z[f * NL + 15], 4))
        lo[20 + f] = jnp.where(near_rows, z[f * NL], rs(z[f * NL + 1], 4))
        if f < 4:
            inside = (ln >= 32 * f) & (ln < 32 * f + 32)
            hi_s = jnp.where(inside, rl(strips[2 * f + 1], 32 * f + 32), hi_s)
            lo_s = jnp.where(inside, rl(strips[2 * f], 32 * f), lo_s)
    hi[25] = hi_s
    lo[25] = lo_s
    for i in range(27):
        near[i] = jnp.where(wn % 2 == 0, hi[i], lo[i])
        far[i] = jnp.where(wn == 1, hi[i], lo[i])
    columns(lambda i: z[i], z_right, z_left)
    to_pairs(tile % 2 == 0, z_right, z_left, z_one, z_two)


def pack_near(wn, near, w, far, _one, _two, out):
    for i in range(27):
        out[i] = near[i]
    for k in range(4):
        out[27 + k] = jnp.where(wn == 0, far[27 + k], w[k])


def advance(wn, tile, tiles, q, h, b, z, strips, w, near, far, z_right, z_left, z_one, z_two, *rest):
    out, h_out, qh, zh, f1x, f2x, gx, f1z, f2z, gz, f3, sx, sz, zst = rest
    ln, rw = lane(), row()
    group, off = ln >> 4, ln & 15
    bottom, top, odd = wn == 0, wn == 3, wn % 2 == 1
    first, last = tile == 0, tile == tiles - 1
    base = (wn * NL).astype(F32) + 0.5

    def put_strip(u, x):
        zst[u] = x

    build_strips(tile, tiles, z_right, z_left, z_one, z_two, put_strip)

    def below(i):
        return jnp.where(odd, near[i], far[i])

    def above(i):
        return jnp.where(odd, far[i], near[i])

    speeds = [jnp.where(top, w[k], jnp.where(bottom, far[27 + k], near[27 + k])) for k in range(4)]
    w0, w0z, w0s, w1 = speeds

    surf, surf_z = strips[10], zst[10]
    strip_q = []
    for f in range(5):
        sign = MIRROR[f]
        bq, bz = b[f], z[81 + f]
        for k in range(4):
            qh[f, k] = jnp.where(bottom, sign * q[f, 3 - k], below(4 * f + k))
            qh[f, 4 + k] = jnp.where(top, bq, above(4 * f + k))
        zb, za = below(20 + f), above(20 + f)
        zh[f, 0] = jnp.where(bottom, sign * z[f * NL + 1], zb)
        zh[f, 1] = jnp.where(bottom, sign * z[f * NL], rs(zb, 4))
        zh[f, 2] = jnp.where(top, bz, za)
        zh[f, 3] = jnp.where(top, bz, rs(za, 4))
        s_lo, s_hi = strips[2 * f], strips[2 * f + 1]
        if f < 4:
            sb, sa = rl(below(25), 96 - 32 * f), rl(above(25), -32 * f)
        else:
            sb, sa = below(26), above(26)
        sb = jnp.where(bottom, sign * jnp.where(group == 7, rl(s_lo, -16), rl(s_lo, 80)), sb)
        sa = jnp.where(top, spread(surf, 1 + f), sa)
        strip_q.append((s_lo, s_hi, jnp.where(ln < 64, sa, sb)))

    def own_q(f, l):
        return q[f, l] if 0 <= l < NL else qh[f, l + 4 if l < 0 else l - 12]

    def halo_q(f, l):
        return z[f * NL + l] if 0 <= l < NL else zh[f, l + 2 if l < 0 else l - 14]

    h0, h0z = h[...], z[80]
    h0s, h0sz = spread(surf, 0), spread(surf_z, 0)
    (hx, hz), (hxz, hzz), (hxs, hzs) = slopes(h0, h0z, h0s, h0sz)
    ih, ihz, ihs = 1.0 / h0, 1.0 / h0z, 1.0 / h0s

    parts, patch = [], []
    for v in range(3):
        a1, a2, a3, g = fluxes([strip_q[f][v] for f in range(5)], move=(hxs, hzs, w0s))
        d1 = [d_lane(a1[f]) for f in range(5)]
        patch.append([strip_patch(d1[f]) for f in range(5)])
        parts.append((d1, a2, a3, g))
    halo3, patch_z = [], []
    for v in range(2):
        z1, z3 = fluxes([zst[2 * f + v] for f in range(5)], (1, 3))
        patch_z.append([strip_patch(d_lane(z1[f])) for f in range(5)])
        halo3.append(z3)

    def layer_shift(x, v, k):
        a = rl(x[v], -16 * k)
        c = rl(x[(v + (1 if k > 0 else -1)) % 3], -16 * k)
        return jnp.where(ln < 128 - 16 * k if k > 0 else ln >= -16 * k, a, c)

    strip_s = []
    for v in range(2):
        eta = (base + (8 * v + group).astype(F32)) / LAYERS
        done = []
        for f in range(5):
            dn, dg = (
                (layer_shift(x, v, -2) - layer_shift(x, v, 2)) + 8.0 * (layer_shift(x, v, 1) - layer_shift(x, v, -1))
                for x in ([parts[i][k][f] for i in range(3)] for k in (1, 3))
            )
            da, _ = d_ring(parts[v][2][f], halo3[v][f])
            s = strip_q[f][v] + C * (ihs * (eta * dg - dn) - (parts[v][0][f] + da))
            s = jnp.where(first & ((off == 2) | (off == 3)), jnp.where(off == 3, rl(s, -1), rl(s, -2)), s)
            s = jnp.where(last & ((off == 12) | (off == 13)), jnp.where(off == 12, rl(s, 1), rl(s, 2)), s)
            done.append(s)
        strip_s.append(done)

    def d_rows(f, l, at):
        m2, m1, p1, p2 = (f3[f, l, at + k : at + k + 8] for k in (-2, -1, 1, 2))
        return (m2 - p2) + 8.0 * (p1 - m1)

    def d_normal(ref, f, l):
        return (ref[f, l - 2] - ref[f, l + 2]) + 8.0 * (ref[f, l + 1] - ref[f, l - 1])

    def eta_of(l):
        return (base + l) / LAYERS

    def patch_shift(l):
        return 116 - 16 * (l & 7)

    def own_flux(l):
        a1, a2, a3, g = fluxes([own_q(f, l) for f in range(5)], move=(hx, hz, w0))
        for f in range(5):
            f2x[f, l + 4], gx[f, l + 4] = a2[f], g[f]
            if -2 <= l < 18:
                f1x[f, l + 4] = a1[f]
                f3[f, l + 4, 16:24] = a3[f]

    def put_halo(f, l, x):
        f3[f, l, 24:32] = x
        f3[f, l, 8:16] = x

    def halo_flux(l):
        a1, a2, a3, g = fluxes([halo_q(f, l) for f in range(5)], move=(hxz, hzz, w0z))
        for f in range(5):
            f2z[f, l + 2], gz[f, l + 2] = a2[f], g[f]
            put_halo(f, l + 4, a3[f])
            if 0 <= l < NL:
                f1z[f, l] = a1[f]

    def section(l):
        eta, shift = eta_of(l), patch_shift(l)
        own, halo = [], []
        for f in range(5):
            dx = patched(d_lane(f1x[f, l + 4]), rl(patch[(l >> 3) % 3][f], shift))
            da = d_rows(f, l + 4, 16)
            dn, dg = d_normal(f2x, f, l + 4), d_normal(gx, f, l + 4)
            own.append(own_q(f, l) + C * (ih * (eta * dg - dn) - (dx + da)))
            if 0 <= l < NL:
                dx = patched(d_lane(f1z[f, l]), rl(patch_z[l >> 3][f], shift))
                da = jnp.where(rw < 4, d_rows(f, l + 4, 24), d_rows(f, l + 4, 8))
                dn, dg = d_normal(f2z, f, l + 2), d_normal(gz, f, l + 2)
                halo.append(halo_q(f, l) + C * (ihz * (eta * dg - dn) - (dx + da)))
        for f in range(5):
            sx[f, l + 2] = own[f]
            if halo:
                sz[f, l] = halo[f]

    for l in range(-4, 20):
        own_flux(l)
        if -2 <= l < 18:
            halo_flux(l)
        if l - 2 >= -2:
            section(l - 2)
    for f in range(5):
        for k in range(2):
            sx[f, k] = jnp.where(bottom, MIRROR[f] * sx[f, 3 - k], sx[f, k])
            sx[f, 18 + k] = jnp.where(top, b[f], sx[f, 18 + k])

    h1, h1z, h1s = h0 + STEP * w0, h0z + STEP * w0z, h0s + STEP * w0s
    hx1 = SCALE * d_ends(h1, rl(strip_ends(h1s), -12))
    hz1 = SCALE * d_ring(h1, h1z)[0]
    ih1 = 1.0 / h1
    h_out[...] = 0.5 * (h0 + h1 + STEP * w1)
    ends = []
    for v in range(2):
        (a1,) = fluxes(strip_s[v], (1,))
        ends.append([strip_ends(a1[f]) for f in range(5)])

    def own_flux_two(l):
        a1, a2, a3, g = fluxes([sx[f, l + 2] for f in range(5)], move=(hx1, hz1, w1))
        for f in range(5):
            f2x[f, l + 4], gx[f, l + 4] = a2[f], g[f]
            if 0 <= l < NL:
                f1x[f, l + 4] = a1[f]
                f3[f, l + 4, 16:24] = a3[f]

    def halo_flux_two(l):
        (a3,) = fluxes([sz[f, l] for f in range(5)], (3,))
        for f in range(5):
            put_halo(f, l + 4, a3[f])

    def final(l):
        eta, shift = eta_of(l), patch_shift(l)
        done = []
        for f in range(5):
            dx = d_ends(f1x[f, l + 4], rl(ends[l >> 3][f], shift))
            da = d_rows(f, l + 4, 16)
            dn, dg = d_normal(f2x, f, l + 4), d_normal(gx, f, l + 4)
            rate = ih1 * (eta * dg - dn) - (dx + da)
            done.append(0.5 * (q[f, l] + sx[f, l + 2] + C * rate))
        for f in range(5):
            out[f, l] = done[f]

    for l in range(-2, 18):
        own_flux_two(l)
        if 0 <= l < NL:
            halo_flux_two(l)
        if l - 2 >= 0:
            final(l - 2)


def call(body, ins, outs, scratch=(), sems=0, space=VM):
    shapes = tuple(jax.ShapeDtypeStruct(s, F32) for s in outs)
    return pl.pallas_call(
        body,
        out_shape=shapes,
        in_specs=[space] * len(ins),
        out_specs=tuple([VM] * len(shapes)),
        scratch_shapes=[pltpu.VMEM(s, F32) for s in scratch] + [pltpu.SemaphoreType.DMA((sems,))] * (sems > 0),
        compiler_params=pltpu.CompilerParams(vmem_limit_bytes=40 * 1024 * 1024),
    )(*ins)


def where_am_i():
    return lax.axis_index("sx"), lax.axis_size("sx")


def stage_rows(*refs):
    pack_rows(lax.axis_index("az") % 2 == 1, *refs)


def stage_columns(*refs):
    pack_columns(lax.axis_index("sx") % 2 == 0, *refs)


def stage_second(*refs):
    pack_second(lax.axis_index("az") % 2 == 1, lax.axis_index("wn"), *where_am_i(), *refs)


def stage_near(*refs):
    pack_near(lax.axis_index("wn"), *refs)


def stage_advance(*refs):
    advance(lax.axis_index("wn"), *where_am_i(), *refs)


def swaps(size, start, wrap):
    pairs = [(i, (i + 1) % size) for i in range(start, size if wrap else size - 1, 2)]
    return pairs + [(j, i) for i, j in pairs]


def per_device(fields, height, behind):
    around = lax.axis_size("az")
    tiles = lax.axis_size("sx")
    plane = (8, 128)
    *own, one, two = call(
        stage_rows,
        [pltpu.with_memory_space_constraint(x, pltpu.HBM) for x in (fields, height, behind)],
        [fields.shape, height.shape, behind.shape] + [(HALF, *plane)] * 2,
        sems=3,
        space=pl.BlockSpec(memory_space=pltpu.HBM),
    )
    a2 = lax.ppermute(two, "az", swaps(around, 1, True))
    a1 = lax.ppermute(one, "az", swaps(around, 0, True))
    right, left, one, two = call(stage_columns, own, [(3, *plane)] * 4)
    s2 = lax.ppermute(two, "sx", swaps(tiles, 1, False))
    s1 = lax.ppermute(one, "sx", swaps(tiles, 0, False))
    halo, strips, w, near, far, z_right, z_left, one, two = call(
        stage_second,
        (*own, a1, a2, right, left, s1, s2),
        [(NP, *plane), (UNITS, *plane), (4, *plane), (27, *plane), (31, *plane)] + [(3, *plane)] * 4,
        [(27, *plane)] * 2,
    )
    far = lax.ppermute(far, "wn", [(1, 2), (2, 1), (3, 0)])
    s2 = lax.ppermute(two, "sx", swaps(tiles, 1, False))
    s1 = lax.ppermute(one, "sx", swaps(tiles, 0, False))
    (near,) = call(stage_near, (near, w, far, s1, s2), [(31, *plane)])
    near = lax.ppermute(near, "wn", [(0, 1), (1, 0), (2, 3), (3, 2)])
    return call(
        stage_advance,
        (*own, halo, strips, w, near, far, z_right, z_left, s1, s2),
        [(5, NL, 8, 128), (8, 128)],
        [(5, 8, 8, 128), (5, 4, 8, 128)]
        + [(5, 24, 8, 128)] * 3
        + [(5, NL, 8, 128)]
        + [(5, 20, 8, 128)] * 2
        + [(5, 24, 40, 128)]
        + [(5, 20, 8, 128), (5, NL, 8, 128), (UNITS, 8, 128)],
    )


def solution(mesh):
    in_specs = (P(None, "wn", "az", "sx"), P("az", "sx"), P(None, "az", "sx"))
    out_specs = (P(None, "wn", "az", "sx"), P("az", "sx"))
    return jax.shard_map(
        per_device, mesh=mesh, in_specs=in_specs, out_specs=out_specs, check_vma=False
    )
```

```python
import functools

import jax
import jax.numpy as jnp
from jax import lax
from jax.experimental import pallas as pl
from jax.experimental.pallas import tpu as pltpu
from jax.sharding import PartitionSpec as P

GAMMA = 1.4
CFL_STEP = 0.08
LAYERS = 64
NL = 16
NP = 86
HALF = 43
UNITS = 11
SCALE = LAYERS / 12.0
STEP = CFL_STEP / LAYERS
C = CFL_STEP / 12.0
VM = pl.BlockSpec(memory_space=pltpu.VMEM)
F32 = jnp.float32
MIRROR = (1.0, -1.0, -1.0, -1.0, 1.0)


def lane():
    return lax.broadcasted_iota(jnp.int32, (8, 128), 1)


def row():
    return lax.broadcasted_iota(jnp.int32, (8, 128), 0)


def rl(x, shift):
    return pltpu.roll(x, shift % 128, 1) if shift % 128 else x


def rs(x, shift):
    return pltpu.roll(x, shift % 8, 0) if shift % 8 else x


def d_lane(x):
    return (rl(x, 2) - rl(x, -2)) + 8.0 * (rl(x, -1) - rl(x, 1))


def strip_patch(d):
    off = lane() & 15
    return jnp.where((off == 12) | (off == 13), rl(d, 8), d)


def strip_ends(x):
    off = lane() & 15
    return jnp.where((off == 10) | (off == 11), rl(x, 8), x)


def d_ends(x, e):
    ln = lane()
    p1 = rl(jnp.where(ln < 1, e, x), -1)
    p2 = rl(jnp.where(ln < 2, e, x), -2)
    m1 = rl(jnp.where(ln >= 127, e, x), 1)
    m2 = rl(jnp.where(ln >= 126, e, x), 2)
    return (m2 - p2) + 8.0 * (p1 - m1)


def patched(d, patch):
    ln = lane()
    return jnp.where((ln < 2) | (ln >= 126), patch, d)


def ring(x, z, shift):
    keep = row() >= shift if shift > 0 else row() < 8 + shift
    a, b = rs(x, shift), rs(z, shift)
    return jnp.where(keep, a, b), jnp.where(keep, b, a)


def d_ring(x, z):
    m2, m1, p1, p2 = ring(x, z, 2), ring(x, z, 1), ring(x, z, -1), ring(x, z, -2)
    return tuple((m2[i] - p2[i]) + 8.0 * (p1[i] - m1[i]) for i in (0, 1))


def spread(x, group):
    ln = lane()
    x = rl(x, -16 * group)
    x = jnp.where(ln < 16, x, rl(x, 16))
    x = jnp.where(ln < 32, x, rl(x, 32))
    return jnp.where(ln < 64, x, rl(x, 64))


def pressure(q):
    kinetic = (q[1] * q[1] + q[2] * q[2] + q[3] * q[3]) / q[0]
    return (GAMMA - 1.0) * (q[4] - 0.5 * kinetic)


def speed(q, b):
    behind = pressure(b)
    return (pressure(q) - behind) / jnp.sqrt(GAMMA * behind * b[0])


def fluxes(q, want=(1, 2, 3), move=None):
    inv = 1.0 / q[0]
    v1, v2, v3 = q[1] * inv, q[2] * inv, q[3] * inv
    q11, q22, q33 = q[1] * v1, q[2] * v2, q[3] * v3
    p = (GAMMA - 1.0) * (q[4] - 0.5 * (q11 + q22 + q33))
    e = q[4] + p
    q12, q13, q23 = q[1] * v2, q[1] * v3, q[2] * v3
    out = []
    if 1 in want:
        out.append([q[1], q11 + p, q12, q13, e * v1])
    if 2 in want:
        out.append([q[2], q12, q22 + p, q23, e * v2])
    if 3 in want:
        out.append([q[3], q13, q23, q33 + p, e * v3])
    if move is not None:
        hx, hz, w = move
        s = hx * v1 + hz * v3
        t = s + w
        out.append([q[0] * t, q[1] * t + p * hx, q[2] * t, q[3] * t + p * hz, q[4] * t + p * s])
    return out


def slopes(h, hz, hs, hsz):
    ds, dsz = d_lane(hs), d_lane(hsz)
    x = SCALE * patched(d_lane(h), rl(strip_patch(ds), -12))
    xz = SCALE * patched(d_lane(hz), rl(strip_patch(dsz), -12))
    a, az = d_ring(h, hz)
    s, _ = d_ring(hs, hsz)
    return (x, SCALE * a), (xz, SCALE * az), (SCALE * ds, SCALE * s)


def plane_of(q, h, b):
    def get(i):
        if i < 80:
            return q[i // NL, i % NL]
        return h[...] if i == 80 else b[i - 81]

    return get


def unit_planes(u):
    return [8 * u + j for j in range(8)] if u < 10 else [80 + j for j in range(6)]


def columns(get, right, left):
    ln = lane()
    for v in range(3):
        r_acc = jnp.zeros((8, 128), F32)
        l_acc = jnp.zeros((8, 128), F32)
        for u in range(4 * v, min(4 * v + 4, UNITS)):
            for j, i in enumerate(unit_planes(u)):
                at = 16 * j + 4 * (u - 4 * v)
                x = rl(get(i), at + 4)
                r_acc = jnp.where((ln >= at) & (ln < at + 4), x, r_acc)
                at = (at + 4) % 128
                l_acc = jnp.where((ln >= at) & (ln < at + 4), x, l_acc)
        right[v] = r_acc
        left[v] = rl(l_acc, -4)


def to_pairs(even, right, left, one, two):
    for v in range(3):
        one[v] = jnp.where(even, right[v], left[v])
        two[v] = jnp.where(even, left[v], right[v])


def build_strips(tile, tiles, right, left, one, two, put):
    m = lane() & 3
    quad = (lane() >> 2) & 3
    even = tile % 2 == 0
    for v in range(3):
        lm, rm = left[v], right[v]
        end_l = jnp.where(m == 0, lm, jnp.where(m == 1, rl(lm, 1), jnp.where(m == 2, rl(lm, 2), rl(lm, 3))))
        end_r = jnp.where(m == 3, rm, jnp.where(m == 2, rl(rm, -1), jnp.where(m == 1, rl(rm, -2), rl(rm, -3))))
        lh = jnp.where(tile == 0, end_l, jnp.where(even, two[v], one[v]))
        rh = jnp.where(tile == tiles - 1, end_r, jnp.where(even, one[v], two[v]))
        for t in range(min(4, UNITS - 4 * v)):
            a, b, c, d = (rl(x, 4 * (i - t)) for i, x in enumerate((lh, lm, rm, rh)))
            put(4 * v + t, jnp.where(quad < 2, jnp.where(quad == 0, a, b), jnp.where(quad == 2, c, d)))


def pack_rows(odd, q_hbm, h_hbm, b_hbm, q, h, b, one, two, sems):
    copies = [
        pltpu.make_async_copy(x, y, sems.at[i]) for i, (x, y) in enumerate(((q_hbm, q), (h_hbm, h), (b_hbm, b)))
    ]
    for c in copies:
        c.start()
    for c in copies:
        c.wait()
    get = plane_of(q, h, b)
    mask = (row() >= 4) ^ odd
    for i in range(HALF):
        x, y = get(i), rs(get(i + HALF), 4)
        one[i] = jnp.where(mask, x, y)
        two[i] = jnp.where(mask, y, x)


def pack_columns(even, q, h, b, right, left, one, two):
    columns(plane_of(q, h, b), right, left)
    to_pairs(even, right, left, one, two)


def pack_second(odd, wn, tile, tiles, q, h, b, a1, a2, right, left, s1, s2, *outs):
    z, strips, w, near, far, z_right, z_left, z_one, z_two, hi, lo = outs
    ln, rw = lane(), row()
    mask = (rw >= 4) ^ odd
    for i in range(HALF):
        x, y = a2[i], a1[i]
        z[i] = jnp.where(mask, x, y)
        z[i + HALF] = rs(jnp.where(mask, y, x), 4)

    def put(u, x):
        strips[u] = x

    build_strips(tile, tiles, right, left, s1, s2, put)
    surf = strips[10]
    own, bq = [q[f, 15] for f in range(5)], [b[f] for f in range(5)]
    zq, bz = [z[f * NL + 15] for f in range(5)], [z[81 + f] for f in range(5)]
    sq = [strips[2 * f + 1] for f in range(5)]
    w0 = speed(own, bq)
    w0z = speed(zq, bz)
    w0s = spread(speed(sq, [rl(surf, 16 * (6 - f)) for f in range(5)]), 7)
    hx = SCALE * patched(d_lane(h[...]), rl(strip_patch(d_lane(surf)), -12))
    hz = SCALE * d_ring(h[...], z[80])[0]
    (f1s,) = fluxes(sq, (1,))
    (f3z,) = fluxes(zq, (3,))
    levels = []
    for x in ([q[f, 13] for f in range(5)], [q[f, 14] for f in range(5)], own, bq):
        levels.append(fluxes(x, move=(hx, hz, w0)))
    eta = (LAYERS - 0.5) / LAYERS
    ih = 1.0 / h[...]
    top = []
    for f in range(5):
        dx = patched(d_lane(levels[2][0][f]), rl(strip_patch(d_lane(f1s[f])), -124))
        da, _ = d_ring(levels[2][2][f], f3z[f])
        dn, dg = ((levels[0][k][f] - 8.0 * levels[1][k][f]) + 7.0 * levels[3][k][f] for k in (1, 3))
        top.append(own[f] + C * (ih * (eta * dg - dn) - (dx + da)))
    speeds = (w0, w0z, w0s, speed(top, bq))
    for k in range(4):
        w[k] = speeds[k]
        near[27 + k] = speeds[k]
    near_rows = (rw < 2) | (rw >= 6)
    hi_s = hi[26] = strips[9]
    lo_s = lo[26] = strips[8]
    for f in range(5):
        for k in range(4):
            hi[4 * f + k] = q[f, 12 + k]
            lo[4 * f + k] = q[f, k]
        hi[20 + f] = jnp.where(near_rows, z[f * NL + 14], rs(z[f * NL + 15], 4))
        lo[20 + f] = jnp.where(near_rows, z[f * NL], rs(z[f * NL + 1], 4))
        if f < 4:
            inside = (ln >= 32 * f) & (ln < 32 * f + 32)
            hi_s = jnp.where(inside, rl(strips[2 * f + 1], 32 * f + 32), hi_s)
            lo_s = jnp.where(inside, rl(strips[2 * f], 32 * f), lo_s)
    hi[25] = hi_s
    lo[25] = lo_s
    for i in range(27):
        near[i] = jnp.where(wn % 2 == 0, hi[i], lo[i])
        far[i] = jnp.where(wn == 1, hi[i], lo[i])
    columns(lambda i: z[i], z_right, z_left)
    to_pairs(tile % 2 == 0, z_right, z_left, z_one, z_two)


def pack_far(wn, far, w, near, out):
    for i in range(27):
        out[i] = far[i]
    for k in range(4):
        out[27 + k] = jnp.where(wn == 2, near[27 + k], w[k])


def advance(wn, tile, tiles, q, h, b, z, strips, w, near, far, z_right, z_left, z_one, z_two, *rest):
    out, h_out, qx, qz, f1x, f2x, gx, f1z, f2z, gz, f3, sx, sz, pt, ptz, zst = rest
    first, last = tile == 0, tile == tiles - 1

    def put_strip(u, x):
        zst[u] = x

    build_strips(tile, tiles, z_right, z_left, z_one, z_two, put_strip)
    odd = wn % 2 == 1

    def below(i):
        return jnp.where(odd, near[i], far[i])

    def above(i):
        return jnp.where(odd, far[i], near[i])

    ln, rw = lane(), row()
    group, off = ln >> 4, ln & 15
    bottom, top = wn == 0, wn == 3
    near_rows = (rw < 2) | (rw >= 6)

    speeds = [jnp.where(top, w[k], jnp.where(wn == 2, near[27 + k], far[27 + k])) for k in range(4)]
    w0, w0z, w0s, w1 = speeds

    surf, surf_z = strips[10], zst[10]
    strip_q = []
    for f in range(5):
        sign = MIRROR[f]
        bq, bz = b[f], z[81 + f]
        for k in range(NL):
            qx[f, 4 + k] = q[f, k]
            qz[f, 2 + k] = z[f * NL + k]
        for k in range(4):
            qx[f, k] = jnp.where(bottom, sign * q[f, 3 - k], below(4 * f + k))
            qx[f, 20 + k] = jnp.where(top, bq, above(4 * f + k))
        zb, za = below(20 + f), above(20 + f)
        qz[f, 0] = jnp.where(bottom, sign * z[f * NL + 1], zb)
        qz[f, 1] = jnp.where(bottom, sign * z[f * NL], rs(zb, 4))
        qz[f, 18] = jnp.where(top, bz, za)
        qz[f, 19] = jnp.where(top, bz, rs(za, 4))
        s_lo, s_hi = strips[2 * f], strips[2 * f + 1]
        if f < 4:
            sb, sa = rl(below(25), 96 - 32 * f), rl(above(25), -32 * f)
        else:
            sb, sa = below(26), above(26)
        sb = jnp.where(bottom, sign * jnp.where(group == 7, rl(s_lo, -16), rl(s_lo, 80)), sb)
        sa = jnp.where(top, spread(surf, 1 + f), sa)
        strip_q.append((s_lo, s_hi, jnp.where(ln < 64, sa, sb)))

    h0, h0z = h[...], z[80]
    h0s, h0sz = spread(surf, 0), spread(surf_z, 0)
    (hx, hz), (hxz, hzz), (hxs, hzs) = slopes(h0, h0z, h0s, h0sz)
    ih, ihz, ihs = 1.0 / h0, 1.0 / h0z, 1.0 / h0s
    base = wn * NL

    parts = []
    for v in range(3):
        x = [strip_q[f][v] for f in range(5)]
        a1, a2, a3, g = fluxes(x, move=(hxs, hzs, w0s))
        d1 = [d_lane(a1[f]) for f in range(5)]
        for f in range(5):
            pt[f, v] = strip_patch(d1[f])
        parts.append((d1, a2, a3, g))
    halo3 = []
    for v in range(2):
        x = [zst[2 * f + v] for f in range(5)]
        z1, z3 = fluxes(x, (1, 3))
        for f in range(5):
            ptz[f, v] = strip_patch(d_lane(z1[f]))
        halo3.append(z3)

    def layer_shift(x, v, k):
        a = rl(x[v], -16 * k)
        c = rl(x[(v + (1 if k > 0 else -1)) % 3], -16 * k)
        return jnp.where(ln < 128 - 16 * k if k > 0 else ln >= -16 * k, a, c)

    strip_s = []
    for v in range(2):
        eta = ((base + 8 * v + group).astype(F32) + 0.5) / LAYERS
        done = []
        for f in range(5):
            dn, dg = (
                (layer_shift(x, v, -2) - layer_shift(x, v, 2)) + 8.0 * (layer_shift(x, v, 1) - layer_shift(x, v, -1))
                for x in ([parts[i][k][f] for i in range(3)] for k in (1, 3))
            )
            da, _ = d_ring(parts[v][2][f], halo3[v][f])
            s = strip_q[f][v] + C * (ihs * (eta * dg - dn) - (parts[v][0][f] + da))
            s = jnp.where(first & ((off == 2) | (off == 3)), jnp.where(off == 3, rl(s, -1), rl(s, -2)), s)
            s = jnp.where(last & ((off == 12) | (off == 13)), jnp.where(off == 12, rl(s, 1), rl(s, 2)), s)
            done.append(s)
        strip_s.append(done)

    def d_rows(ref, f, l, at):
        m2, m1, p1, p2 = (ref[f, l, pl.ds(at + k, 8)] for k in (-2, -1, 1, 2))
        return (m2 - p2) + 8.0 * (p1 - m1)

    def d_around(f, l):
        return d_rows(f3, f, l, 16)

    def d_around_halo(f, l):
        return jnp.where(rw < 4, d_rows(f3, f, l, 24), d_rows(f3, f, l, 8))

    def batches(first_l, count, size, body):
        def step(i, _):
            todo = []
            for k in range(size):
                todo += body(first_l + i * size + k)
            for ref, at, x in todo:
                ref[at] = x
            return 0

        lax.fori_loop(0, count // size, step, 0)

    def put_halo(f, l, x):
        return [(f3, (f, l, slice(24, 32)), x), (f3, (f, l, slice(8, 16)), x)]

    def own_flux(l):
        a1, a2, a3, g = fluxes([qx[f, l + 4] for f in range(5)], move=(hx, hz, w0))
        todo = []
        for f in range(5):
            todo += [(r, (f, l + 4), x[f]) for r, x in ((f1x, a1), (f2x, a2), (gx, g))]
            todo += [(f3, (f, l + 4, slice(16, 24)), a3[f])]
        return todo

    def halo_flux(l):
        a1, a2, a3, g = fluxes([qz[f, l + 2] for f in range(5)], move=(hxz, hzz, w0z))
        todo = []
        for f in range(5):
            todo += [(r, (f, l + 2), x[f]) for r, x in ((f1z, a1), (f2z, a2), (gz, g))] + put_halo(f, l + 4, a3[f])
        return todo

    batches(-4, 24, 4, own_flux)
    batches(-2, 20, 4, halo_flux)

    def d_normal(ref, f, l):
        return (ref[f, l - 2] - ref[f, l + 2]) + 8.0 * (ref[f, l + 1] - ref[f, l - 1])

    def eta_of(l):
        return ((base + l).astype(F32) + 0.5) / LAYERS

    def patch_shift(l):
        return 116 - 16 * (l & 7)

    def own_section(l):
        eta, shift, todo = eta_of(l), patch_shift(l), []
        third = (l + 8) >> 3
        third = jnp.where((third == 0) | (third == 3), 2, third - 1)
        for f in range(5):
            dx = patched(d_lane(f1x[f, l + 4]), pltpu.roll(pt[f, third], shift, 1))
            da = d_around(f, l + 4)
            dn, dg = d_normal(f2x, f, l + 4), d_normal(gx, f, l + 4)
            todo.append((sx, (f, l + 2), qx[f, l + 4] + C * (ih * (eta * dg - dn) - (dx + da))))
        return todo

    def halo_section(l):
        eta, shift, todo = eta_of(l), patch_shift(l), []
        for f in range(5):
            dx = patched(d_lane(f1z[f, l + 2]), pltpu.roll(ptz[f, l >> 3], shift, 1))
            da = d_around_halo(f, l + 4)
            dn, dg = d_normal(f2z, f, l + 2), d_normal(gz, f, l + 2)
            todo.append((sz, (f, l), qz[f, l + 2] + C * (ihz * (eta * dg - dn) - (dx + da))))
        return todo

    batches(-2, 20, 4, own_section)
    batches(0, NL, 4, halo_section)
    for f in range(5):
        for k in range(2):
            sx[f, k] = jnp.where(bottom, MIRROR[f] * sx[f, 3 - k], sx[f, k])
            sx[f, 18 + k] = jnp.where(top, b[f], sx[f, 18 + k])

    h1, h1z, h1s = h0 + STEP * w0, h0z + STEP * w0z, h0s + STEP * w0s
    hx1 = SCALE * d_ends(h1, rl(strip_ends(h1s), -12))
    hz1 = SCALE * d_ring(h1, h1z)[0]
    ih1 = 1.0 / h1
    h_out[...] = 0.5 * (h0 + h1 + STEP * w1)
    for v in range(2):
        (a1,) = fluxes(strip_s[v], (1,))
        for f in range(5):
            pt[f, v] = strip_ends(a1[f])

    def own_flux_two(l):
        a1, a2, a3, g = fluxes([sx[f, l + 2] for f in range(5)], move=(hx1, hz1, w1))
        todo = []
        for f in range(5):
            todo += [(r, (f, l + 4), x[f]) for r, x in ((f1x, a1), (f2x, a2), (gx, g))]
            todo += [(f3, (f, l + 4, slice(16, 24)), a3[f])]
        return todo

    def halo_flux_two(l):
        (a3,) = fluxes([sz[f, l] for f in range(5)], (3,))
        return [x for f in range(5) for x in put_halo(f, l + 4, a3[f])]

    def final(l):
        eta, shift, todo = eta_of(l), patch_shift(l), []
        for f in range(5):
            dx = d_ends(f1x[f, l + 4], pltpu.roll(pt[f, l >> 3], shift, 1))
            da = d_around(f, l + 4)
            dn, dg = d_normal(f2x, f, l + 4), d_normal(gx, f, l + 4)
            rate = ih1 * (eta * dg - dn) - (dx + da)
            todo.append((out, (f, l), 0.5 * (qx[f, l + 4] + sx[f, l + 2] + C * rate)))
        return todo

    batches(-2, 20, 4, own_flux_two)
    batches(0, NL, 4, halo_flux_two)
    batches(0, NL, 4, final)


def call(body, ins, outs, scratch=(), sems=0, space=VM):
    shapes = tuple(jax.ShapeDtypeStruct(s, F32) for s in outs)
    return pl.pallas_call(
        body,
        out_shape=shapes,
        in_specs=[space] * len(ins),
        out_specs=tuple([VM] * len(shapes)),
        scratch_shapes=[pltpu.VMEM(s, F32) for s in scratch] + [pltpu.SemaphoreType.DMA((sems,))] * (sems > 0),
        compiler_params=pltpu.CompilerParams(vmem_limit_bytes=40 * 1024 * 1024),
    )(*ins)


def where_am_i():
    return lax.axis_index("sx"), lax.axis_size("sx")


def stage_rows(*refs):
    pack_rows(lax.axis_index("az") % 2 == 1, *refs)


def stage_columns(*refs):
    pack_columns(lax.axis_index("sx") % 2 == 0, *refs)


def stage_second(*refs):
    pack_second(lax.axis_index("az") % 2 == 1, lax.axis_index("wn"), *where_am_i(), *refs)


def stage_far(*refs):
    pack_far(lax.axis_index("wn"), *refs)


def stage_advance(*refs):
    advance(lax.axis_index("wn"), *where_am_i(), *refs)


def swaps(size, start, wrap):
    pairs = [(i, (i + 1) % size) for i in range(start, size if wrap else size - 1, 2)]
    return pairs + [(j, i) for i, j in pairs]


def per_device(fields, height, behind):
    around = lax.axis_size("az")
    tiles = lax.axis_size("sx")
    plane = (8, 128)
    *own, one, two = call(
        stage_rows,
        [pltpu.with_memory_space_constraint(x, pltpu.HBM) for x in (fields, height, behind)],
        [fields.shape, height.shape, behind.shape] + [(HALF, *plane)] * 2,
        sems=3,
        space=pl.BlockSpec(memory_space=pltpu.HBM),
    )
    a2 = lax.ppermute(two, "az", swaps(around, 1, True))
    a1 = lax.ppermute(one, "az", swaps(around, 0, True))
    right, left, one, two = call(stage_columns, own, [(3, *plane)] * 4)
    s2 = lax.ppermute(two, "sx", swaps(tiles, 1, False))
    s1 = lax.ppermute(one, "sx", swaps(tiles, 0, False))
    halo, strips, w, near, far, z_right, z_left, one, two = call(
        stage_second,
        (*own, a1, a2, right, left, s1, s2),
        [(NP, *plane), (UNITS, *plane), (4, *plane), (31, *plane), (27, *plane)] + [(3, *plane)] * 4,
        [(27, *plane)] * 2,
    )
    near = lax.ppermute(near, "wn", [(0, 1), (1, 0), (2, 3), (3, 2)])
    s2 = lax.ppermute(two, "sx", swaps(tiles, 1, False))
    s1 = lax.ppermute(one, "sx", swaps(tiles, 0, False))
    (far,) = call(stage_far, (far, w, near), [(31, *plane)])
    far = lax.ppermute(far, "wn", [(1, 2), (2, 1), (3, 0)])
    return call(
        stage_advance,
        (*own, halo, strips, w, near, far, z_right, z_left, s1, s2),
        [(5, NL, 8, 128), (8, 128)],
        [(5, 24, 8, 128), (5, 20, 8, 128)]
        + [(5, 24, 8, 128)] * 3
        + [(5, 20, 8, 128)] * 3
        + [(5, 24, 40, 128)]
        + [(5, 20, 8, 128), (5, NL, 8, 128), (5, 3, 8, 128), (5, 2, 8, 128), (UNITS, 8, 128)],
    )


def solution(mesh):
    in_specs = (P(None, "wn", "az", "sx"), P("az", "sx"), P(None, "az", "sx"))
    out_specs = (P(None, "wn", "az", "sx"), P("az", "sx"))
    return jax.shard_map(
        per_device, mesh=mesh, in_specs=in_specs, out_specs=out_specs, check_vma=False
    )
```

```python
import functools

import jax
import jax.numpy as jnp
from jax import lax
from jax.experimental import pallas as pl
from jax.experimental.pallas import tpu as pltpu
from jax.sharding import PartitionSpec as P

GAMMA = 1.4
CFL_STEP = 0.08
LAYERS = 64
NL = 16
NP = 86
HALF = 43
UNITS = 11
SCALE = LAYERS / 12.0
STEP = CFL_STEP / LAYERS
C = CFL_STEP / 12.0
VM = pl.BlockSpec(memory_space=pltpu.VMEM)
F32 = jnp.float32
MIRROR = (1.0, -1.0, -1.0, -1.0, 1.0)


def lane():
    return lax.broadcasted_iota(jnp.int32, (8, 128), 1)


def row():
    return lax.broadcasted_iota(jnp.int32, (8, 128), 0)


def rl(x, shift):
    return pltpu.roll(x, shift % 128, 1) if shift % 128 else x


def rs(x, shift):
    return pltpu.roll(x, shift % 8, 0) if shift % 8 else x


def d_lane(x):
    return (rl(x, 2) - rl(x, -2)) + 8.0 * (rl(x, -1) - rl(x, 1))


def strip_patch(d):
    off = lane() & 15
    return jnp.where((off == 12) | (off == 13), rl(d, 8), d)


def strip_ends(x):
    off = lane() & 15
    return jnp.where((off == 10) | (off == 11), rl(x, 8), x)


def d_ends(x, e):
    ln = lane()
    p1 = rl(jnp.where(ln < 1, e, x), -1)
    p2 = rl(jnp.where(ln < 2, e, x), -2)
    m1 = rl(jnp.where(ln >= 127, e, x), 1)
    m2 = rl(jnp.where(ln >= 126, e, x), 2)
    return (m2 - p2) + 8.0 * (p1 - m1)


def patched(d, patch):
    ln = lane()
    return jnp.where((ln < 2) | (ln >= 126), patch, d)


def ring(x, z, shift):
    keep = row() >= shift if shift > 0 else row() < 8 + shift
    a, b = rs(x, shift), rs(z, shift)
    return jnp.where(keep, a, b), jnp.where(keep, b, a)


def d_ring(x, z):
    m2, m1, p1, p2 = ring(x, z, 2), ring(x, z, 1), ring(x, z, -1), ring(x, z, -2)
    return tuple((m2[i] - p2[i]) + 8.0 * (p1[i] - m1[i]) for i in (0, 1))


def spread(x, group):
    ln = lane()
    x = rl(x, -16 * group)
    x = jnp.where(ln < 16, x, rl(x, 16))
    x = jnp.where(ln < 32, x, rl(x, 32))
    return jnp.where(ln < 64, x, rl(x, 64))


def pressure(q):
    kinetic = (q[1] * q[1] + q[2] * q[2] + q[3] * q[3]) / q[0]
    return (GAMMA - 1.0) * (q[4] - 0.5 * kinetic)


def speed(q, b):
    behind = pressure(b)
    return (pressure(q) - behind) / jnp.sqrt(GAMMA * behind * b[0])


def fluxes(q, want=(1, 2, 3), move=None):
    inv = 1.0 / q[0]
    v1, v2, v3 = q[1] * inv, q[2] * inv, q[3] * inv
    q11, q22, q33 = q[1] * v1, q[2] * v2, q[3] * v3
    p = (GAMMA - 1.0) * (q[4] - 0.5 * (q11 + q22 + q33))
    e = q[4] + p
    q12, q13, q23 = q[1] * v2, q[1] * v3, q[2] * v3
    out = []
    if 1 in want:
        out.append([q[1], q11 + p, q12, q13, e * v1])
    if 2 in want:
        out.append([q[2], q12, q22 + p, q23, e * v2])
    if 3 in want:
        out.append([q[3], q13, q23, q33 + p, e * v3])
    if move is not None:
        hx, hz, w = move
        s = hx * v1 + hz * v3
        t = s + w
        out.append([q[0] * t, q[1] * t + p * hx, q[2] * t, q[3] * t + p * hz, q[4] * t + p * s])
    return out


def slopes(h, hz, hs, hsz):
    ds, dsz = d_lane(hs), d_lane(hsz)
    x = SCALE * patched(d_lane(h), rl(strip_patch(ds), -12))
    xz = SCALE * patched(d_lane(hz), rl(strip_patch(dsz), -12))
    a, az = d_ring(h, hz)
    s, _ = d_ring(hs, hsz)
    return (x, SCALE * a), (xz, SCALE * az), (SCALE * ds, SCALE * s)


def plane_of(q, h, b):
    def get(i):
        if i < 80:
            return q[i // NL, i % NL]
        return h[...] if i == 80 else b[i - 81]

    return get


def unit_planes(u):
    return [8 * u + j for j in range(8)] if u < 10 else [80 + j for j in range(6)]


def columns(get, right, left):
    ln = lane()
    for v in range(3):
        r_acc = jnp.zeros((8, 128), F32)
        l_acc = jnp.zeros((8, 128), F32)
        for u in range(4 * v, min(4 * v + 4, UNITS)):
            for j, i in enumerate(unit_planes(u)):
                at = 16 * j + 4 * (u - 4 * v)
                x = rl(get(i), at + 4)
                r_acc = jnp.where((ln >= at) & (ln < at + 4), x, r_acc)
                at = (at + 4) % 128
                l_acc = jnp.where((ln >= at) & (ln < at + 4), x, l_acc)
        right[v] = r_acc
        left[v] = rl(l_acc, -4)


def to_pairs(even, right, left, one, two):
    for v in range(3):
        one[v] = jnp.where(even, right[v], left[v])
        two[v] = jnp.where(even, left[v], right[v])


def build_strips(tile, tiles, right, left, one, two, put):
    m = lane() & 3
    quad = (lane() >> 2) & 3
    even = tile % 2 == 0
    for v in range(3):
        lm, rm = left[v], right[v]
        end_l = jnp.where(m == 0, lm, jnp.where(m == 1, rl(lm, 1), jnp.where(m == 2, rl(lm, 2), rl(lm, 3))))
        end_r = jnp.where(m == 3, rm, jnp.where(m == 2, rl(rm, -1), jnp.where(m == 1, rl(rm, -2), rl(rm, -3))))
        lh = jnp.where(tile == 0, end_l, jnp.where(even, two[v], one[v]))
        rh = jnp.where(tile == tiles - 1, end_r, jnp.where(even, one[v], two[v]))
        for t in range(min(4, UNITS - 4 * v)):
            a, b, c, d = (rl(x, 4 * (i - t)) for i, x in enumerate((lh, lm, rm, rh)))
            put(4 * v + t, jnp.where(quad < 2, jnp.where(quad == 0, a, b), jnp.where(quad == 2, c, d)))


def pack_rows(odd, q_hbm, h_hbm, b_hbm, q, h, b, one, two, sems):
    copies = [
        pltpu.make_async_copy(x, y, sems.at[i]) for i, (x, y) in enumerate(((q_hbm, q), (h_hbm, h), (b_hbm, b)))
    ]
    for c in copies:
        c.start()
    for c in copies:
        c.wait()
    get = plane_of(q, h, b)
    mask = (row() >= 4) ^ odd
    for i in range(HALF):
        x, y = get(i), rs(get(i + HALF), 4)
        one[i] = jnp.where(mask, x, y)
        two[i] = jnp.where(mask, y, x)


def pack_columns(even, q, h, b, right, left, one, two):
    columns(plane_of(q, h, b), right, left)
    to_pairs(even, right, left, one, two)


def pack_second(odd, wn, tile, tiles, q, h, b, a1, a2, right, left, s1, s2, *outs):
    z, strips, w, near, far, z_right, z_left, z_one, z_two, hi, lo = outs
    ln, rw = lane(), row()
    mask = (rw >= 4) ^ odd
    for i in range(HALF):
        x, y = a2[i], a1[i]
        z[i] = jnp.where(mask, x, y)
        z[i + HALF] = rs(jnp.where(mask, y, x), 4)

    def put(u, x):
        strips[u] = x

    build_strips(tile, tiles, right, left, s1, s2, put)
    surf = strips[10]
    own, bq = [q[f, 15] for f in range(5)], [b[f] for f in range(5)]
    zq, bz = [z[f * NL + 15] for f in range(5)], [z[81 + f] for f in range(5)]
    sq = [strips[2 * f + 1] for f in range(5)]
    w0 = speed(own, bq)
    w0z = speed(zq, bz)
    w0s = spread(speed(sq, [rl(surf, 16 * (6 - f)) for f in range(5)]), 7)
    hx = SCALE * patched(d_lane(h[...]), rl(strip_patch(d_lane(surf)), -12))
    hz = SCALE * d_ring(h[...], z[80])[0]
    (f1s,) = fluxes(sq, (1,))
    (f3z,) = fluxes(zq, (3,))
    levels = []
    for x in ([q[f, 13] for f in range(5)], [q[f, 14] for f in range(5)], own, bq):
        levels.append(fluxes(x, move=(hx, hz, w0)))
    eta = (LAYERS - 0.5) / LAYERS
    ih = 1.0 / h[...]
    top = []
    for f in range(5):
        dx = patched(d_lane(levels[2][0][f]), rl(strip_patch(d_lane(f1s[f])), -124))
        da, _ = d_ring(levels[2][2][f], f3z[f])
        dn, dg = ((levels[0][k][f] - 8.0 * levels[1][k][f]) + 7.0 * levels[3][k][f] for k in (1, 3))
        top.append(own[f] + C * (ih * (eta * dg - dn) - (dx + da)))
    speeds = (w0, w0z, w0s, speed(top, bq))
    for k in range(4):
        w[k] = speeds[k]
        near[27 + k] = speeds[k]
    near_rows = (rw < 2) | (rw >= 6)
    hi_s = hi[26] = strips[9]
    lo_s = lo[26] = strips[8]
    for f in range(5):
        for k in range(4):
            hi[4 * f + k] = q[f, 12 + k]
            lo[4 * f + k] = q[f, k]
        hi[20 + f] = jnp.where(near_rows, z[f * NL + 14], rs(z[f * NL + 15], 4))
        lo[20 + f] = jnp.where(near_rows, z[f * NL], rs(z[f * NL + 1], 4))
        if f < 4:
            inside = (ln >= 32 * f) & (ln < 32 * f + 32)
            hi_s = jnp.where(inside, rl(strips[2 * f + 1], 32 * f + 32), hi_s)
            lo_s = jnp.where(inside, rl(strips[2 * f], 32 * f), lo_s)
    hi[25] = hi_s
    lo[25] = lo_s
    for i in range(27):
        near[i] = jnp.where(wn % 2 == 0, hi[i], lo[i])
        far[i] = jnp.where(wn == 1, hi[i], lo[i])
    columns(lambda i: z[i], z_right, z_left)
    to_pairs(tile % 2 == 0, z_right, z_left, z_one, z_two)


def pack_far(wn, far, w, near, out):
    for i in range(27):
        out[i] = far[i]
    for k in range(4):
        out[27 + k] = jnp.where(wn == 2, near[27 + k], w[k])


def d_rows(f3, f, l, at):
    m2, m1, p1, p2 = (f3[f, l, pl.ds(at + k, 8)] for k in (-2, -1, 1, 2))
    return (m2 - p2) + 8.0 * (p1 - m1)


def d_around(f3, f, l):
    return d_rows(f3, f, l, 16)


def d_around_halo(f3, f, l):
    return jnp.where(row() < 4, d_rows(f3, f, l, 24), d_rows(f3, f, l, 8))


def put_halo(f3, f, l, x):
    return [(f3, (f, l, slice(24, 32)), x), (f3, (f, l, slice(8, 16)), x)]


def d_normal(get, l):
    return (get(l - 2) - get(l + 2)) + 8.0 * (get(l + 1) - get(l - 1))


def plane_at(ref, f):
    return lambda l: ref[f, l]


def patch_shift(l):
    return 116 - 16 * (l & 7)


def edges(patch):
    return patched(jnp.zeros_like(patch), patch)


def batches(first_l, count, size, body):
    def step(i, _):
        todo = []
        for k in range(size):
            todo += body(first_l + i * size + k)
        for ref, at, x in todo:
            ref[at] = x
        return 0

    lax.fori_loop(0, count // size, step, 0)


def prepare(wn, q, h, z, strips, _far, tx, bx, tz, bz, ez, f1x, f2x, gx, f1z, f2z, gz, f3, pt):
    h0, h0z = h[...], z[80]
    hx = SCALE * patched(d_lane(h0), rl(strip_patch(d_lane(spread(strips[10], 0))), -12))
    hz, hzz = (SCALE * x for x in d_ring(h0, h0z))
    ih, ihz = C / h0, C / h0z
    base = wn * NL
    for v in range(2):
        (a1,) = fluxes([strips[2 * f + v] for f in range(5)], (1,))
        for f in range(5):
            pt[f, v] = strip_patch(d_lane(a1[f]))

    def own_flux(l):
        a1, a2, a3, g = fluxes([q[f, l] for f in range(5)], move=(hx, hz, 0.0))
        todo = []
        for f in range(5):
            todo += [(r, (f, l), x[f]) for r, x in ((f1x, a1), (f2x, a2), (gx, g))]
            todo += [(f3, (f, l, slice(16, 24)), a3[f])]
        return todo

    def halo_flux(l):
        a1, a2, a3 = fluxes([z[f * NL + l] for f in range(5)])
        todo = []
        for f in range(5):
            todo += [(r, (f, l), x) for r, x in ((f1z, a1[f]), (f2z, a2[f]), (gz, hzz * a3[f]))]
            todo += put_halo(f3, f, l, a3[f])
        return todo

    batches(0, NL, 4, own_flux)
    batches(0, NL, 4, halo_flux)

    def own_surface(f, l):
        dx = patched(d_lane(f1x[f, l]), pltpu.roll(pt[f, l >> 3], patch_shift(l), 1))
        return q[f, l] - C * (dx + d_around(f3, f, l))

    def halo_surface(f, l):
        ln = lane()
        dx = jnp.where((ln < 2) | (ln >= 126), 0.0, d_lane(f1z[f, l]))
        return z[f * NL + l] - C * (dx + d_around_halo(f3, f, l))

    def own_inner(l):
        k, todo = ih * (((base + l).astype(F32) + 0.5) / LAYERS), []
        for f in range(5):
            t = own_surface(f, l) + (k * d_normal(plane_at(gx, f), l) - ih * d_normal(plane_at(f2x, f), l))
            todo += [(tx, (f, l), t), (bx, (f, l), k * d_normal(plane_at(q, f), l))]
        return todo

    def halo_inner(l):
        k, todo = ihz * (((base + l).astype(F32) + 0.5) / LAYERS), []
        for f in range(5):
            t = halo_surface(f, l) + (k * d_normal(plane_at(gz, f), l) - ihz * d_normal(plane_at(f2z, f), l))
            todo += [(tz, (f, l), t), (bz, (f, l), k * d_normal(lambda i, f=f: z[f * NL + i], l))]
            todo += [(ez, (f, l), k * d_normal(plane_at(f1z, f), l))]
        return todo

    def outer(l):
        return [(tx, (f, l), own_surface(f, l)) for f in range(5)] + [
            (tz, (f, l), halo_surface(f, l)) for f in range(5)
        ]

    batches(2, 12, 4, own_inner)
    batches(2, 12, 4, halo_inner)
    for l in (0, 14):
        batches(l, 2, 2, outer)


def advance(wn, tile, tiles, q, h, b, z, strips, w, near, far, z_right, z_left, z_one, z_two, tx, bx, tz, bz, ez, *rest):
    out, h_out, qw, zw, f1w, f2w, gw, f2zw, gzw, f1x, f2x, gx, f3, sx, sz, pt, ptz, zst = rest
    first, last = tile == 0, tile == tiles - 1

    def put_strip(u, x):
        zst[u] = x

    build_strips(tile, tiles, z_right, z_left, z_one, z_two, put_strip)
    odd = wn % 2 == 1

    def below(i):
        return jnp.where(odd, near[i], far[i])

    def above(i):
        return jnp.where(odd, far[i], near[i])

    ln, rw = lane(), row()
    group, off = ln >> 4, ln & 15
    bottom, top = wn == 0, wn == 3
    near_rows = (rw < 2) | (rw >= 6)

    speeds = [jnp.where(top, w[k], jnp.where(wn == 2, near[27 + k], far[27 + k])) for k in range(4)]
    w0, w0z, w0s, w1 = speeds

    surf, surf_z = strips[10], zst[10]
    strip_q = []
    for f in range(5):
        sign = MIRROR[f]
        bq, bz_ = b[f], z[81 + f]
        for k in range(4):
            qw[f, k] = jnp.where(bottom, sign * q[f, 3 - k], below(4 * f + k))
            qw[f, 4 + k] = q[f, k]
            qw[f, 8 + k] = q[f, 12 + k]
            qw[f, 12 + k] = jnp.where(top, bq, above(4 * f + k))
            zw[f, 2 + k] = z[f * NL + k]
            zw[f, 6 + k] = z[f * NL + 12 + k]
        zb, za = below(20 + f), above(20 + f)
        zw[f, 0] = jnp.where(bottom, sign * z[f * NL + 1], zb)
        zw[f, 1] = jnp.where(bottom, sign * z[f * NL], rs(zb, 4))
        zw[f, 10] = jnp.where(top, bz_, za)
        zw[f, 11] = jnp.where(top, bz_, rs(za, 4))
        s_lo, s_hi = strips[2 * f], strips[2 * f + 1]
        if f < 4:
            sb, sa = rl(below(25), 96 - 32 * f), rl(above(25), -32 * f)
        else:
            sb, sa = below(26), above(26)
        sb = jnp.where(bottom, sign * jnp.where(group == 7, rl(s_lo, -16), rl(s_lo, 80)), sb)
        sa = jnp.where(top, spread(surf, 1 + f), sa)
        strip_q.append((s_lo, s_hi, jnp.where(ln < 64, sa, sb)))

    h0, h0z = h[...], z[80]
    h0s, h0sz = spread(surf, 0), spread(surf_z, 0)
    (hx, hz), (hxz, hzz), (hxs, hzs) = slopes(h0, h0z, h0s, h0sz)
    ih, ihz, ihs = 1.0 / h0, 1.0 / h0z, 1.0 / h0s
    base = wn * NL

    parts = []
    for v in range(3):
        x = [strip_q[f][v] for f in range(5)]
        a1, a2, a3, g = fluxes(x, move=(hxs, hzs, w0s))
        d1 = [d_lane(a1[f]) for f in range(5)]
        for f in range(5):
            pt[f, v] = strip_patch(d1[f])
        parts.append((d1, a2, a3, g))
    halo3 = []
    for v in range(2):
        x = [zst[2 * f + v] for f in range(5)]
        z1, z3 = fluxes(x, (1, 3))
        for f in range(5):
            ptz[f, v] = strip_patch(d_lane(z1[f]))
        halo3.append(z3)

    def layer_shift(x, v, k):
        a = rl(x[v], -16 * k)
        c = rl(x[(v + (1 if k > 0 else -1)) % 3], -16 * k)
        return jnp.where(ln < 128 - 16 * k if k > 0 else ln >= -16 * k, a, c)

    strip_s = []
    for v in range(2):
        eta = ((base + 8 * v + group).astype(F32) + 0.5) / LAYERS
        done = []
        for f in range(5):
            dn, dg = (
                (layer_shift(x, v, -2) - layer_shift(x, v, 2)) + 8.0 * (layer_shift(x, v, 1) - layer_shift(x, v, -1))
                for x in ([parts[i][k][f] for i in range(3)] for k in (1, 3))
            )
            da, _ = d_ring(parts[v][2][f], halo3[v][f])
            s = strip_q[f][v] + C * (ihs * (eta * dg - dn) - (parts[v][0][f] + da))
            s = jnp.where(first & ((off == 2) | (off == 3)), jnp.where(off == 3, rl(s, -1), rl(s, -2)), s)
            s = jnp.where(last & ((off == 12) | (off == 13)), jnp.where(off == 12, rl(s, 1), rl(s, 2)), s)
            done.append(s)
        strip_s.append(done)

    def own_flux(k):
        a1, a2, a3, g = fluxes([qw[f, k] for f in range(5)], move=(hx, hz, w0))
        todo = []
        for f in range(5):
            todo += [(r, (f, k), x[f]) for r, x in ((f1w, a1), (f2w, a2), (gw, g))]
            todo += [(f3, (f, k, slice(16, 24)), a3[f])]
        return todo

    def eta_of(l):
        return ((base + l).astype(F32) + 0.5) / LAYERS

    batches(0, 16, 4, own_flux)
    for k in range(12):
        a2, a3, g = fluxes([zw[f, k] for f in range(5)], (2, 3), move=(hxz, hzz, w0z))
        for f in range(5):
            f2zw[f, k], gzw[f, k] = a2[f], g[f]
            if k in (0, 1, 10, 11):
                for ref, at, x in put_halo(f3, f, k + 2, a3[f]):
                    ref[at] = x

    def normal_own(f, k, eta):
        return ih * (eta * d_normal(plane_at(gw, f), k) - d_normal(plane_at(f2w, f), k))

    def ghost_layer(m):
        upper = (m >= 2).astype(jnp.int32)
        k, l, todo = 2 + m + 8 * upper, m - 2 + 16 * upper, []
        for f in range(5):
            dx = patched(d_lane(f1w[f, k]), pltpu.roll(pt[f, 2], patch_shift(l), 1))
            s = qw[f, k] + C * (normal_own(f, k, eta_of(l)) - (dx + d_around(f3, f, k)))
            todo.append((sx, (f, l + 2), s))
        return todo

    def outer(m):
        upper = (m >= 2).astype(jnp.int32)
        k, kz, l, todo = 4 + m + 4 * upper, 2 + m + 4 * upper, m + 12 * upper, []
        eta, half, shift = eta_of(l), l >> 3, patch_shift(l)
        for f in range(5):
            todo.append((sx, (f, l + 2), tx[f, l] + C * normal_own(f, k, eta)))
            dn, dg = d_normal(plane_at(f2zw, f), kz), d_normal(plane_at(gzw, f), kz)
            edge = edges(pltpu.roll(ptz[f, half], shift, 1))
            todo.append((sz, (f, l), tz[f, l] + C * (ihz * (eta * dg - dn) - edge)))
        return todo

    def inner(l):
        half, shift, todo = l >> 3, patch_shift(l), []
        for f in range(5):
            todo.append((sx, (f, l + 2), tx[f, l] + w0 * bx[f, l]))
            edge = edges(pltpu.roll(ptz[f, half], shift, 1))
            todo.append((sz, (f, l), (tz[f, l] + w0z * bz[f, l]) + (hxz * ez[f, l] - C * edge)))
        return todo

    batches(0, 4, 2, ghost_layer)
    batches(0, 4, 2, outer)
    batches(2, 12, 4, inner)
    for f in range(5):
        for k in range(2):
            sx[f, k] = jnp.where(bottom, MIRROR[f] * sx[f, 3 - k], sx[f, k])
            sx[f, 18 + k] = jnp.where(top, b[f], sx[f, 18 + k])

    h1, h1z, h1s = h0 + STEP * w0, h0z + STEP * w0z, h0s + STEP * w0s
    hx1 = SCALE * d_ends(h1, rl(strip_ends(h1s), -12))
    hz1 = SCALE * d_ring(h1, h1z)[0]
    ih1 = 1.0 / h1
    h_out[...] = 0.5 * (h0 + h1 + STEP * w1)
    for v in range(2):
        (a1,) = fluxes(strip_s[v], (1,))
        for f in range(5):
            pt[f, v] = strip_ends(a1[f])

    def own_flux_two(l):
        a1, a2, a3, g = fluxes([sx[f, l + 2] for f in range(5)], move=(hx1, hz1, w1))
        todo = []
        for f in range(5):
            todo += [(r, (f, l + 2), x[f]) for r, x in ((f1x, a1), (f2x, a2), (gx, g))]
            todo += [(f3, (f, l + 2, slice(16, 24)), a3[f])]
        return todo

    def halo_flux_two(l):
        (a3,) = fluxes([sz[f, l] for f in range(5)], (3,))
        return [x for f in range(5) for x in put_halo(f3, f, l + 2, a3[f])]

    def final(l):
        eta, shift, todo = eta_of(l), patch_shift(l), []
        for f in range(5):
            dx = d_ends(f1x[f, l + 2], pltpu.roll(pt[f, l >> 3], shift, 1))
            da = d_around(f3, f, l + 2)
            dn, dg = d_normal(plane_at(f2x, f), l + 2), d_normal(plane_at(gx, f), l + 2)
            rate = ih1 * (eta * dg - dn) - (dx + da)
            todo.append((out, (f, l), 0.5 * (q[f, l] + sx[f, l + 2] + C * rate)))
        return todo

    batches(-2, 20, 4, own_flux_two)
    batches(0, NL, 4, halo_flux_two)
    batches(0, NL, 4, final)


def call(body, ins, outs, scratch=(), sems=0, space=VM):
    shapes = tuple(jax.ShapeDtypeStruct(s, F32) for s in outs)
    return pl.pallas_call(
        body,
        out_shape=shapes,
        in_specs=[space] * len(ins),
        out_specs=tuple([VM] * len(shapes)),
        scratch_shapes=[pltpu.VMEM(s, F32) for s in scratch] + [pltpu.SemaphoreType.DMA((sems,))] * (sems > 0),
        compiler_params=pltpu.CompilerParams(vmem_limit_bytes=40 * 1024 * 1024),
    )(*ins)


def where_am_i():
    return lax.axis_index("sx"), lax.axis_size("sx")


def stage_rows(*refs):
    pack_rows(lax.axis_index("az") % 2 == 1, *refs)


def stage_columns(*refs):
    pack_columns(lax.axis_index("sx") % 2 == 0, *refs)


def stage_second(*refs):
    pack_second(lax.axis_index("az") % 2 == 1, lax.axis_index("wn"), *where_am_i(), *refs)


def stage_far(*refs):
    pack_far(lax.axis_index("wn"), *refs)


def stage_prepare(*refs):
    prepare(lax.axis_index("wn"), *refs)


def stage_advance(*refs):
    advance(lax.axis_index("wn"), *where_am_i(), *refs)


def swaps(size, start, wrap):
    pairs = [(i, (i + 1) % size) for i in range(start, size if wrap else size - 1, 2)]
    return pairs + [(j, i) for i, j in pairs]


def per_device(fields, height, behind):
    around = lax.axis_size("az")
    tiles = lax.axis_size("sx")
    plane = (8, 128)
    *own, one, two = call(
        stage_rows,
        [pltpu.with_memory_space_constraint(x, pltpu.HBM) for x in (fields, height, behind)],
        [fields.shape, height.shape, behind.shape] + [(HALF, *plane)] * 2,
        sems=3,
        space=pl.BlockSpec(memory_space=pltpu.HBM),
    )
    a2 = lax.ppermute(two, "az", swaps(around, 1, True))
    a1 = lax.ppermute(one, "az", swaps(around, 0, True))
    right, left, one, two = call(stage_columns, own, [(3, *plane)] * 4)
    s2 = lax.ppermute(two, "sx", swaps(tiles, 1, False))
    s1 = lax.ppermute(one, "sx", swaps(tiles, 0, False))
    halo, strips, w, near, far, z_right, z_left, one, two = call(
        stage_second,
        (*own, a1, a2, right, left, s1, s2),
        [(NP, *plane), (UNITS, *plane), (4, *plane), (31, *plane), (27, *plane)] + [(3, *plane)] * 4,
        [(27, *plane)] * 2,
    )
    near = lax.ppermute(near, "wn", [(0, 1), (1, 0), (2, 3), (3, 2)])
    s2 = lax.ppermute(two, "sx", swaps(tiles, 1, False))
    s1 = lax.ppermute(one, "sx", swaps(tiles, 0, False))
    (far,) = call(stage_far, (far, w, near), [(31, *plane)])
    parts = call(
        stage_prepare,
        (own[0], own[1], halo, strips, far),
        [(5, NL, *plane)] * 5,
        [(5, NL, *plane)] * 6 + [(5, NL, 40, 128), (5, 2, *plane)],
    )
    far = lax.ppermute(far, "wn", [(1, 2), (2, 1), (3, 0)])
    return call(
        stage_advance,
        (*own, halo, strips, w, near, far, z_right, z_left, s1, s2, *parts),
        [(5, NL, *plane), plane],
        [(5, 16, *plane), (5, 12, *plane)]
        + [(5, 16, *plane)] * 3
        + [(5, 12, *plane)] * 2
        + [(5, 20, *plane)] * 3
        + [(5, 20, 40, 128)]
        + [(5, 20, *plane), (5, NL, *plane), (5, 3, *plane), (5, 2, *plane), (UNITS, *plane)],
    )


def solution(mesh):
    in_specs = (P(None, "wn", "az", "sx"), P("az", "sx"), P(None, "az", "sx"))
    out_specs = (P(None, "wn", "az", "sx"), P("az", "sx"))
    return jax.shard_map(
        per_device, mesh=mesh, in_specs=in_specs, out_specs=out_specs, check_vma=False
    )
```

```python
import functools

import jax
import jax.numpy as jnp
from jax import lax
from jax.experimental import pallas as pl
from jax.experimental.pallas import tpu as pltpu
from jax.sharding import PartitionSpec as P

GAMMA = 1.4
CFL_STEP = 0.08
LAYERS = 64
NL = 16
NP = 86
HALF = 43
UNITS = 11
SCALE = LAYERS / 12.0
STEP = CFL_STEP / LAYERS
C = CFL_STEP / 12.0
VM = pl.BlockSpec(memory_space=pltpu.VMEM)
HBM = pl.BlockSpec(memory_space=pltpu.HBM)
F32 = jnp.float32
MIRROR = (1.0, -1.0, -1.0, -1.0, 1.0)


def lane():
    return lax.broadcasted_iota(jnp.int32, (8, 128), 1)


def row():
    return lax.broadcasted_iota(jnp.int32, (8, 128), 0)


def rl(x, shift):
    return pltpu.roll(x, shift % 128, 1) if shift % 128 else x


def rs(x, shift):
    return pltpu.roll(x, shift % 8, 0) if shift % 8 else x


def d_lane(x):
    return (rl(x, 2) - rl(x, -2)) + 8.0 * (rl(x, -1) - rl(x, 1))


def strip_patch(d):
    off = lane() & 15
    return jnp.where((off == 12) | (off == 13), rl(d, 8), d)


def strip_ends(x):
    off = lane() & 15
    return jnp.where((off == 10) | (off == 11), rl(x, 8), x)


def d_ends(x, e):
    ln = lane()
    p1 = rl(jnp.where(ln < 1, e, x), -1)
    p2 = rl(jnp.where(ln < 2, e, x), -2)
    m1 = rl(jnp.where(ln >= 127, e, x), 1)
    m2 = rl(jnp.where(ln >= 126, e, x), 2)
    return (m2 - p2) + 8.0 * (p1 - m1)


def patched(d, patch):
    ln = lane()
    return jnp.where((ln < 2) | (ln >= 126), patch, d)


def ring(x, z, shift):
    keep = row() >= shift if shift > 0 else row() < 8 + shift
    a, b = rs(x, shift), rs(z, shift)
    return jnp.where(keep, a, b), jnp.where(keep, b, a)


def d_ring(x, z):
    m2, m1, p1, p2 = ring(x, z, 2), ring(x, z, 1), ring(x, z, -1), ring(x, z, -2)
    return tuple((m2[i] - p2[i]) + 8.0 * (p1[i] - m1[i]) for i in (0, 1))


def spread(x, group):
    ln = lane()
    x = rl(x, -16 * group)
    x = jnp.where(ln < 16, x, rl(x, 16))
    x = jnp.where(ln < 32, x, rl(x, 32))
    return jnp.where(ln < 64, x, rl(x, 64))


def pressure(q):
    kinetic = (q[1] * q[1] + q[2] * q[2] + q[3] * q[3]) / q[0]
    return (GAMMA - 1.0) * (q[4] - 0.5 * kinetic)


def speed(q, b):
    behind = pressure(b)
    return (pressure(q) - behind) / jnp.sqrt(GAMMA * behind * b[0])


def fluxes(q, want=(1, 2, 3), move=None):
    inv = 1.0 / q[0]
    v1, v2, v3 = q[1] * inv, q[2] * inv, q[3] * inv
    q11, q22, q33 = q[1] * v1, q[2] * v2, q[3] * v3
    p = (GAMMA - 1.0) * (q[4] - 0.5 * (q11 + q22 + q33))
    e = q[4] + p
    q12, q13, q23 = q[1] * v2, q[1] * v3, q[2] * v3
    out = []
    if 1 in want:
        out.append([q[1], q11 + p, q12, q13, e * v1])
    if 2 in want:
        out.append([q[2], q12, q22 + p, q23, e * v2])
    if 3 in want:
        out.append([q[3], q13, q23, q33 + p, e * v3])
    if move is not None:
        hx, hz, w = move
        s = hx * v1 + hz * v3
        t = s + w
        out.append([q[0] * t, q[1] * t + p * hx, q[2] * t, q[3] * t + p * hz, q[4] * t + p * s])
    return out


def slopes(h, hz, hs, hsz):
    ds, dsz = d_lane(hs), d_lane(hsz)
    x = SCALE * patched(d_lane(h), rl(strip_patch(ds), -12))
    xz = SCALE * patched(d_lane(hz), rl(strip_patch(dsz), -12))
    a, az = d_ring(h, hz)
    s, _ = d_ring(hs, hsz)
    return (x, SCALE * a), (xz, SCALE * az), (SCALE * ds, SCALE * s)


def plane_of(q, h, b):
    def get(i):
        if i < 80:
            return q[i // NL, i % NL]
        return h[...] if i == 80 else b[i - 81]

    return get


def unit_planes(u):
    return [8 * u + j for j in range(8)] if u < 10 else [80 + j for j in range(6)]


def columns(get, right, left):
    ln = lane()
    for v in range(3):
        r_acc = jnp.zeros((8, 128), F32)
        l_acc = jnp.zeros((8, 128), F32)
        for u in range(4 * v, min(4 * v + 4, UNITS)):
            for j, i in enumerate(unit_planes(u)):
                at = 16 * j + 4 * (u - 4 * v)
                x = rl(get(i), at + 4)
                r_acc = jnp.where((ln >= at) & (ln < at + 4), x, r_acc)
                at = (at + 4) % 128
                l_acc = jnp.where((ln >= at) & (ln < at + 4), x, l_acc)
        right[v] = r_acc
        left[v] = rl(l_acc, -4)


def to_pairs(even, right, left, one, two):
    for v in range(3):
        one[v] = jnp.where(even, right[v], left[v])
        two[v] = jnp.where(even, left[v], right[v])


def build_strips(tile, tiles, right, left, one, two, put):
    m = lane() & 3
    quad = (lane() >> 2) & 3
    even = tile % 2 == 0
    for v in range(3):
        lm, rm = left[v], right[v]
        end_l = jnp.where(m == 0, lm, jnp.where(m == 1, rl(lm, 1), jnp.where(m == 2, rl(lm, 2), rl(lm, 3))))
        end_r = jnp.where(m == 3, rm, jnp.where(m == 2, rl(rm, -1), jnp.where(m == 1, rl(rm, -2), rl(rm, -3))))
        lh = jnp.where(tile == 0, end_l, jnp.where(even, two[v], one[v]))
        rh = jnp.where(tile == tiles - 1, end_r, jnp.where(even, one[v], two[v]))
        for t in range(min(4, UNITS - 4 * v)):
            a, b, c, d = (rl(x, 4 * (i - t)) for i, x in enumerate((lh, lm, rm, rh)))
            put(4 * v + t, jnp.where(quad < 2, jnp.where(quad == 0, a, b), jnp.where(quad == 2, c, d)))


def pack_rows(odd, q_hbm, h_hbm, b_hbm, q, h, b, one, two, sems):
    copies = [
        pltpu.make_async_copy(x, y, sems.at[i]) for i, (x, y) in enumerate(((q_hbm, q), (h_hbm, h), (b_hbm, b)))
    ]
    for c in copies:
        c.start()
    for c in copies:
        c.wait()
    get = plane_of(q, h, b)
    mask = (row() >= 4) ^ odd
    for i in range(HALF):
        x, y = get(i), rs(get(i + HALF), 4)
        one[i] = jnp.where(mask, x, y)
        two[i] = jnp.where(mask, y, x)


def pack_columns(even, q, h, b, right, left, one, two):
    columns(plane_of(q, h, b), right, left)
    to_pairs(even, right, left, one, two)


def pack_corners(even, z, right, left, one, two):
    columns(lambda i: z[i], right, left)
    to_pairs(even, right, left, one, two)


def pack_second(odd, wn, tile, tiles, q, h, b, a1, a2, right, left, s1, s2, _parts, *outs):
    z, strips, w, near, far, hi, lo = outs
    ln, rw = lane(), row()
    mask = (rw >= 4) ^ odd
    for i in range(HALF):
        x, y = a2[i], a1[i]
        z[i] = jnp.where(mask, x, y)
        z[i + HALF] = rs(jnp.where(mask, y, x), 4)

    def put(u, x):
        strips[u] = x

    build_strips(tile, tiles, right, left, s1, s2, put)
    surf = strips[10]
    own, bq = [q[f, 15] for f in range(5)], [b[f] for f in range(5)]
    zq, bz = [z[f * NL + 15] for f in range(5)], [z[81 + f] for f in range(5)]
    sq = [strips[2 * f + 1] for f in range(5)]
    w0 = speed(own, bq)
    w0z = speed(zq, bz)
    w0s = spread(speed(sq, [rl(surf, 16 * (6 - f)) for f in range(5)]), 7)
    hx = SCALE * patched(d_lane(h[...]), rl(strip_patch(d_lane(surf)), -12))
    hz = SCALE * d_ring(h[...], z[80])[0]
    (f1s,) = fluxes(sq, (1,))
    (f3z,) = fluxes(zq, (3,))
    levels = []
    for x in ([q[f, 13] for f in range(5)], [q[f, 14] for f in range(5)], own, bq):
        levels.append(fluxes(x, move=(hx, hz, w0)))
    eta = (LAYERS - 0.5) / LAYERS
    ih = 1.0 / h[...]
    top = []
    for f in range(5):
        dx = patched(d_lane(levels[2][0][f]), rl(strip_patch(d_lane(f1s[f])), -124))
        da, _ = d_ring(levels[2][2][f], f3z[f])
        dn, dg = ((levels[0][k][f] - 8.0 * levels[1][k][f]) + 7.0 * levels[3][k][f] for k in (1, 3))
        top.append(own[f] + C * (ih * (eta * dg - dn) - (dx + da)))
    speeds = (w0, w0z, w0s, speed(top, bq))
    for k in range(4):
        w[k] = speeds[k]
        near[27 + k] = speeds[k]
    near_rows = (rw < 2) | (rw >= 6)
    hi_s = hi[26] = strips[9]
    lo_s = lo[26] = strips[8]
    for f in range(5):
        for k in range(4):
            hi[4 * f + k] = q[f, 12 + k]
            lo[4 * f + k] = q[f, k]
        hi[20 + f] = jnp.where(near_rows, z[f * NL + 14], rs(z[f * NL + 15], 4))
        lo[20 + f] = jnp.where(near_rows, z[f * NL], rs(z[f * NL + 1], 4))
        if f < 4:
            inside = (ln >= 32 * f) & (ln < 32 * f + 32)
            hi_s = jnp.where(inside, rl(strips[2 * f + 1], 32 * f + 32), hi_s)
            lo_s = jnp.where(inside, rl(strips[2 * f], 32 * f), lo_s)
    hi[25] = hi_s
    lo[25] = lo_s
    for i in range(27):
        near[i] = jnp.where(wn % 2 == 0, hi[i], lo[i])
        far[i] = jnp.where(wn == 1, hi[i], lo[i])


def pack_far(wn, far, w, near, _corners, out):
    for i in range(27):
        out[i] = far[i]
    for k in range(4):
        out[27 + k] = jnp.where(wn == 2, near[27 + k], w[k])


def d_rows(f3, f, l, at):
    m2, m1, p1, p2 = (f3[f, l, pl.ds(at + k, 8)] for k in (-2, -1, 1, 2))
    return (m2 - p2) + 8.0 * (p1 - m1)


def d_around(f3, f, l):
    return d_rows(f3, f, l, 16)


def d_around_halo(f3, f, l):
    return jnp.where(row() < 4, d_rows(f3, f, l, 24), d_rows(f3, f, l, 8))


def put_halo(f3, f, l, x):
    return [(f3, (f, l, slice(24, 32)), x), (f3, (f, l, slice(8, 16)), x)]


def d_normal(get, l):
    return (get(l - 2) - get(l + 2)) + 8.0 * (get(l + 1) - get(l - 1))


def plane_at(ref, f):
    return lambda l: ref[f, l]


def patch_shift(l):
    return 116 - 16 * (l & 7)


def edges(patch):
    return patched(jnp.zeros_like(patch), patch)


def batches(first_l, count, size, body, after=None):
    def step(i, _):
        todo = []
        for k in range(size):
            todo += body(first_l + i * size + k)
        for ref, at, x in todo:
            ref[at] = x
        if after is not None:
            after(i)
        return 0

    lax.fori_loop(0, count // size, step, 0)


def own_parts(q, _right, f1, f3, d1, dn, dq, f2):
    def flux(l):
        a1, a2, a3 = fluxes([q[f, l] for f in range(5)])
        return [(r, (f, l), x[f]) for f in range(5) for r, x in ((f1, a1), (f2, a2), (f3, a3), (d1, [d_lane(y) for y in a1]))]

    def inner(l):
        return [
            (r, (f, l), d_normal(plane_at(x, f), l)) for f in range(5) for r, x in ((dn, f2), (dq, q))
        ]

    batches(0, NL, 4, flux)
    batches(2, 12, 4, inner)


def prepare(wn, q, h, z, strips, f1x, f3x, d1x, dnx, dqx, _far, tx, bx, tz, bz, ez, gx, f1z, f2z, gz, f3, pt):
    h0, h0z = h[...], z[80]
    hx = SCALE * patched(d_lane(h0), rl(strip_patch(d_lane(spread(strips[10], 0))), -12))
    hz, hzz = (SCALE * x for x in d_ring(h0, h0z))
    ih, ihz = C / h0, C / h0z
    base = wn * NL
    for v in range(2):
        (a1,) = fluxes([strips[2 * f + v] for f in range(5)], (1,))
        for f in range(5):
            pt[f, v] = strip_patch(d_lane(a1[f]))

    def own_moving(l):
        todo = []
        for f in range(5):
            a = f3x[f, l]
            todo += [(gx, (f, l), hx * f1x[f, l] + hz * a), (f3, (f, l, slice(16, 24)), a)]
        return todo

    def halo_flux(l):
        a1, a2, a3 = fluxes([z[f * NL + l] for f in range(5)])
        todo = []
        for f in range(5):
            todo += [(r, (f, l), x) for r, x in ((f1z, a1[f]), (f2z, a2[f]), (gz, hzz * a3[f]))]
            todo += put_halo(f3, f, l, a3[f])
        return todo

    batches(0, NL, 4, own_moving)
    batches(0, NL, 4, halo_flux)

    def own_surface(f, l):
        dx = patched(d1x[f, l], pltpu.roll(pt[f, l >> 3], patch_shift(l), 1))
        return q[f, l] - C * (dx + d_around(f3, f, l))

    def halo_surface(f, l):
        ln = lane()
        dx = jnp.where((ln < 2) | (ln >= 126), 0.0, d_lane(f1z[f, l]))
        return z[f * NL + l] - C * (dx + d_around_halo(f3, f, l))

    def own_inner(l):
        k, todo = ih * (((base + l).astype(F32) + 0.5) / LAYERS), []
        for f in range(5):
            t = own_surface(f, l) + (k * d_normal(plane_at(gx, f), l) - ih * dnx[f, l])
            todo += [(tx, (f, l), t), (bx, (f, l), k * dqx[f, l])]
        return todo

    def halo_inner(l):
        k, todo = ihz * (((base + l).astype(F32) + 0.5) / LAYERS), []
        for f in range(5):
            t = halo_surface(f, l) + (k * d_normal(plane_at(gz, f), l) - ihz * d_normal(plane_at(f2z, f), l))
            todo += [(tz, (f, l), t), (bz, (f, l), k * d_normal(lambda i, f=f: z[f * NL + i], l))]
            todo += [(ez, (f, l), k * d_normal(plane_at(f1z, f), l))]
        return todo

    def outer(l):
        return [(tx, (f, l), own_surface(f, l)) for f in range(5)] + [
            (tz, (f, l), halo_surface(f, l)) for f in range(5)
        ]

    batches(2, 12, 4, own_inner)
    batches(2, 12, 4, halo_inner)
    for l in (0, 14):
        batches(l, 2, 2, outer)


def advance(wn, tile, tiles, q, h, b, z, strips, w, near, far, z_right, z_left, z_one, z_two, tx, bx, tz, bz, ez, *rest):
    out_hbm, h_hbm, qw, zw, f1w, f2w, gw, f2zw, gzw, f1x, f2x, gx, f3, sx, sz, pt, ptz, zst, out, h_out, sems = rest
    first, last = tile == 0, tile == tiles - 1

    def put_strip(u, x):
        zst[u] = x

    build_strips(tile, tiles, z_right, z_left, z_one, z_two, put_strip)
    odd = wn % 2 == 1

    def below(i):
        return jnp.where(odd, near[i], far[i])

    def above(i):
        return jnp.where(odd, far[i], near[i])

    ln, rw = lane(), row()
    group, off = ln >> 4, ln & 15
    bottom, top = wn == 0, wn == 3
    near_rows = (rw < 2) | (rw >= 6)

    speeds = [jnp.where(top, w[k], jnp.where(wn == 2, near[27 + k], far[27 + k])) for k in range(4)]
    w0, w0z, w0s, w1 = speeds

    surf, surf_z = strips[10], zst[10]
    strip_q = []
    for f in range(5):
        sign = MIRROR[f]
        bq, bz_ = b[f], z[81 + f]
        for k in range(4):
            qw[f, k] = jnp.where(bottom, sign * q[f, 3 - k], below(4 * f + k))
            qw[f, 4 + k] = q[f, k]
            qw[f, 8 + k] = q[f, 12 + k]
            qw[f, 12 + k] = jnp.where(top, bq, above(4 * f + k))
            zw[f, 2 + k] = z[f * NL + k]
            zw[f, 6 + k] = z[f * NL + 12 + k]
        zb, za = below(20 + f), above(20 + f)
        zw[f, 0] = jnp.where(bottom, sign * z[f * NL + 1], zb)
        zw[f, 1] = jnp.where(bottom, sign * z[f * NL], rs(zb, 4))
        zw[f, 10] = jnp.where(top, bz_, za)
        zw[f, 11] = jnp.where(top, bz_, rs(za, 4))
        s_lo, s_hi = strips[2 * f], strips[2 * f + 1]
        if f < 4:
            sb, sa = rl(below(25), 96 - 32 * f), rl(above(25), -32 * f)
        else:
            sb, sa = below(26), above(26)
        sb = jnp.where(bottom, sign * jnp.where(group == 7, rl(s_lo, -16), rl(s_lo, 80)), sb)
        sa = jnp.where(top, spread(surf, 1 + f), sa)
        strip_q.append((s_lo, s_hi, jnp.where(ln < 64, sa, sb)))

    h0, h0z = h[...], z[80]
    h0s, h0sz = spread(surf, 0), spread(surf_z, 0)
    (hx, hz), (hxz, hzz), (hxs, hzs) = slopes(h0, h0z, h0s, h0sz)
    ih, ihz, ihs = 1.0 / h0, 1.0 / h0z, 1.0 / h0s
    base = wn * NL

    parts = []
    for v in range(3):
        x = [strip_q[f][v] for f in range(5)]
        a1, a2, a3, g = fluxes(x, move=(hxs, hzs, w0s))
        d1 = [d_lane(a1[f]) for f in range(5)]
        for f in range(5):
            pt[f, v] = strip_patch(d1[f])
        parts.append((d1, a2, a3, g))
    halo3 = []
    for v in range(2):
        x = [zst[2 * f + v] for f in range(5)]
        z1, z3 = fluxes(x, (1, 3))
        for f in range(5):
            ptz[f, v] = strip_patch(d_lane(z1[f]))
        halo3.append(z3)

    def layer_shift(x, v, k):
        a = rl(x[v], -16 * k)
        c = rl(x[(v + (1 if k > 0 else -1)) % 3], -16 * k)
        return jnp.where(ln < 128 - 16 * k if k > 0 else ln >= -16 * k, a, c)

    strip_s = []
    for v in range(2):
        eta = ((base + 8 * v + group).astype(F32) + 0.5) / LAYERS
        done = []
        for f in range(5):
            dn, dg = (
                (layer_shift(x, v, -2) - layer_shift(x, v, 2)) + 8.0 * (layer_shift(x, v, 1) - layer_shift(x, v, -1))
                for x in ([parts[i][k][f] for i in range(3)] for k in (1, 3))
            )
            da, _ = d_ring(parts[v][2][f], halo3[v][f])
            s = strip_q[f][v] + C * (ihs * (eta * dg - dn) - (parts[v][0][f] + da))
            s = jnp.where(first & ((off == 2) | (off == 3)), jnp.where(off == 3, rl(s, -1), rl(s, -2)), s)
            s = jnp.where(last & ((off == 12) | (off == 13)), jnp.where(off == 12, rl(s, 1), rl(s, 2)), s)
            done.append(s)
        strip_s.append(done)

    def own_flux(k):
        a1, a2, a3, g = fluxes([qw[f, k] for f in range(5)], move=(hx, hz, w0))
        todo = []
        for f in range(5):
            todo += [(r, (f, k), x[f]) for r, x in ((f1w, a1), (f2w, a2), (gw, g))]
            todo += [(f3, (f, k, slice(16, 24)), a3[f])]
        return todo

    def eta_of(l):
        return ((base + l).astype(F32) + 0.5) / LAYERS

    batches(0, 16, 4, own_flux)

    def halo_flux(k):
        a2, a3, g = fluxes([zw[f, k] for f in range(5)], (2, 3), move=(hxz, hzz, w0z))
        todo = []
        for f in range(5):
            todo += [(r, (f, k), x[f]) for r, x in ((f2zw, a2), (gzw, g))] + put_halo(f3, f, k + 2, a3[f])
        return todo

    batches(0, 12, 4, halo_flux)

    def normal_own(f, k, eta):
        return ih * (eta * d_normal(plane_at(gw, f), k) - d_normal(plane_at(f2w, f), k))

    def ghost_layer(m):
        upper = (m >= 2).astype(jnp.int32)
        k, l, todo = 2 + m + 8 * upper, m - 2 + 16 * upper, []
        for f in range(5):
            dx = patched(d_lane(f1w[f, k]), pltpu.roll(pt[f, 2], patch_shift(l), 1))
            s = qw[f, k] + C * (normal_own(f, k, eta_of(l)) - (dx + d_around(f3, f, k)))
            todo.append((sx, (f, l + 2), s))
        return todo

    def outer(m):
        upper = (m >= 2).astype(jnp.int32)
        k, kz, l, todo = 4 + m + 4 * upper, 2 + m + 4 * upper, m + 12 * upper, []
        eta, half, shift = eta_of(l), l >> 3, patch_shift(l)
        for f in range(5):
            todo.append((sx, (f, l + 2), tx[f, l] + C * normal_own(f, k, eta)))
            dn, dg = d_normal(plane_at(f2zw, f), kz), d_normal(plane_at(gzw, f), kz)
            edge = edges(pltpu.roll(ptz[f, half], shift, 1))
            todo.append((sz, (f, l), tz[f, l] + C * (ihz * (eta * dg - dn) - edge)))
        return todo

    def inner(l):
        half, shift, todo = l >> 3, patch_shift(l), []
        for f in range(5):
            todo.append((sx, (f, l + 2), tx[f, l] + w0 * bx[f, l]))
            edge = edges(pltpu.roll(ptz[f, half], shift, 1))
            todo.append((sz, (f, l), (tz[f, l] + w0z * bz[f, l]) + (hxz * ez[f, l] - C * edge)))
        return todo

    batches(0, 4, 2, ghost_layer)
    batches(0, 4, 2, outer)
    batches(2, 12, 4, inner)
    for f in range(5):
        for k in range(2):
            sx[f, k] = jnp.where(bottom, MIRROR[f] * sx[f, 3 - k], sx[f, k])
            sx[f, 18 + k] = jnp.where(top, b[f], sx[f, 18 + k])

    h1, h1z, h1s = h0 + STEP * w0, h0z + STEP * w0z, h0s + STEP * w0s
    hx1 = SCALE * d_ends(h1, rl(strip_ends(h1s), -12))
    hz1 = SCALE * d_ring(h1, h1z)[0]
    ih1 = 1.0 / h1
    h_out[...] = 0.5 * (h0 + h1 + STEP * w1)
    h_copy = pltpu.make_async_copy(h_out, h_hbm, sems.at[4])
    h_copy.start()
    for v in range(2):
        (a1,) = fluxes(strip_s[v], (1,))
        for f in range(5):
            pt[f, v] = strip_ends(a1[f])

    def own_flux_two(l):
        a1, a2, a3, g = fluxes([sx[f, l + 2] for f in range(5)], move=(hx1, hz1, w1))
        todo = []
        for f in range(5):
            todo += [(r, (f, l + 2), x[f]) for r, x in ((f1x, a1), (f2x, a2), (gx, g))]
            todo += [(f3, (f, l + 2, slice(16, 24)), a3[f])]
        return todo

    def halo_flux_two(l):
        (a3,) = fluxes([sz[f, l] for f in range(5)], (3,))
        return [x for f in range(5) for x in put_halo(f3, f, l + 2, a3[f])]

    def final(l):
        eta, shift, todo = eta_of(l), patch_shift(l), []
        for f in range(5):
            dx = d_ends(f1x[f, l + 2], pltpu.roll(pt[f, l >> 3], shift, 1))
            da = d_around(f3, f, l + 2)
            dn, dg = d_normal(plane_at(f2x, f), l + 2), d_normal(plane_at(gx, f), l + 2)
            rate = ih1 * (eta * dg - dn) - (dx + da)
            todo.append((out, (f, l), 0.5 * (q[f, l] + sx[f, l + 2] + C * rate)))
        return todo

    batches(-2, 20, 4, own_flux_two)
    batches(0, NL, 4, halo_flux_two)

    def out_copy(i):
        part = (slice(None), pl.ds(4 * i, 4))
        return pltpu.make_async_copy(out.at[part], out_hbm.at[part], sems.at[i])

    batches(0, NL, 4, final, lambda i: out_copy(i).start())
    for i in range(4):
        out_copy(i).wait()
    h_copy.wait()


def call(body, ins, outs, scratch=(), sems=0, space=VM, out_space=VM):
    shapes = tuple(jax.ShapeDtypeStruct(s, F32) for s in outs)
    return pl.pallas_call(
        body,
        out_shape=shapes,
        in_specs=[space] * len(ins),
        out_specs=tuple([out_space] * len(shapes)),
        scratch_shapes=[pltpu.VMEM(s, F32) for s in scratch] + [pltpu.SemaphoreType.DMA((sems,))] * (sems > 0),
        compiler_params=pltpu.CompilerParams(vmem_limit_bytes=40 * 1024 * 1024),
    )(*ins)


def where_am_i():
    return lax.axis_index("sx"), lax.axis_size("sx")


def stage_rows(*refs):
    pack_rows(lax.axis_index("az") % 2 == 1, *refs)


def stage_own(*refs):
    own_parts(*refs)


def stage_columns(*refs):
    pack_columns(lax.axis_index("sx") % 2 == 0, *refs)


def stage_corners(*refs):
    pack_corners(lax.axis_index("sx") % 2 == 0, *refs)


def stage_second(*refs):
    pack_second(lax.axis_index("az") % 2 == 1, lax.axis_index("wn"), *where_am_i(), *refs)


def stage_far(*refs):
    pack_far(lax.axis_index("wn"), *refs)


def stage_prepare(*refs):
    prepare(lax.axis_index("wn"), *refs)


def stage_advance(*refs):
    advance(lax.axis_index("wn"), *where_am_i(), *refs)


def swaps(size, start, wrap):
    pairs = [(i, (i + 1) % size) for i in range(start, size if wrap else size - 1, 2)]
    return pairs + [(j, i) for i, j in pairs]


def per_device(fields, height, behind):
    around = lax.axis_size("az")
    tiles = lax.axis_size("sx")
    plane = (8, 128)
    *own, one, two = call(
        stage_rows,
        [pltpu.with_memory_space_constraint(x, pltpu.HBM) for x in (fields, height, behind)],
        [fields.shape, height.shape, behind.shape] + [(HALF, *plane)] * 2,
        sems=3,
        space=HBM,
    )
    a2 = lax.ppermute(two, "az", swaps(around, 1, True))
    a1 = lax.ppermute(one, "az", swaps(around, 0, True))
    right, left, one, two = call(stage_columns, own, [(3, *plane)] * 4)
    s2 = lax.ppermute(two, "sx", swaps(tiles, 1, False))
    s1 = lax.ppermute(one, "sx", swaps(tiles, 0, False))
    parts = call(stage_own, (own[0], right), [(5, NL, *plane)] * 5, [(5, NL, *plane)])
    halo, strips, w, near, far = call(
        stage_second,
        (*own, a1, a2, right, left, s1, s2, parts[3]),
        [(NP, *plane), (UNITS, *plane), (4, *plane), (31, *plane), (27, *plane)],
        [(27, *plane)] * 2,
    )
    z_right, z_left, one, two = call(stage_corners, (halo,), [(3, *plane)] * 4)
    near = lax.ppermute(near, "wn", [(0, 1), (1, 0), (2, 3), (3, 2)])
    s2 = lax.ppermute(two, "sx", swaps(tiles, 1, False))
    s1 = lax.ppermute(one, "sx", swaps(tiles, 0, False))
    (far,) = call(stage_far, (far, w, near, two), [(31, *plane)])
    parts = call(
        stage_prepare,
        (own[0], own[1], halo, strips, *parts, far),
        [(5, NL, *plane)] * 5,
        [(5, NL, *plane)] * 4 + [(5, NL, 40, 128), (5, 2, *plane)],
    )
    far = lax.ppermute(far, "wn", [(1, 2), (2, 1), (3, 0)])
    return call(
        stage_advance,
        (*own, halo, strips, w, near, far, z_right, z_left, s1, s2, *parts),
        [(5, NL, *plane), plane],
        [(5, 16, *plane), (5, 12, *plane)]
        + [(5, 16, *plane)] * 3
        + [(5, 12, *plane)] * 2
        + [(5, 20, *plane)] * 3
        + [(5, 20, 40, 128)]
        + [(5, 20, *plane), (5, NL, *plane), (5, 3, *plane), (5, 2, *plane), (UNITS, *plane), (5, NL, *plane), plane],
        sems=5,
        out_space=HBM,
    )


def solution(mesh):
    in_specs = (P(None, "wn", "az", "sx"), P("az", "sx"), P(None, "az", "sx"))
    out_specs = (P(None, "wn", "az", "sx"), P("az", "sx"))
    return jax.shard_map(
        per_device, mesh=mesh, in_specs=in_specs, out_specs=out_specs, check_vma=False
    )
```

```python
import functools

import jax
import jax.numpy as jnp
from jax import lax
from jax.experimental import pallas as pl
from jax.experimental.pallas import tpu as pltpu
from jax.sharding import PartitionSpec as P

GAMMA = 1.4
CFL_STEP = 0.08
LAYERS = 64
NL = 16
NP = 86
HALF = 43
UNITS = 11
SCALE = LAYERS / 12.0
STEP = CFL_STEP / LAYERS
C = CFL_STEP / 12.0
VM = pl.BlockSpec(memory_space=pltpu.VMEM)
HBM = pl.BlockSpec(memory_space=pltpu.HBM)
F32 = jnp.float32
MIRROR = (1.0, -1.0, -1.0, -1.0, 1.0)


def lane():
    return lax.broadcasted_iota(jnp.int32, (8, 128), 1)


def row():
    return lax.broadcasted_iota(jnp.int32, (8, 128), 0)


def rl(x, shift):
    return pltpu.roll(x, shift % 128, 1) if shift % 128 else x


def rs(x, shift):
    return pltpu.roll(x, shift % 8, 0) if shift % 8 else x


def d_lane(x):
    return (rl(x, 2) - rl(x, -2)) + 8.0 * (rl(x, -1) - rl(x, 1))


def strip_patch(d):
    off = lane() & 15
    return jnp.where((off == 12) | (off == 13), rl(d, 8), d)


def strip_ends(x):
    off = lane() & 15
    return jnp.where((off == 10) | (off == 11), rl(x, 8), x)


def d_ends(x, e):
    ln = lane()
    p1 = rl(jnp.where(ln < 1, e, x), -1)
    p2 = rl(jnp.where(ln < 2, e, x), -2)
    m1 = rl(jnp.where(ln >= 127, e, x), 1)
    m2 = rl(jnp.where(ln >= 126, e, x), 2)
    return (m2 - p2) + 8.0 * (p1 - m1)


def patched(d, patch):
    ln = lane()
    return jnp.where((ln < 2) | (ln >= 126), patch, d)


def ring(x, z, shift):
    keep = row() >= shift if shift > 0 else row() < 8 + shift
    a, b = rs(x, shift), rs(z, shift)
    return jnp.where(keep, a, b), jnp.where(keep, b, a)


def d_ring(x, z):
    m2, m1, p1, p2 = ring(x, z, 2), ring(x, z, 1), ring(x, z, -1), ring(x, z, -2)
    return tuple((m2[i] - p2[i]) + 8.0 * (p1[i] - m1[i]) for i in (0, 1))


def spread(x, group):
    ln = lane()
    x = rl(x, -16 * group)
    x = jnp.where(ln < 16, x, rl(x, 16))
    x = jnp.where(ln < 32, x, rl(x, 32))
    return jnp.where(ln < 64, x, rl(x, 64))


def pressure(q):
    kinetic = (q[1] * q[1] + q[2] * q[2] + q[3] * q[3]) / q[0]
    return (GAMMA - 1.0) * (q[4] - 0.5 * kinetic)


def speed(q, b):
    behind = pressure(b)
    return (pressure(q) - behind) / jnp.sqrt(GAMMA * behind * b[0])


def fluxes(q, want=(1, 2, 3), move=None):
    inv = 1.0 / q[0]
    v1, v2, v3 = q[1] * inv, q[2] * inv, q[3] * inv
    q11, q22, q33 = q[1] * v1, q[2] * v2, q[3] * v3
    p = (GAMMA - 1.0) * (q[4] - 0.5 * (q11 + q22 + q33))
    e = q[4] + p
    q12, q13, q23 = q[1] * v2, q[1] * v3, q[2] * v3
    out = []
    if 1 in want:
        out.append([q[1], q11 + p, q12, q13, e * v1])
    if 2 in want:
        out.append([q[2], q12, q22 + p, q23, e * v2])
    if 3 in want:
        out.append([q[3], q13, q23, q33 + p, e * v3])
    if move is not None:
        hx, hz, w = move
        s = hx * v1 + hz * v3
        t = s + w
        out.append([q[0] * t, q[1] * t + p * hx, q[2] * t, q[3] * t + p * hz, q[4] * t + p * s])
    return out


def slopes(h, hz, hs, hsz):
    ds, dsz = d_lane(hs), d_lane(hsz)
    x = SCALE * patched(d_lane(h), rl(strip_patch(ds), -12))
    xz = SCALE * patched(d_lane(hz), rl(strip_patch(dsz), -12))
    a, az = d_ring(h, hz)
    s, _ = d_ring(hs, hsz)
    return (x, SCALE * a), (xz, SCALE * az), (SCALE * ds, SCALE * s)


def plane_of(q, h, b):
    def get(i):
        if i < 80:
            return q[i // NL, i % NL]
        return h[...] if i == 80 else b[i - 81]

    return get


def unit_planes(u):
    return [8 * u + j for j in range(8)] if u < 10 else [80 + j for j in range(6)]


def columns(get, right, left):
    ln = lane()
    for v in range(3):
        r_acc = jnp.zeros((8, 128), F32)
        l_acc = jnp.zeros((8, 128), F32)
        for u in range(4 * v, min(4 * v + 4, UNITS)):
            for j, i in enumerate(unit_planes(u)):
                at = 16 * j + 4 * (u - 4 * v)
                x = rl(get(i), at + 4)
                r_acc = jnp.where((ln >= at) & (ln < at + 4), x, r_acc)
                at = (at + 4) % 128
                l_acc = jnp.where((ln >= at) & (ln < at + 4), x, l_acc)
        right[v] = r_acc
        left[v] = rl(l_acc, -4)


def to_pairs(even, right, left, one, two):
    for v in range(3):
        one[v] = jnp.where(even, right[v], left[v])
        two[v] = jnp.where(even, left[v], right[v])


def build_strips(tile, tiles, right, left, one, two, put):
    m = lane() & 3
    quad = (lane() >> 2) & 3
    even = tile % 2 == 0
    for v in range(3):
        lm, rm = left[v], right[v]
        end_l = jnp.where(m == 0, lm, jnp.where(m == 1, rl(lm, 1), jnp.where(m == 2, rl(lm, 2), rl(lm, 3))))
        end_r = jnp.where(m == 3, rm, jnp.where(m == 2, rl(rm, -1), jnp.where(m == 1, rl(rm, -2), rl(rm, -3))))
        lh = jnp.where(tile == 0, end_l, jnp.where(even, two[v], one[v]))
        rh = jnp.where(tile == tiles - 1, end_r, jnp.where(even, one[v], two[v]))
        for t in range(min(4, UNITS - 4 * v)):
            a, b, c, d = (rl(x, 4 * (i - t)) for i, x in enumerate((lh, lm, rm, rh)))
            put(4 * v + t, jnp.where(quad < 2, jnp.where(quad == 0, a, b), jnp.where(quad == 2, c, d)))


def pack_rows(odd, q_hbm, h_hbm, b_hbm, q, h, b, one, two, sems):
    copies = [
        pltpu.make_async_copy(x, y, sems.at[i]) for i, (x, y) in enumerate(((q_hbm, q), (h_hbm, h), (b_hbm, b)))
    ]
    for c in copies:
        c.start()
    for c in copies:
        c.wait()
    get = plane_of(q, h, b)
    mask = (row() >= 4) ^ odd
    for i in range(HALF):
        x, y = get(i), rs(get(i + HALF), 4)
        one[i] = jnp.where(mask, x, y)
        two[i] = jnp.where(mask, y, x)


def pack_columns(even, q, h, b, right, left, one, two):
    columns(plane_of(q, h, b), right, left)
    to_pairs(even, right, left, one, two)


def pack_corners(even, z, right, left, one, two):
    columns(lambda i: z[i], right, left)
    to_pairs(even, right, left, one, two)


def pack_second(odd, wn, tile, tiles, q, h, b, a1, a2, right, left, s1, s2, _parts, *outs):
    z, strips, w, near, far, hi, lo = outs
    ln, rw = lane(), row()
    mask = (rw >= 4) ^ odd
    for i in range(HALF):
        x, y = a2[i], a1[i]
        z[i] = jnp.where(mask, x, y)
        z[i + HALF] = rs(jnp.where(mask, y, x), 4)

    def put(u, x):
        strips[u] = x

    build_strips(tile, tiles, right, left, s1, s2, put)
    surf = strips[10]
    own, bq = [q[f, 15] for f in range(5)], [b[f] for f in range(5)]
    zq, bz = [z[f * NL + 15] for f in range(5)], [z[81 + f] for f in range(5)]
    sq = [strips[2 * f + 1] for f in range(5)]
    w0 = speed(own, bq)
    w0z = speed(zq, bz)
    w0s = spread(speed(sq, [rl(surf, 16 * (6 - f)) for f in range(5)]), 7)
    hx = SCALE * patched(d_lane(h[...]), rl(strip_patch(d_lane(surf)), -12))
    hz = SCALE * d_ring(h[...], z[80])[0]
    (f1s,) = fluxes(sq, (1,))
    (f3z,) = fluxes(zq, (3,))
    levels = []
    for x in ([q[f, 13] for f in range(5)], [q[f, 14] for f in range(5)], own, bq):
        levels.append(fluxes(x, move=(hx, hz, w0)))
    eta = (LAYERS - 0.5) / LAYERS
    ih = 1.0 / h[...]
    top = []
    for f in range(5):
        dx = patched(d_lane(levels[2][0][f]), rl(strip_patch(d_lane(f1s[f])), -124))
        da, _ = d_ring(levels[2][2][f], f3z[f])
        dn, dg = ((levels[0][k][f] - 8.0 * levels[1][k][f]) + 7.0 * levels[3][k][f] for k in (1, 3))
        top.append(own[f] + C * (ih * (eta * dg - dn) - (dx + da)))
    speeds = (w0, w0z, w0s, speed(top, bq))
    for k in range(4):
        w[k] = speeds[k]
        near[27 + k] = speeds[k]
    near_rows = (rw < 2) | (rw >= 6)
    hi_s = hi[26] = strips[9]
    lo_s = lo[26] = strips[8]
    for f in range(5):
        for k in range(4):
            hi[4 * f + k] = q[f, 12 + k]
            lo[4 * f + k] = q[f, k]
        hi[20 + f] = jnp.where(near_rows, z[f * NL + 14], rs(z[f * NL + 15], 4))
        lo[20 + f] = jnp.where(near_rows, z[f * NL], rs(z[f * NL + 1], 4))
        if f < 4:
            inside = (ln >= 32 * f) & (ln < 32 * f + 32)
            hi_s = jnp.where(inside, rl(strips[2 * f + 1], 32 * f + 32), hi_s)
            lo_s = jnp.where(inside, rl(strips[2 * f], 32 * f), lo_s)
    hi[25] = hi_s
    lo[25] = lo_s
    for i in range(27):
        near[i] = jnp.where(wn % 2 == 0, hi[i], lo[i])
        far[i] = jnp.where(wn == 1, hi[i], lo[i])


def pack_far(wn, far, w, near, _corners, out):
    for i in range(27):
        out[i] = far[i]
    for k in range(4):
        out[27 + k] = jnp.where(wn == 2, near[27 + k], w[k])


def rows(at):
    return pl.ds(2 * at, 8, 2)


def d_rows(f3, f, l, at):
    m2, m1, p1, p2 = (f3[f, l, rows(at + k)] for k in (-2, -1, 1, 2))
    return (m2 - p2) + 8.0 * (p1 - m1)


def d_around(f3, f, l):
    return d_rows(f3, f, l, 16)


def d_around_halo(f3, f, l):
    return jnp.where(row() < 4, d_rows(f3, f, l, 24), d_rows(f3, f, l, 8))


def put_halo(f3, f, l, x):
    return [(f3, (f, l, rows(24)), x), (f3, (f, l, rows(8)), x)]


def d_normal(get, l):
    return (get(l - 2) - get(l + 2)) + 8.0 * (get(l + 1) - get(l - 1))


def plane_at(ref, f):
    return lambda l: ref[f, l]


def patch_shift(l):
    return 116 - 16 * (l & 7)


def edges(patch):
    return patched(jnp.zeros_like(patch), patch)


def batches(first_l, count, size, body, after=None):
    def step(i, _):
        todo = []
        for k in range(size):
            todo += body(first_l + i * size + k)
        for ref, at, x in todo:
            ref[at] = x
        if after is not None:
            after(i)
        return 0

    lax.fori_loop(0, count // size, step, 0)


def own_parts(q, _right, f1, f3, d1, dn, dq, f2):
    def flux(l):
        a1, a2, a3 = fluxes([q[f, l] for f in range(5)])
        return [(r, (f, l), x[f]) for f in range(5) for r, x in ((f1, a1), (f2, a2), (f3, a3), (d1, [d_lane(y) for y in a1]))]

    def inner(l):
        return [
            (r, (f, l), d_normal(plane_at(x, f), l)) for f in range(5) for r, x in ((dn, f2), (dq, q))
        ]

    batches(0, NL, 4, flux)
    batches(2, 12, 4, inner)


def prepare(wn, q, h, z, strips, f1x, f3x, d1x, dnx, dqx, _far, tx, bx, tz, bz, ez, gx, f1z, f2z, gz, f3, pt):
    h0, h0z = h[...], z[80]
    hx = SCALE * patched(d_lane(h0), rl(strip_patch(d_lane(spread(strips[10], 0))), -12))
    hz, hzz = (SCALE * x for x in d_ring(h0, h0z))
    ih, ihz = C / h0, C / h0z
    base = wn * NL
    for v in range(2):
        (a1,) = fluxes([strips[2 * f + v] for f in range(5)], (1,))
        for f in range(5):
            pt[f, v] = strip_patch(d_lane(a1[f]))

    def own_moving(l):
        todo = []
        for f in range(5):
            a = f3x[f, l]
            todo += [(gx, (f, l), hx * f1x[f, l] + hz * a), (f3, (f, l, rows(16)), a)]
        return todo

    def halo_flux(l):
        a1, a2, a3 = fluxes([z[f * NL + l] for f in range(5)])
        todo = []
        for f in range(5):
            todo += [(r, (f, l), x) for r, x in ((f1z, a1[f]), (f2z, a2[f]), (gz, hzz * a3[f]))]
            todo += put_halo(f3, f, l, a3[f])
        return todo

    batches(0, NL, 4, own_moving)
    batches(0, NL, 4, halo_flux)

    def own_surface(f, l):
        dx = patched(d1x[f, l], pltpu.roll(pt[f, l >> 3], patch_shift(l), 1))
        return q[f, l] - C * (dx + d_around(f3, f, l))

    def halo_surface(f, l):
        ln = lane()
        dx = jnp.where((ln < 2) | (ln >= 126), 0.0, d_lane(f1z[f, l]))
        return z[f * NL + l] - C * (dx + d_around_halo(f3, f, l))

    def own_inner(l):
        k, todo = ih * (((base + l).astype(F32) + 0.5) / LAYERS), []
        for f in range(5):
            t = own_surface(f, l) + (k * d_normal(plane_at(gx, f), l) - ih * dnx[f, l])
            todo += [(tx, (f, l), t), (bx, (f, l), k * dqx[f, l])]
        return todo

    def halo_inner(l):
        k, todo = ihz * (((base + l).astype(F32) + 0.5) / LAYERS), []
        for f in range(5):
            t = halo_surface(f, l) + (k * d_normal(plane_at(gz, f), l) - ihz * d_normal(plane_at(f2z, f), l))
            todo += [(tz, (f, l), t), (bz, (f, l), k * d_normal(lambda i, f=f: z[f * NL + i], l))]
            todo += [(ez, (f, l), k * d_normal(plane_at(f1z, f), l))]
        return todo

    def outer(l):
        return [(tx, (f, l), own_surface(f, l)) for f in range(5)] + [
            (tz, (f, l), halo_surface(f, l)) for f in range(5)
        ]

    batches(2, 12, 4, own_inner)
    batches(2, 12, 4, halo_inner)
    for l in (0, 14):
        batches(l, 2, 2, outer)


def advance(wn, tile, tiles, q, h, b, z, strips, w, near, far, z_right, z_left, z_one, z_two, tx, bx, tz, bz, ez, *rest):
    out_hbm, h_hbm, qw, zw, f1w, f2w, gw, f2zw, gzw, f1x, f2x, gx, f3, sx, sz, pt, ptz, zst, out, h_out, sems = rest
    first, last = tile == 0, tile == tiles - 1

    def put_strip(u, x):
        zst[u] = x

    build_strips(tile, tiles, z_right, z_left, z_one, z_two, put_strip)
    odd = wn % 2 == 1

    def below(i):
        return jnp.where(odd, near[i], far[i])

    def above(i):
        return jnp.where(odd, far[i], near[i])

    ln, rw = lane(), row()
    group, off = ln >> 4, ln & 15
    bottom, top = wn == 0, wn == 3
    near_rows = (rw < 2) | (rw >= 6)

    speeds = [jnp.where(top, w[k], jnp.where(wn == 2, near[27 + k], far[27 + k])) for k in range(4)]
    w0, w0z, w0s, w1 = speeds

    surf, surf_z = strips[10], zst[10]
    strip_q = []
    for f in range(5):
        sign = MIRROR[f]
        bq, bz_ = b[f], z[81 + f]
        for k in range(4):
            qw[f, k] = jnp.where(bottom, sign * q[f, 3 - k], below(4 * f + k))
            qw[f, 4 + k] = q[f, k]
            qw[f, 8 + k] = q[f, 12 + k]
            qw[f, 12 + k] = jnp.where(top, bq, above(4 * f + k))
            zw[f, 2 + k] = z[f * NL + k]
            zw[f, 6 + k] = z[f * NL + 12 + k]
        zb, za = below(20 + f), above(20 + f)
        zw[f, 0] = jnp.where(bottom, sign * z[f * NL + 1], zb)
        zw[f, 1] = jnp.where(bottom, sign * z[f * NL], rs(zb, 4))
        zw[f, 10] = jnp.where(top, bz_, za)
        zw[f, 11] = jnp.where(top, bz_, rs(za, 4))
        s_lo, s_hi = strips[2 * f], strips[2 * f + 1]
        if f < 4:
            sb, sa = rl(below(25), 96 - 32 * f), rl(above(25), -32 * f)
        else:
            sb, sa = below(26), above(26)
        sb = jnp.where(bottom, sign * jnp.where(group == 7, rl(s_lo, -16), rl(s_lo, 80)), sb)
        sa = jnp.where(top, spread(surf, 1 + f), sa)
        strip_q.append((s_lo, s_hi, jnp.where(ln < 64, sa, sb)))

    h0, h0z = h[...], z[80]
    h0s, h0sz = spread(surf, 0), spread(surf_z, 0)
    (hx, hz), (hxz, hzz), (hxs, hzs) = slopes(h0, h0z, h0s, h0sz)
    ih, ihz, ihs = 1.0 / h0, 1.0 / h0z, 1.0 / h0s
    base = wn * NL

    parts = []
    for v in range(3):
        x = [strip_q[f][v] for f in range(5)]
        a1, a2, a3, g = fluxes(x, move=(hxs, hzs, w0s))
        d1 = [d_lane(a1[f]) for f in range(5)]
        for f in range(5):
            pt[f, v] = strip_patch(d1[f])
        parts.append((d1, a2, a3, g))
    halo3 = []
    for v in range(2):
        x = [zst[2 * f + v] for f in range(5)]
        z1, z3 = fluxes(x, (1, 3))
        for f in range(5):
            ptz[f, v] = strip_patch(d_lane(z1[f]))
        halo3.append(z3)

    def layer_shift(x, v, k):
        a = rl(x[v], -16 * k)
        c = rl(x[(v + (1 if k > 0 else -1)) % 3], -16 * k)
        return jnp.where(ln < 128 - 16 * k if k > 0 else ln >= -16 * k, a, c)

    strip_s = []
    for v in range(2):
        eta = ((base + 8 * v + group).astype(F32) + 0.5) / LAYERS
        done = []
        for f in range(5):
            dn, dg = (
                (layer_shift(x, v, -2) - layer_shift(x, v, 2)) + 8.0 * (layer_shift(x, v, 1) - layer_shift(x, v, -1))
                for x in ([parts[i][k][f] for i in range(3)] for k in (1, 3))
            )
            da, _ = d_ring(parts[v][2][f], halo3[v][f])
            s = strip_q[f][v] + C * (ihs * (eta * dg - dn) - (parts[v][0][f] + da))
            s = jnp.where(first & ((off == 2) | (off == 3)), jnp.where(off == 3, rl(s, -1), rl(s, -2)), s)
            s = jnp.where(last & ((off == 12) | (off == 13)), jnp.where(off == 12, rl(s, 1), rl(s, 2)), s)
            done.append(s)
        strip_s.append(done)

    def own_flux(k):
        a1, a2, a3, g = fluxes([qw[f, k] for f in range(5)], move=(hx, hz, w0))
        todo = []
        for f in range(5):
            todo += [(r, (f, k), x[f]) for r, x in ((f1w, a1), (f2w, a2), (gw, g))]
            todo += [(f3, (f, k, rows(16)), a3[f])]
        return todo

    def eta_of(l):
        return ((base + l).astype(F32) + 0.5) / LAYERS

    batches(0, 16, 4, own_flux)

    def halo_flux(k):
        a2, a3, g = fluxes([zw[f, k] for f in range(5)], (2, 3), move=(hxz, hzz, w0z))
        todo = []
        for f in range(5):
            todo += [(r, (f, k), x[f]) for r, x in ((f2zw, a2), (gzw, g))] + put_halo(f3, f, k + 2, a3[f])
        return todo

    batches(0, 12, 4, halo_flux)

    def normal_own(f, k, eta):
        return ih * (eta * d_normal(plane_at(gw, f), k) - d_normal(plane_at(f2w, f), k))

    def ghost_layer(m):
        upper = (m >= 2).astype(jnp.int32)
        k, l, todo = 2 + m + 8 * upper, m - 2 + 16 * upper, []
        for f in range(5):
            dx = patched(d_lane(f1w[f, k]), pltpu.roll(pt[f, 2], patch_shift(l), 1))
            s = qw[f, k] + C * (normal_own(f, k, eta_of(l)) - (dx + d_around(f3, f, k)))
            todo.append((sx, (f, l + 2), s))
        return todo

    def outer(m):
        upper = (m >= 2).astype(jnp.int32)
        k, kz, l, todo = 4 + m + 4 * upper, 2 + m + 4 * upper, m + 12 * upper, []
        eta, half, shift = eta_of(l), l >> 3, patch_shift(l)
        for f in range(5):
            todo.append((sx, (f, l + 2), tx[f, l] + C * normal_own(f, k, eta)))
            dn, dg = d_normal(plane_at(f2zw, f), kz), d_normal(plane_at(gzw, f), kz)
            edge = edges(pltpu.roll(ptz[f, half], shift, 1))
            todo.append((sz, (f, l), tz[f, l] + C * (ihz * (eta * dg - dn) - edge)))
        return todo

    def inner(l):
        half, shift, todo = l >> 3, patch_shift(l), []
        for f in range(5):
            todo.append((sx, (f, l + 2), tx[f, l] + w0 * bx[f, l]))
            edge = edges(pltpu.roll(ptz[f, half], shift, 1))
            todo.append((sz, (f, l), (tz[f, l] + w0z * bz[f, l]) + (hxz * ez[f, l] - C * edge)))
        return todo

    batches(0, 4, 2, ghost_layer)
    batches(0, 4, 2, outer)
    batches(2, 12, 4, inner)
    for f in range(5):
        for k in range(2):
            sx[f, k] = jnp.where(bottom, MIRROR[f] * sx[f, 3 - k], sx[f, k])
            sx[f, 18 + k] = jnp.where(top, b[f], sx[f, 18 + k])

    h1, h1z, h1s = h0 + STEP * w0, h0z + STEP * w0z, h0s + STEP * w0s
    hx1 = SCALE * d_ends(h1, rl(strip_ends(h1s), -12))
    hz1 = SCALE * d_ring(h1, h1z)[0]
    ih1 = 1.0 / h1
    h_out[...] = 0.5 * (h0 + h1 + STEP * w1)
    h_copy = pltpu.make_async_copy(h_out, h_hbm, sems.at[4])
    h_copy.start()
    for v in range(2):
        (a1,) = fluxes(strip_s[v], (1,))
        for f in range(5):
            pt[f, v] = strip_ends(a1[f])

    def own_flux_two(l):
        a1, a2, a3, g = fluxes([sx[f, l + 2] for f in range(5)], move=(hx1, hz1, w1))
        todo = []
        for f in range(5):
            todo += [(r, (f, l + 2), x[f]) for r, x in ((f1x, a1), (f2x, a2), (gx, g))]
            todo += [(f3, (f, l + 2, rows(16)), a3[f])]
        return todo

    def halo_flux_two(l):
        (a3,) = fluxes([sz[f, l] for f in range(5)], (3,))
        return [x for f in range(5) for x in put_halo(f3, f, l + 2, a3[f])]

    def final(l):
        eta, shift, todo = eta_of(l), patch_shift(l), []
        for f in range(5):
            dx = d_ends(f1x[f, l + 2], pltpu.roll(pt[f, l >> 3], shift, 1))
            da = d_around(f3, f, l + 2)
            dn, dg = d_normal(plane_at(f2x, f), l + 2), d_normal(plane_at(gx, f), l + 2)
            rate = ih1 * (eta * dg - dn) - (dx + da)
            todo.append((out, (f, l), 0.5 * (q[f, l] + sx[f, l + 2] + C * rate)))
        return todo

    batches(-2, 20, 4, own_flux_two)
    batches(0, NL, 4, halo_flux_two)

    def out_copy(i):
        part = (slice(None), pl.ds(4 * i, 4))
        return pltpu.make_async_copy(out.at[part], out_hbm.at[part], sems.at[i])

    batches(0, NL, 4, final, lambda i: out_copy(i).start())
    for i in range(4):
        out_copy(i).wait()
    h_copy.wait()


def call(body, ins, outs, scratch=(), sems=0, space=VM, out_space=VM):
    shapes = tuple(jax.ShapeDtypeStruct(s, F32) for s in outs)
    return pl.pallas_call(
        body,
        out_shape=shapes,
        in_specs=[space] * len(ins),
        out_specs=tuple([out_space] * len(shapes)),
        scratch_shapes=[pltpu.VMEM(s, F32) for s in scratch] + [pltpu.SemaphoreType.DMA((sems,))] * (sems > 0),
        compiler_params=pltpu.CompilerParams(vmem_limit_bytes=40 * 1024 * 1024),
    )(*ins)


def where_am_i():
    return lax.axis_index("sx"), lax.axis_size("sx")


def stage_rows(*refs):
    pack_rows(lax.axis_index("az") % 2 == 1, *refs)


def stage_own(*refs):
    own_parts(*refs)


def stage_columns(*refs):
    pack_columns(lax.axis_index("sx") % 2 == 0, *refs)


def stage_corners(*refs):
    pack_corners(lax.axis_index("sx") % 2 == 0, *refs)


def stage_second(*refs):
    pack_second(lax.axis_index("az") % 2 == 1, lax.axis_index("wn"), *where_am_i(), *refs)


def stage_far(*refs):
    pack_far(lax.axis_index("wn"), *refs)


def stage_prepare(*refs):
    prepare(lax.axis_index("wn"), *refs)


def stage_advance(*refs):
    advance(lax.axis_index("wn"), *where_am_i(), *refs)


def swaps(size, start, wrap):
    pairs = [(i, (i + 1) % size) for i in range(start, size if wrap else size - 1, 2)]
    return pairs + [(j, i) for i, j in pairs]


def per_device(fields, height, behind):
    around = lax.axis_size("az")
    tiles = lax.axis_size("sx")
    plane = (8, 128)
    *own, one, two = call(
        stage_rows,
        [pltpu.with_memory_space_constraint(x, pltpu.HBM) for x in (fields, height, behind)],
        [fields.shape, height.shape, behind.shape] + [(HALF, *plane)] * 2,
        sems=3,
        space=HBM,
    )
    a2 = lax.ppermute(two, "az", swaps(around, 1, True))
    a1 = lax.ppermute(one, "az", swaps(around, 0, True))
    right, left, one, two = call(stage_columns, own, [(3, *plane)] * 4)
    s2 = lax.ppermute(two, "sx", swaps(tiles, 1, False))
    s1 = lax.ppermute(one, "sx", swaps(tiles, 0, False))
    parts = call(stage_own, (own[0], right), [(5, NL, *plane)] * 5, [(5, NL, *plane)])
    halo, strips, w, near, far = call(
        stage_second,
        (*own, a1, a2, right, left, s1, s2, parts[3]),
        [(NP, *plane), (UNITS, *plane), (4, *plane), (31, *plane), (27, *plane)],
        [(27, *plane)] * 2,
    )
    z_right, z_left, one, two = call(stage_corners, (halo,), [(3, *plane)] * 4)
    near = lax.ppermute(near, "wn", [(0, 1), (1, 0), (2, 3), (3, 2)])
    s2 = lax.ppermute(two, "sx", swaps(tiles, 1, False))
    s1 = lax.ppermute(one, "sx", swaps(tiles, 0, False))
    (far,) = call(stage_far, (far, w, near, two), [(31, *plane)])
    parts = call(
        stage_prepare,
        (own[0], own[1], halo, strips, *parts, far),
        [(5, NL, *plane)] * 5,
        [(5, NL, *plane)] * 4 + [(5, NL, 80, 128), (5, 2, *plane)],
    )
    far = lax.ppermute(far, "wn", [(1, 2), (2, 1), (3, 0)])
    return call(
        stage_advance,
        (*own, halo, strips, w, near, far, z_right, z_left, s1, s2, *parts),
        [(5, NL, *plane), plane],
        [(5, 16, *plane), (5, 12, *plane)]
        + [(5, 16, *plane)] * 3
        + [(5, 12, *plane)] * 2
        + [(5, 20, *plane)] * 3
        + [(5, 20, 80, 128)]
        + [(5, 20, *plane), (5, NL, *plane), (5, 3, *plane), (5, 2, *plane), (UNITS, *plane), (5, NL, *plane), plane],
        sems=5,
        out_space=HBM,
    )


def solution(mesh):
    in_specs = (P(None, "wn", "az", "sx"), P("az", "sx"), P(None, "az", "sx"))
    out_specs = (P(None, "wn", "az", "sx"), P("az", "sx"))
    return jax.shard_map(
        per_device, mesh=mesh, in_specs=in_specs, out_specs=out_specs, check_vma=False
    )
```

```python
import functools

import jax
import jax.numpy as jnp
from jax import lax
from jax.experimental import pallas as pl
from jax.experimental.pallas import tpu as pltpu
from jax.sharding import PartitionSpec as P

GAMMA = 1.4
CFL_STEP = 0.08
LAYERS = 64
NL = 16
NP = 86
HALF = 43
UNITS = 12
SCALE = LAYERS / 12.0
STEP = CFL_STEP / LAYERS
C = CFL_STEP / 12.0
VM = pl.BlockSpec(memory_space=pltpu.VMEM)
HBM = pl.BlockSpec(memory_space=pltpu.HBM)
F32 = jnp.float32
MIRROR = (1.0, -1.0, -1.0, -1.0, 1.0)


def lane():
    return lax.broadcasted_iota(jnp.int32, (8, 128), 1)


def row():
    return lax.broadcasted_iota(jnp.int32, (8, 128), 0)


def rl(x, shift):
    return pltpu.roll(x, shift % 128, 1) if shift % 128 else x


def rs(x, shift):
    return pltpu.roll(x, shift % 8, 0) if shift % 8 else x


def d_lane(x):
    return (rl(x, 2) - rl(x, -2)) + 8.0 * (rl(x, -1) - rl(x, 1))


def strip_patch(d):
    off = lane() & 15
    return jnp.where((off == 12) | (off == 13), rl(d, 8), d)


def strip_ends(x):
    off = lane() & 15
    return jnp.where((off == 10) | (off == 11), rl(x, 8), x)


def d_ends(x, e):
    ln = lane()
    p1 = rl(jnp.where(ln < 1, e, x), -1)
    p2 = rl(jnp.where(ln < 2, e, x), -2)
    m1 = rl(jnp.where(ln >= 127, e, x), 1)
    m2 = rl(jnp.where(ln >= 126, e, x), 2)
    return (m2 - p2) + 8.0 * (p1 - m1)


def patched(d, patch):
    ln = lane()
    return jnp.where((ln < 2) | (ln >= 126), patch, d)


def ring(x, z, shift):
    keep = row() >= shift if shift > 0 else row() < 8 + shift
    a, b = rs(x, shift), rs(z, shift)
    return jnp.where(keep, a, b), jnp.where(keep, b, a)


def d_ring(x, z):
    m2, m1, p1, p2 = ring(x, z, 2), ring(x, z, 1), ring(x, z, -1), ring(x, z, -2)
    return tuple((m2[i] - p2[i]) + 8.0 * (p1[i] - m1[i]) for i in (0, 1))


def spread(x, group):
    ln = lane()
    x = rl(x, -16 * group)
    x = jnp.where(ln < 16, x, rl(x, 16))
    x = jnp.where(ln < 32, x, rl(x, 32))
    return jnp.where(ln < 64, x, rl(x, 64))


def pressure(q):
    kinetic = (q[1] * q[1] + q[2] * q[2] + q[3] * q[3]) / q[0]
    return (GAMMA - 1.0) * (q[4] - 0.5 * kinetic)


def speed(q, b):
    behind = pressure(b)
    return (pressure(q) - behind) / jnp.sqrt(GAMMA * behind * b[0])


def fluxes(q, want=(1, 2, 3), move=None):
    inv = 1.0 / q[0]
    v1, v2, v3 = q[1] * inv, q[2] * inv, q[3] * inv
    q11, q22, q33 = q[1] * v1, q[2] * v2, q[3] * v3
    p = (GAMMA - 1.0) * (q[4] - 0.5 * (q11 + q22 + q33))
    e = q[4] + p
    q12, q13, q23 = q[1] * v2, q[1] * v3, q[2] * v3
    out = []
    if 1 in want:
        out.append([q[1], q11 + p, q12, q13, e * v1])
    if 2 in want:
        out.append([q[2], q12, q22 + p, q23, e * v2])
    if 3 in want:
        out.append([q[3], q13, q23, q33 + p, e * v3])
    if move is not None:
        hx, hz, w = move
        s = hx * v1 + hz * v3
        t = s + w
        out.append([q[0] * t, q[1] * t + p * hx, q[2] * t, q[3] * t + p * hz, q[4] * t + p * s])
    return out


def plane_of(q, h, b):
    def get(i):
        if i < 80:
            return q[i // NL, i % NL]
        return h[...] if i == 80 else b[i - 81]

    return get


def unit_planes(u):
    return [8 * u + j for j in range(8)] if u < 10 else [80] * 8 if u == 11 else [80 + j for j in range(6)]


def columns(get, right, left):
    ln = lane()
    for v in range(3):
        r_acc = jnp.zeros((8, 128), F32)
        l_acc = jnp.zeros((8, 128), F32)
        for u in range(4 * v, min(4 * v + 4, UNITS)):
            for j, i in enumerate(unit_planes(u)):
                at = 16 * j + 4 * (u - 4 * v)
                x = rl(get(i), at + 4)
                r_acc = jnp.where((ln >= at) & (ln < at + 4), x, r_acc)
                at = (at + 4) % 128
                l_acc = jnp.where((ln >= at) & (ln < at + 4), x, l_acc)
        right[v] = r_acc
        left[v] = rl(l_acc, -4)


def to_pairs(even, right, left, one, two):
    for v in range(3):
        one[v] = jnp.where(even, right[v], left[v])
        two[v] = jnp.where(even, left[v], right[v])


def build_strips(tile, tiles, right, left, one, two, put):
    m = lane() & 3
    quad = (lane() >> 2) & 3
    even = tile % 2 == 0
    for v in range(3):
        lm, rm = left[v], right[v]
        end_l = jnp.where(m == 0, lm, jnp.where(m == 1, rl(lm, 1), jnp.where(m == 2, rl(lm, 2), rl(lm, 3))))
        end_r = jnp.where(m == 3, rm, jnp.where(m == 2, rl(rm, -1), jnp.where(m == 1, rl(rm, -2), rl(rm, -3))))
        lh = jnp.where(tile == 0, end_l, jnp.where(even, two[v], one[v]))
        rh = jnp.where(tile == tiles - 1, end_r, jnp.where(even, one[v], two[v]))
        for t in range(min(4, UNITS - 4 * v)):
            a, b, c, d = (rl(x, 4 * (i - t)) for i, x in enumerate((lh, lm, rm, rh)))
            put(4 * v + t, jnp.where(quad < 2, jnp.where(quad == 0, a, b), jnp.where(quad == 2, c, d)))


def pack_rows(odd, q_hbm, h_hbm, b_hbm, q, h, b, one, two, sems):
    copies = [
        pltpu.make_async_copy(x, y, sems.at[i]) for i, (x, y) in enumerate(((q_hbm, q), (h_hbm, h), (b_hbm, b)))
    ]
    for c in copies:
        c.start()
    for c in copies:
        c.wait()
    get = plane_of(q, h, b)
    mask = (row() >= 4) ^ odd
    for i in range(HALF):
        x, y = get(i), rs(get(i + HALF), 4)
        one[i] = jnp.where(mask, x, y)
        two[i] = jnp.where(mask, y, x)


def pack_columns(even, q, h, b, right, left, one, two):
    columns(plane_of(q, h, b), right, left)
    to_pairs(even, right, left, one, two)


def pack_corners(even, z, right, left, one, two):
    columns(lambda i: z[i], right, left)
    to_pairs(even, right, left, one, two)


def pack_second(odd, wn, tile, tiles, q, h, b, a1, a2, right, left, s1, s2, _parts, *outs):
    z, strips, w, near, far, slope, hi, lo = outs
    ln, rw = lane(), row()
    mask = (rw >= 4) ^ odd
    for i in range(HALF):
        x, y = a2[i], a1[i]
        z[i] = jnp.where(mask, x, y)
        z[i + HALF] = rs(jnp.where(mask, y, x), 4)

    def put(u, x):
        strips[u] = x

    build_strips(tile, tiles, right, left, s1, s2, put)
    surf = strips[10]
    own, bq = [q[f, 15] for f in range(5)], [b[f] for f in range(5)]
    zq, bz = [z[f * NL + 15] for f in range(5)], [z[81 + f] for f in range(5)]
    sq = [strips[2 * f + 1] for f in range(5)]
    w0 = speed(own, bq)
    w0z = speed(zq, bz)
    w0s = spread(speed(sq, [rl(surf, 16 * (6 - f)) for f in range(5)]), 7)
    hx = slope[0] = SCALE * patched(d_lane(h[...]), rl(strip_patch(d_lane(strips[11])), -12))
    hz, hzz = (SCALE * x for x in d_ring(h[...], z[80]))
    slope[1], slope[2] = hz, hzz
    (f1s,) = fluxes(sq, (1,))
    (f3z,) = fluxes(zq, (3,))
    levels = []
    for x in ([q[f, 13] for f in range(5)], [q[f, 14] for f in range(5)], own, bq):
        levels.append(fluxes(x, move=(hx, hz, w0)))
    eta = (LAYERS - 0.5) / LAYERS
    ih = 1.0 / h[...]
    top = []
    for f in range(5):
        dx = patched(d_lane(levels[2][0][f]), rl(strip_patch(d_lane(f1s[f])), -124))
        da, _ = d_ring(levels[2][2][f], f3z[f])
        dn, dg = ((levels[0][k][f] - 8.0 * levels[1][k][f]) + 7.0 * levels[3][k][f] for k in (1, 3))
        top.append(own[f] + C * (ih * (eta * dg - dn) - (dx + da)))
    speeds = (w0, w0z, w0s, speed(top, bq))
    for k in range(4):
        w[k] = speeds[k]
        near[27 + k] = speeds[k]
    near_rows = (rw < 2) | (rw >= 6)
    hi_s = hi[26] = strips[9]
    lo_s = lo[26] = strips[8]
    for f in range(5):
        for k in range(4):
            hi[4 * f + k] = q[f, 12 + k]
            lo[4 * f + k] = q[f, k]
        hi[20 + f] = jnp.where(near_rows, z[f * NL + 14], rs(z[f * NL + 15], 4))
        lo[20 + f] = jnp.where(near_rows, z[f * NL], rs(z[f * NL + 1], 4))
        if f < 4:
            inside = (ln >= 32 * f) & (ln < 32 * f + 32)
            hi_s = jnp.where(inside, rl(strips[2 * f + 1], 32 * f + 32), hi_s)
            lo_s = jnp.where(inside, rl(strips[2 * f], 32 * f), lo_s)
    hi[25] = hi_s
    lo[25] = lo_s
    for i in range(27):
        near[i] = jnp.where(wn % 2 == 0, hi[i], lo[i])
        far[i] = jnp.where(wn == 1, hi[i], lo[i])


def pack_far(wn, far, w, near, _corners, out):
    for i in range(27):
        out[i] = far[i]
    for k in range(4):
        out[27 + k] = jnp.where(wn == 2, near[27 + k], w[k])


def d_rows(f3, f, l, at):
    m2, m1, p1, p2 = (f3[f, l, pl.ds(at + k, 8)] for k in (-2, -1, 1, 2))
    return (m2 - p2) + 8.0 * (p1 - m1)


def d_around(f3, f, l):
    return d_rows(f3, f, l, 16)


def d_around_halo(f3, f, l):
    return jnp.where(row() < 4, d_rows(f3, f, l, 24), d_rows(f3, f, l, 8))


def put_halo(f3, f, l, x):
    return [(f3, (f, l, slice(24, 32)), x), (f3, (f, l, slice(8, 16)), x)]


def d_normal(get, l):
    return (get(l - 2) - get(l + 2)) + 8.0 * (get(l + 1) - get(l - 1))


def plane_at(ref, f):
    return lambda l: ref[f, l]


def patch_shift(l):
    return 116 - 16 * (l & 7)


def edges(patch):
    return patched(jnp.zeros_like(patch), patch)


def together(count, *parts, after=None):
    def step(i, _):
        todo = []
        for first, size, body in parts:
            for k in range(size):
                todo += body(first + i * size + k)
        for ref, at, x in todo:
            ref[at] = x
        if after is not None:
            after(i)
        return 0

    lax.fori_loop(0, count, step, 0)


def own_parts(q, _right, f1, f3, d1, dn, dq, f2):
    def flux(l):
        a1, a2, a3 = fluxes([q[f, l] for f in range(5)])
        return [(r, (f, l), x[f]) for f in range(5) for r, x in ((f1, a1), (f2, a2), (f3, a3), (d1, [d_lane(y) for y in a1]))]

    def inner(l):
        return [
            (r, (f, l), d_normal(plane_at(x, f), l)) for f in range(5) for r, x in ((dn, f2), (dq, q))
        ]

    together(4, (0, 4, flux))
    together(3, (2, 4, inner))


def prepare(wn, q, h, z, strips, slope, f1x, f3x, d1x, dnx, dqx, _far, tx, bx, tz, bz, ez, ghost, gx, f1z, f2z, gz, f3, pt):
    h0, h0z = h[...], z[80]
    hx, hz, hzz = (slope[k] for k in range(3))
    ih, ihz = C / h0, C / h0z
    base = wn * NL
    ln = lane()
    for f in range(5):
        s_lo = strips[2 * f]
        mirrored = MIRROR[f] * jnp.where(ln >= 112, rl(s_lo, -16), rl(s_lo, 80))
        ghost[f] = jnp.where(ln < 64, spread(strips[10], 1 + f), mirrored)
    for v in range(2):
        (a1,) = fluxes([strips[2 * f + v] for f in range(5)], (1,))
        for f in range(5):
            pt[f, v] = strip_patch(d_lane(a1[f]))

    def own_moving(l):
        todo = []
        for f in range(5):
            a = f3x[f, l]
            todo += [(gx, (f, l), hx * f1x[f, l] + hz * a), (f3, (f, l, slice(16, 24)), a)]
        return todo

    def halo_flux(l):
        a1, a2, a3 = fluxes([z[f * NL + l] for f in range(5)])
        todo = []
        for f in range(5):
            todo += [(r, (f, l), x) for r, x in ((f1z, a1[f]), (f2z, a2[f]), (gz, hzz * a3[f]))]
            todo += put_halo(f3, f, l, a3[f])
        return todo

    together(4, (0, 4, own_moving), (0, 4, halo_flux))

    def own_surface(f, l):
        dx = patched(d1x[f, l], pltpu.roll(pt[f, l >> 3], patch_shift(l), 1))
        return q[f, l] - C * (dx + d_around(f3, f, l))

    def halo_surface(f, l):
        dx = jnp.where((ln < 2) | (ln >= 126), 0.0, d_lane(f1z[f, l]))
        return z[f * NL + l] - C * (dx + d_around_halo(f3, f, l))

    def own_inner(l):
        k, todo = ih * (((base + l).astype(F32) + 0.5) / LAYERS), []
        for f in range(5):
            t = own_surface(f, l) + (k * d_normal(plane_at(gx, f), l) - ih * dnx[f, l])
            todo += [(tx, (f, l), t), (bx, (f, l), k * dqx[f, l])]
        return todo

    def halo_inner(l):
        k, todo = ihz * (((base + l).astype(F32) + 0.5) / LAYERS), []
        for f in range(5):
            t = halo_surface(f, l) + (k * d_normal(plane_at(gz, f), l) - ihz * d_normal(plane_at(f2z, f), l))
            todo += [(tz, (f, l), t), (bz, (f, l), k * d_normal(lambda i, f=f: z[f * NL + i], l))]
            todo += [(ez, (f, l), k * d_normal(plane_at(f1z, f), l))]
        return todo

    def outer(m):
        l = m + 12 * (m >= 2).astype(jnp.int32)
        return [(tx, (f, l), own_surface(f, l)) for f in range(5)] + [
            (tz, (f, l), halo_surface(f, l)) for f in range(5)
        ]

    together(4, (2, 3, own_inner), (2, 3, halo_inner), (0, 1, outer))


def advance(wn, tile, tiles, q, h, b, z, strips, w, near, far, z_right, z_left, z_one, z_two, slope, tx, bx, tz, bz, ez, ghost, *rest):
    out_hbm, h_hbm, qw, zw, f1w, f2w, gw, f2zw, gzw, f1x, f2x, gx, f3, sx, sz, pt, ptz, zst, out, h_out, sems = rest
    first, last = tile == 0, tile == tiles - 1

    def put_strip(u, x):
        zst[u] = x

    build_strips(tile, tiles, z_right, z_left, z_one, z_two, put_strip)
    odd = wn % 2 == 1

    def below(i):
        return jnp.where(odd, near[i], far[i])

    def above(i):
        return jnp.where(odd, far[i], near[i])

    ln, rw = lane(), row()
    group, off = ln >> 4, ln & 15
    bottom, top = wn == 0, wn == 3
    near_rows = (rw < 2) | (rw >= 6)

    speeds = [jnp.where(top, w[k], jnp.where(wn == 2, near[27 + k], far[27 + k])) for k in range(4)]
    w0, w0z, w0s, w1 = speeds

    strip_q = []
    for f in range(5):
        sign = MIRROR[f]
        bq, bz_ = b[f], z[81 + f]
        for k in range(4):
            qw[f, k] = jnp.where(bottom, sign * q[f, 3 - k], below(4 * f + k))
            qw[f, 4 + k] = q[f, k]
            qw[f, 8 + k] = q[f, 12 + k]
            qw[f, 12 + k] = jnp.where(top, bq, above(4 * f + k))
            zw[f, 2 + k] = z[f * NL + k]
            zw[f, 6 + k] = z[f * NL + 12 + k]
        zb, za = below(20 + f), above(20 + f)
        zw[f, 0] = jnp.where(bottom, sign * z[f * NL + 1], zb)
        zw[f, 1] = jnp.where(bottom, sign * z[f * NL], rs(zb, 4))
        zw[f, 10] = jnp.where(top, bz_, za)
        zw[f, 11] = jnp.where(top, bz_, rs(za, 4))
        s_lo, s_hi = strips[2 * f], strips[2 * f + 1]
        if f < 4:
            sb, sa = rl(below(25), 96 - 32 * f), rl(above(25), -32 * f)
        else:
            sb, sa = below(26), above(26)
        sb = jnp.where(bottom, ghost[f], sb)
        sa = jnp.where(top, ghost[f], sa)
        strip_q.append((s_lo, s_hi, jnp.where(ln < 64, sa, sb)))

    h0, h0z = h[...], z[80]
    h0s, h0sz = strips[11], zst[11]
    hx, hz, hzz = (slope[k] for k in range(3))
    hxz = SCALE * patched(d_lane(h0z), rl(strip_patch(d_lane(h0sz)), -12))
    hxs, hzs = SCALE * d_lane(h0s), SCALE * d_ring(h0s, h0sz)[0]
    ih, ihz, ihs = 1.0 / h0, 1.0 / h0z, 1.0 / h0s
    base = wn * NL

    parts = []
    for v in range(3):
        x = [strip_q[f][v] for f in range(5)]
        a1, a2, a3, g = fluxes(x, move=(hxs, hzs, w0s))
        d1 = [d_lane(a1[f]) for f in range(5)]
        for f in range(5):
            pt[f, v] = strip_patch(d1[f])
        parts.append((d1, a2, a3, g))
    halo3 = []
    for v in range(2):
        x = [zst[2 * f + v] for f in range(5)]
        z1, z3 = fluxes(x, (1, 3))
        for f in range(5):
            ptz[f, v] = strip_patch(d_lane(z1[f]))
        halo3.append(z3)

    def layer_shift(x, v, k):
        a = rl(x[v], -16 * k)
        c = rl(x[(v + (1 if k > 0 else -1)) % 3], -16 * k)
        return jnp.where(ln < 128 - 16 * k if k > 0 else ln >= -16 * k, a, c)

    strip_s = []
    for v in range(2):
        eta = ((base + 8 * v + group).astype(F32) + 0.5) / LAYERS
        done = []
        for f in range(5):
            dn, dg = (
                (layer_shift(x, v, -2) - layer_shift(x, v, 2)) + 8.0 * (layer_shift(x, v, 1) - layer_shift(x, v, -1))
                for x in ([parts[i][k][f] for i in range(3)] for k in (1, 3))
            )
            da, _ = d_ring(parts[v][2][f], halo3[v][f])
            s = strip_q[f][v] + C * (ihs * (eta * dg - dn) - (parts[v][0][f] + da))
            s = jnp.where(first & ((off == 2) | (off == 3)), jnp.where(off == 3, rl(s, -1), rl(s, -2)), s)
            s = jnp.where(last & ((off == 12) | (off == 13)), jnp.where(off == 12, rl(s, 1), rl(s, 2)), s)
            done.append(s)
        strip_s.append(done)

    def own_flux(k):
        a1, a2, a3, g = fluxes([qw[f, k] for f in range(5)], move=(hx, hz, w0))
        todo = []
        for f in range(5):
            todo += [(r, (f, k), x[f]) for r, x in ((f1w, a1), (f2w, a2), (gw, g))]
            todo += [(f3, (f, k, slice(16, 24)), a3[f])]
        return todo

    def eta_of(l):
        return ((base + l).astype(F32) + 0.5) / LAYERS


    def halo_flux(k):
        a2, a3, g = fluxes([zw[f, k] for f in range(5)], (2, 3), move=(hxz, hzz, w0z))
        todo = []
        for f in range(5):
            todo += [(r, (f, k), x[f]) for r, x in ((f2zw, a2), (gzw, g))] + put_halo(f3, f, k + 2, a3[f])
        return todo

    together(4, (0, 4, own_flux), (0, 3, halo_flux))

    def normal_own(f, k, eta):
        return ih * (eta * d_normal(plane_at(gw, f), k) - d_normal(plane_at(f2w, f), k))

    def ghost_layer(m):
        upper = (m >= 2).astype(jnp.int32)
        k, l, todo = 2 + m + 8 * upper, m - 2 + 16 * upper, []
        for f in range(5):
            dx = patched(d_lane(f1w[f, k]), pltpu.roll(pt[f, 2], patch_shift(l), 1))
            s = qw[f, k] + C * (normal_own(f, k, eta_of(l)) - (dx + d_around(f3, f, k)))
            todo.append((sx, (f, l + 2), s))
        return todo

    def outer(m):
        upper = (m >= 2).astype(jnp.int32)
        k, kz, l, todo = 4 + m + 4 * upper, 2 + m + 4 * upper, m + 12 * upper, []
        eta, half, shift = eta_of(l), l >> 3, patch_shift(l)
        for f in range(5):
            todo.append((sx, (f, l + 2), tx[f, l] + C * normal_own(f, k, eta)))
            dn, dg = d_normal(plane_at(f2zw, f), kz), d_normal(plane_at(gzw, f), kz)
            edge = edges(pltpu.roll(ptz[f, half], shift, 1))
            todo.append((sz, (f, l), tz[f, l] + C * (ihz * (eta * dg - dn) - edge)))
        return todo

    def inner(l):
        half, shift, todo = l >> 3, patch_shift(l), []
        for f in range(5):
            todo.append((sx, (f, l + 2), tx[f, l] + w0 * bx[f, l]))
            edge = edges(pltpu.roll(ptz[f, half], shift, 1))
            todo.append((sz, (f, l), (tz[f, l] + w0z * bz[f, l]) + (hxz * ez[f, l] - C * edge)))
        return todo

    together(2, (0, 2, ghost_layer), (0, 2, outer), (2, 6, inner))
    for f in range(5):
        for k in range(2):
            sx[f, k] = jnp.where(bottom, MIRROR[f] * sx[f, 3 - k], sx[f, k])
            sx[f, 18 + k] = jnp.where(top, b[f], sx[f, 18 + k])

    h1, h1z, h1s = h0 + STEP * w0, h0z + STEP * w0z, h0s + STEP * w0s
    hx1 = SCALE * d_ends(h1, rl(strip_ends(h1s), -12))
    hz1 = SCALE * d_ring(h1, h1z)[0]
    ih1 = 1.0 / h1
    h_out[...] = 0.5 * (h0 + h1 + STEP * w1)
    h_copy = pltpu.make_async_copy(h_out, h_hbm, sems.at[4])
    h_copy.start()
    for v in range(2):
        (a1,) = fluxes(strip_s[v], (1,))
        for f in range(5):
            pt[f, v] = strip_ends(a1[f])

    def own_flux_two(l):
        a1, a2, a3, g = fluxes([sx[f, l + 2] for f in range(5)], move=(hx1, hz1, w1))
        todo = []
        for f in range(5):
            todo += [(r, (f, l + 2), x[f]) for r, x in ((f1x, a1), (f2x, a2), (gx, g))]
            todo += [(f3, (f, l + 2, slice(16, 24)), a3[f])]
        return todo

    def halo_flux_two(l):
        (a3,) = fluxes([sz[f, l] for f in range(5)], (3,))
        return [x for f in range(5) for x in put_halo(f3, f, l + 2, a3[f])]

    def final(l):
        eta, shift, todo = eta_of(l), patch_shift(l), []
        for f in range(5):
            dx = d_ends(f1x[f, l + 2], pltpu.roll(pt[f, l >> 3], shift, 1))
            da = d_around(f3, f, l + 2)
            dn, dg = d_normal(plane_at(f2x, f), l + 2), d_normal(plane_at(gx, f), l + 2)
            rate = ih1 * (eta * dg - dn) - (dx + da)
            todo.append((out, (f, l), 0.5 * (q[f, l] + sx[f, l + 2] + C * rate)))
        return todo

    together(4, (-2, 5, own_flux_two), (0, 4, halo_flux_two))

    def out_copy(i):
        part = (slice(None), pl.ds(4 * i, 4))
        return pltpu.make_async_copy(out.at[part], out_hbm.at[part], sems.at[i])

    together(4, (0, 4, final), after=lambda i: out_copy(i).start())
    for i in range(4):
        out_copy(i).wait()
    h_copy.wait()


def call(body, ins, outs, scratch=(), sems=0, space=VM, out_space=VM):
    shapes = tuple(jax.ShapeDtypeStruct(s, F32) for s in outs)
    return pl.pallas_call(
        body,
        out_shape=shapes,
        in_specs=[space] * len(ins),
        out_specs=tuple([out_space] * len(shapes)),
        scratch_shapes=[pltpu.VMEM(s, F32) for s in scratch] + [pltpu.SemaphoreType.DMA((sems,))] * (sems > 0),
        compiler_params=pltpu.CompilerParams(vmem_limit_bytes=40 * 1024 * 1024),
    )(*ins)


def where_am_i():
    return lax.axis_index("sx"), lax.axis_size("sx")


def stage_rows(*refs):
    pack_rows(lax.axis_index("az") % 2 == 1, *refs)


def stage_own(*refs):
    own_parts(*refs)


def stage_columns(*refs):
    pack_columns(lax.axis_index("sx") % 2 == 0, *refs)


def stage_corners(*refs):
    pack_corners(lax.axis_index("sx") % 2 == 0, *refs)


def stage_second(*refs):
    pack_second(lax.axis_index("az") % 2 == 1, lax.axis_index("wn"), *where_am_i(), *refs)


def stage_far(*refs):
    pack_far(lax.axis_index("wn"), *refs)


def stage_prepare(*refs):
    prepare(lax.axis_index("wn"), *refs)


def stage_advance(*refs):
    advance(lax.axis_index("wn"), *where_am_i(), *refs)


def swaps(size, start, wrap):
    pairs = [(i, (i + 1) % size) for i in range(start, size if wrap else size - 1, 2)]
    return pairs + [(j, i) for i, j in pairs]


def per_device(fields, height, behind):
    around = lax.axis_size("az")
    tiles = lax.axis_size("sx")
    plane = (8, 128)
    *own, one, two = call(
        stage_rows,
        [pltpu.with_memory_space_constraint(x, pltpu.HBM) for x in (fields, height, behind)],
        [fields.shape, height.shape, behind.shape] + [(HALF, *plane)] * 2,
        sems=3,
        space=HBM,
    )
    a2 = lax.ppermute(two, "az", swaps(around, 1, True))
    a1 = lax.ppermute(one, "az", swaps(around, 0, True))
    right, left, one, two = call(stage_columns, own, [(3, *plane)] * 4)
    s2 = lax.ppermute(two, "sx", swaps(tiles, 1, False))
    s1 = lax.ppermute(one, "sx", swaps(tiles, 0, False))
    parts = call(stage_own, (own[0], right), [(5, NL, *plane)] * 5, [(5, NL, *plane)])
    halo, strips, w, near, far, slope = call(
        stage_second,
        (*own, a1, a2, right, left, s1, s2, parts[3]),
        [(NP, *plane), (UNITS, *plane), (4, *plane), (31, *plane), (27, *plane), (3, *plane)],
        [(27, *plane)] * 2,
    )
    z_right, z_left, one, two = call(stage_corners, (halo,), [(3, *plane)] * 4)
    near = lax.ppermute(near, "wn", [(0, 1), (1, 0), (2, 3), (3, 2)])
    s2 = lax.ppermute(two, "sx", swaps(tiles, 1, False))
    s1 = lax.ppermute(one, "sx", swaps(tiles, 0, False))
    (far,) = call(stage_far, (far, w, near, two), [(31, *plane)])
    parts = call(
        stage_prepare,
        (own[0], own[1], halo, strips, slope, *parts, far),
        [(5, NL, *plane)] * 5 + [(5, *plane)],
        [(5, NL, *plane)] * 4 + [(5, NL, 40, 128), (5, 2, *plane)],
    )
    far = lax.ppermute(far, "wn", [(1, 2), (2, 1), (3, 0)])
    return call(
        stage_advance,
        (*own, halo, strips, w, near, far, z_right, z_left, s1, s2, slope, *parts),
        [(5, NL, *plane), plane],
        [(5, 16, *plane), (5, 12, *plane)]
        + [(5, 16, *plane)] * 3
        + [(5, 12, *plane)] * 2
        + [(5, 20, *plane)] * 3
        + [(5, 20, 40, 128)]
        + [(5, 20, *plane), (5, NL, *plane), (5, 3, *plane), (5, 2, *plane), (UNITS, *plane), (5, NL, *plane), plane],
        sems=5,
        out_space=HBM,
    )


def solution(mesh):
    in_specs = (P(None, "wn", "az", "sx"), P("az", "sx"), P(None, "az", "sx"))
    out_specs = (P(None, "wn", "az", "sx"), P("az", "sx"))
    return jax.shard_map(
        per_device, mesh=mesh, in_specs=in_specs, out_specs=out_specs, check_vma=False
    )
```

```python
import functools

import jax
import jax.numpy as jnp
from jax import lax
from jax.experimental import pallas as pl
from jax.experimental.pallas import tpu as pltpu
from jax.sharding import PartitionSpec as P

GAMMA = 1.4
CFL_STEP = 0.08
LAYERS = 64
NL = 16
NP = 86
HALF = 43
UNITS = 12
SCALE = LAYERS / 12.0
STEP = CFL_STEP / LAYERS
C = CFL_STEP / 12.0
VM = pl.BlockSpec(memory_space=pltpu.VMEM)
HBM = pl.BlockSpec(memory_space=pltpu.HBM)
F32 = jnp.float32
MIRROR = (1.0, -1.0, -1.0, -1.0, 1.0)


def lane():
    return lax.broadcasted_iota(jnp.int32, (8, 128), 1)


def row():
    return lax.broadcasted_iota(jnp.int32, (8, 128), 0)


def rl(x, shift):
    return pltpu.roll(x, shift % 128, 1) if shift % 128 else x


def rs(x, shift):
    return pltpu.roll(x, shift % 8, 0) if shift % 8 else x


def d_lane(x):
    return (rl(x, 2) - rl(x, -2)) + 8.0 * (rl(x, -1) - rl(x, 1))


def strip_patch(d):
    off = lane() & 15
    return jnp.where((off == 12) | (off == 13), rl(d, 8), d)


def strip_ends(x):
    off = lane() & 15
    return jnp.where((off == 10) | (off == 11), rl(x, 8), x)


def d_ends(x, e):
    ln = lane()
    p1 = rl(jnp.where(ln < 1, e, x), -1)
    p2 = rl(jnp.where(ln < 2, e, x), -2)
    m1 = rl(jnp.where(ln >= 127, e, x), 1)
    m2 = rl(jnp.where(ln >= 126, e, x), 2)
    return (m2 - p2) + 8.0 * (p1 - m1)


def patched(d, patch):
    ln = lane()
    return jnp.where((ln < 2) | (ln >= 126), patch, d)


def ring(x, z, shift):
    keep = row() >= shift if shift > 0 else row() < 8 + shift
    a, b = rs(x, shift), rs(z, shift)
    return jnp.where(keep, a, b), jnp.where(keep, b, a)


def d_ring(x, z):
    m2, m1, p1, p2 = ring(x, z, 2), ring(x, z, 1), ring(x, z, -1), ring(x, z, -2)
    return tuple((m2[i] - p2[i]) + 8.0 * (p1[i] - m1[i]) for i in (0, 1))


def spread(x, group):
    ln = lane()
    x = rl(x, -16 * group)
    x = jnp.where(ln < 16, x, rl(x, 16))
    x = jnp.where(ln < 32, x, rl(x, 32))
    return jnp.where(ln < 64, x, rl(x, 64))


def pressure(q):
    kinetic = (q[1] * q[1] + q[2] * q[2] + q[3] * q[3]) / q[0]
    return (GAMMA - 1.0) * (q[4] - 0.5 * kinetic)


def speed(q, b):
    behind = pressure(b)
    return (pressure(q) - behind) / jnp.sqrt(GAMMA * behind * b[0])


def fluxes(q, want=(1, 2, 3), move=None):
    inv = 1.0 / q[0]
    v1, v2, v3 = q[1] * inv, q[2] * inv, q[3] * inv
    q11, q22, q33 = q[1] * v1, q[2] * v2, q[3] * v3
    p = (GAMMA - 1.0) * (q[4] - 0.5 * (q11 + q22 + q33))
    e = q[4] + p
    q12, q13, q23 = q[1] * v2, q[1] * v3, q[2] * v3
    out = []
    if 1 in want:
        out.append([q[1], q11 + p, q12, q13, e * v1])
    if 2 in want:
        out.append([q[2], q12, q22 + p, q23, e * v2])
    if 3 in want:
        out.append([q[3], q13, q23, q33 + p, e * v3])
    if move is not None:
        hx, hz, w = move
        s = hx * v1 + hz * v3
        t = s + w
        out.append([q[0] * t, q[1] * t + p * hx, q[2] * t, q[3] * t + p * hz, q[4] * t + p * s])
    return out


def plane_of(q, h, b):
    def get(i):
        if i < 80:
            return q[i // NL, i % NL]
        return h[...] if i == 80 else b[i - 81]

    return get


def unit_planes(u):
    return [8 * u + j for j in range(8)] if u < 10 else [80] * 8 if u == 11 else [80 + j for j in range(6)]


def columns(get, right, left):
    ln = lane()
    for v in range(3):
        r_acc = jnp.zeros((8, 128), F32)
        l_acc = jnp.zeros((8, 128), F32)
        for u in range(4 * v, min(4 * v + 4, UNITS)):
            for j, i in enumerate(unit_planes(u)):
                at = 16 * j + 4 * (u - 4 * v)
                x = rl(get(i), at + 4)
                r_acc = jnp.where((ln >= at) & (ln < at + 4), x, r_acc)
                at = (at + 4) % 128
                l_acc = jnp.where((ln >= at) & (ln < at + 4), x, l_acc)
        right[v] = r_acc
        left[v] = rl(l_acc, -4)


def to_pairs(even, right, left, one, two):
    for v in range(3):
        one[v] = jnp.where(even, right[v], left[v])
        two[v] = jnp.where(even, left[v], right[v])


def build_strips(tile, tiles, right, left, one, two, put):
    m = lane() & 3
    quad = (lane() >> 2) & 3
    even = tile % 2 == 0
    for v in range(3):
        lm, rm = left[v], right[v]
        end_l = jnp.where(m == 0, lm, jnp.where(m == 1, rl(lm, 1), jnp.where(m == 2, rl(lm, 2), rl(lm, 3))))
        end_r = jnp.where(m == 3, rm, jnp.where(m == 2, rl(rm, -1), jnp.where(m == 1, rl(rm, -2), rl(rm, -3))))
        lh = jnp.where(tile == 0, end_l, jnp.where(even, two[v], one[v]))
        rh = jnp.where(tile == tiles - 1, end_r, jnp.where(even, one[v], two[v]))
        for t in range(min(4, UNITS - 4 * v)):
            a, b, c, d = (rl(x, 4 * (i - t)) for i, x in enumerate((lh, lm, rm, rh)))
            put(4 * v + t, jnp.where(quad < 2, jnp.where(quad == 0, a, b), jnp.where(quad == 2, c, d)))


def pack_rows(odd, q_hbm, h_hbm, b_hbm, q, h, b, one, two, sems):
    copies = [
        pltpu.make_async_copy(x, y, sems.at[i]) for i, (x, y) in enumerate(((q_hbm, q), (h_hbm, h), (b_hbm, b)))
    ]
    for c in copies:
        c.start()
    for c in copies:
        c.wait()
    get = plane_of(q, h, b)
    mask = (row() >= 4) ^ odd
    for i in range(HALF):
        x, y = get(i), rs(get(i + HALF), 4)
        one[i] = jnp.where(mask, x, y)
        two[i] = jnp.where(mask, y, x)


def pack_columns(even, q, h, b, right, left, one, two):
    columns(plane_of(q, h, b), right, left)
    to_pairs(even, right, left, one, two)


def pack_corners(even, z, right, left, one, two):
    columns(lambda i: z[i], right, left)
    to_pairs(even, right, left, one, two)


def pack_second(odd, wn, tile, tiles, q, h, b, a1, a2, right, left, s1, s2, _parts, *outs):
    z, strips, w, near, far, slope, hi, lo = outs
    ln, rw = lane(), row()
    mask = (rw >= 4) ^ odd
    for i in range(HALF):
        x, y = a2[i], a1[i]
        z[i] = jnp.where(mask, x, y)
        z[i + HALF] = rs(jnp.where(mask, y, x), 4)

    def put(u, x):
        strips[u] = x

    build_strips(tile, tiles, right, left, s1, s2, put)
    surf = strips[10]
    own, bq = [q[f, 15] for f in range(5)], [b[f] for f in range(5)]
    zq, bz = [z[f * NL + 15] for f in range(5)], [z[81 + f] for f in range(5)]
    sq = [strips[2 * f + 1] for f in range(5)]
    w0 = speed(own, bq)
    w0z = speed(zq, bz)
    w0s = spread(speed(sq, [rl(surf, 16 * (6 - f)) for f in range(5)]), 7)
    hx = slope[0] = SCALE * patched(d_lane(h[...]), rl(strip_patch(d_lane(strips[11])), -12))
    hz, hzz = (SCALE * x for x in d_ring(h[...], z[80]))
    slope[1], slope[2] = hz, hzz
    (f1s,) = fluxes(sq, (1,))
    (f3z,) = fluxes(zq, (3,))
    levels = []
    for x in ([q[f, 13] for f in range(5)], [q[f, 14] for f in range(5)], own, bq):
        levels.append(fluxes(x, move=(hx, hz, w0)))
    eta = (LAYERS - 0.5) / LAYERS
    ih = 1.0 / h[...]
    top = []
    for f in range(5):
        dx = patched(d_lane(levels[2][0][f]), rl(strip_patch(d_lane(f1s[f])), -124))
        da, _ = d_ring(levels[2][2][f], f3z[f])
        dn, dg = ((levels[0][k][f] - 8.0 * levels[1][k][f]) + 7.0 * levels[3][k][f] for k in (1, 3))
        top.append(own[f] + C * (ih * (eta * dg - dn) - (dx + da)))
    speeds = (w0, w0z, w0s, speed(top, bq))
    for k in range(4):
        w[k] = speeds[k]
        near[27 + k] = speeds[k]
    near_rows = (rw < 2) | (rw >= 6)
    hi_s = hi[26] = strips[9]
    lo_s = lo[26] = strips[8]
    for f in range(5):
        for k in range(4):
            hi[4 * f + k] = q[f, 12 + k]
            lo[4 * f + k] = q[f, k]
        hi[20 + f] = jnp.where(near_rows, z[f * NL + 14], rs(z[f * NL + 15], 4))
        lo[20 + f] = jnp.where(near_rows, z[f * NL], rs(z[f * NL + 1], 4))
        if f < 4:
            inside = (ln >= 32 * f) & (ln < 32 * f + 32)
            hi_s = jnp.where(inside, rl(strips[2 * f + 1], 32 * f + 32), hi_s)
            lo_s = jnp.where(inside, rl(strips[2 * f], 32 * f), lo_s)
    hi[25] = hi_s
    lo[25] = lo_s
    for i in range(27):
        near[i] = jnp.where(wn % 2 == 0, hi[i], lo[i])
        far[i] = jnp.where(wn == 1, hi[i], lo[i])


def pack_far(wn, far, w, near, _corners, out):
    for i in range(27):
        out[i] = far[i]
    for k in range(4):
        out[27 + k] = jnp.where(wn == 2, near[27 + k], w[k])


def d_rows(f3, f, l, at):
    m2, m1, p1, p2 = (f3[f, l, pl.ds(at + k, 8)] for k in (-2, -1, 1, 2))
    return (m2 - p2) + 8.0 * (p1 - m1)


def d_around(f3, f, l):
    return d_rows(f3, f, l, 16)


def d_around_halo(f3, f, l):
    return jnp.where(row() < 4, d_rows(f3, f, l, 24), d_rows(f3, f, l, 8))


def put_halo(f3, f, l, x):
    return [(f3, (f, l, slice(24, 32)), x), (f3, (f, l, slice(8, 16)), x)]


def d_normal(get, l):
    return (get(l - 2) - get(l + 2)) + 8.0 * (get(l + 1) - get(l - 1))


def plane_at(ref, f):
    return lambda l: ref[f, l]


def patch_shift(l):
    return 116 - 16 * (l & 7)


def edges(patch):
    return patched(jnp.zeros_like(patch), patch)


def together(count, *parts, after=None):
    def step(i, _):
        todo = []
        for first, size, body in parts:
            for k in range(size):
                todo += body(first + i * size + k)
        for ref, at, x in todo:
            ref[at] = x
        if after is not None:
            after(i)
        return 0

    lax.fori_loop(0, count, step, 0)


def own_parts(q, _right, f1, f3, d1, dn, dq, f2):
    def flux(l):
        a1, a2, a3 = fluxes([q[f, l] for f in range(5)])
        return [(r, (f, l), x[f]) for f in range(5) for r, x in ((f1, a1), (f2, a2), (f3, a3), (d1, [d_lane(y) for y in a1]))]

    def inner(l):
        return [
            (r, (f, l), d_normal(plane_at(x, f), l)) for f in range(5) for r, x in ((dn, f2), (dq, q))
        ]

    together(4, (0, 4, flux))
    together(3, (2, 4, inner))


def prepare(wn, q, h, z, strips, slope, f1x, f3x, d1x, dnx, dqx, _far, tx, bx, tz, bz, ez, ghost, gx, f1z, f2z, gz, f3, pt):
    h0, h0z = h[...], z[80]
    hx, hz, hzz = (slope[k] for k in range(3))
    ih, ihz = C / h0, C / h0z
    base = wn * NL
    ln = lane()
    for f in range(5):
        s_lo = strips[2 * f]
        mirrored = MIRROR[f] * jnp.where(ln >= 112, rl(s_lo, -16), rl(s_lo, 80))
        ghost[f] = jnp.where(ln < 64, spread(strips[10], 1 + f), mirrored)
    for v in range(2):
        (a1,) = fluxes([strips[2 * f + v] for f in range(5)], (1,))
        for f in range(5):
            pt[f, v] = strip_patch(d_lane(a1[f]))

    def own_moving(l):
        todo = []
        for f in range(5):
            a = f3x[f, l]
            todo += [(gx, (f, l), hx * f1x[f, l] + hz * a), (f3, (f, l, slice(16, 24)), a)]
        return todo

    def halo_flux(l):
        a1, a2, a3 = fluxes([z[f * NL + l] for f in range(5)])
        todo = []
        for f in range(5):
            todo += [(r, (f, l), x) for r, x in ((f1z, a1[f]), (f2z, a2[f]), (gz, hzz * a3[f]))]
            todo += put_halo(f3, f, l, a3[f])
        return todo

    together(4, (0, 4, own_moving), (0, 4, halo_flux))

    def own_surface(f, l):
        dx = patched(d1x[f, l], pltpu.roll(pt[f, l >> 3], patch_shift(l), 1))
        return q[f, l] - C * (dx + d_around(f3, f, l))

    def halo_surface(f, l):
        dx = jnp.where((ln < 2) | (ln >= 126), 0.0, d_lane(f1z[f, l]))
        return z[f * NL + l] - C * (dx + d_around_halo(f3, f, l))

    def own_inner(l):
        k, todo = ih * (((base + l).astype(F32) + 0.5) / LAYERS), []
        for f in range(5):
            t = own_surface(f, l) + (k * d_normal(plane_at(gx, f), l) - ih * dnx[f, l])
            todo += [(tx, (f, l), t), (bx, (f, l), k * dqx[f, l])]
        return todo

    def halo_inner(l):
        k, todo = ihz * (((base + l).astype(F32) + 0.5) / LAYERS), []
        for f in range(5):
            t = halo_surface(f, l) + (k * d_normal(plane_at(gz, f), l) - ihz * d_normal(plane_at(f2z, f), l))
            todo += [(tz, (f, l), t), (bz, (f, l), k * d_normal(lambda i, f=f: z[f * NL + i], l))]
            todo += [(ez, (f, l), k * d_normal(plane_at(f1z, f), l))]
        return todo

    def outer(m):
        l = m + 12 * (m >= 2).astype(jnp.int32)
        return [(tx, (f, l), own_surface(f, l)) for f in range(5)] + [
            (tz, (f, l), halo_surface(f, l)) for f in range(5)
        ]

    together(4, (2, 3, own_inner), (2, 3, halo_inner), (0, 1, outer))


def advance(wn, tile, tiles, q, h, b, z, strips, w, near, far, z_right, z_left, z_one, z_two, slope, tx, bx, tz, bz, ez, ghost, *rest):
    out_hbm, h_hbm, qw, zw, f1w, f2w, gw, f2zw, gzw, f1x, f2x, gx, f3, sx, sz, pt, ptz, zst, out, h_out, sems = rest
    first, last = tile == 0, tile == tiles - 1

    def put_strip(u, x):
        zst[u] = x

    build_strips(tile, tiles, z_right, z_left, z_one, z_two, put_strip)
    odd = wn % 2 == 1

    def below(i):
        return jnp.where(odd, near[i], far[i])

    def above(i):
        return jnp.where(odd, far[i], near[i])

    ln, rw = lane(), row()
    group, off = ln >> 4, ln & 15
    bottom, top = wn == 0, wn == 3
    near_rows = (rw < 2) | (rw >= 6)

    speeds = [jnp.where(top, w[k], jnp.where(wn == 2, near[27 + k], far[27 + k])) for k in range(4)]
    w0, w0z, w0s, w1 = speeds

    strip_q = []
    for f in range(5):
        sign = MIRROR[f]
        bq, bz_ = b[f], z[81 + f]
        for k in range(4):
            qw[f, k] = jnp.where(bottom, sign * q[f, 3 - k], below(4 * f + k))
            qw[f, 4 + k] = q[f, k]
            qw[f, 8 + k] = q[f, 12 + k]
            qw[f, 12 + k] = jnp.where(top, bq, above(4 * f + k))
            zw[f, 2 + k] = z[f * NL + k]
            zw[f, 6 + k] = z[f * NL + 12 + k]
        zb, za = below(20 + f), above(20 + f)
        zw[f, 0] = jnp.where(bottom, sign * z[f * NL + 1], zb)
        zw[f, 1] = jnp.where(bottom, sign * z[f * NL], rs(zb, 4))
        zw[f, 10] = jnp.where(top, bz_, za)
        zw[f, 11] = jnp.where(top, bz_, rs(za, 4))
        s_lo, s_hi = strips[2 * f], strips[2 * f + 1]
        if f < 4:
            sb, sa = rl(below(25), 96 - 32 * f), rl(above(25), -32 * f)
        else:
            sb, sa = below(26), above(26)
        sb = jnp.where(bottom, ghost[f], sb)
        sa = jnp.where(top, ghost[f], sa)
        strip_q.append((s_lo, s_hi, jnp.where(ln < 64, sa, sb)))

    h0, h0z = h[...], z[80]
    h0s, h0sz = strips[11], zst[11]
    hx, hz, hzz = (slope[k] for k in range(3))
    hxz = SCALE * patched(d_lane(h0z), rl(strip_patch(d_lane(h0sz)), -12))
    hxs, hzs = SCALE * d_lane(h0s), SCALE * d_ring(h0s, h0sz)[0]
    ih, ihz, ihs = 1.0 / h0, 1.0 / h0z, 1.0 / h0s
    base = wn * NL

    parts = []
    for v in range(3):
        x = [strip_q[f][v] for f in range(5)]
        a1, a2, a3, g = fluxes(x, move=(hxs, hzs, w0s))
        d1 = [d_lane(a1[f]) for f in range(5)]
        for f in range(5):
            pt[f, v] = strip_patch(d1[f])
        parts.append((d1, a2, a3, g))
    halo3 = []
    for v in range(2):
        x = [zst[2 * f + v] for f in range(5)]
        z1, z3 = fluxes(x, (1, 3))
        for f in range(5):
            ptz[f, v] = strip_patch(d_lane(z1[f]))
        halo3.append(z3)

    def layer_shift(x, v, k):
        a = rl(x[v], -16 * k)
        c = rl(x[(v + (1 if k > 0 else -1)) % 3], -16 * k)
        return jnp.where(ln < 128 - 16 * k if k > 0 else ln >= -16 * k, a, c)

    strip_s = []
    for v in range(2):
        eta = ((base + 8 * v + group).astype(F32) + 0.5) / LAYERS
        done = []
        for f in range(5):
            dn, dg = (
                (layer_shift(x, v, -2) - layer_shift(x, v, 2)) + 8.0 * (layer_shift(x, v, 1) - layer_shift(x, v, -1))
                for x in ([parts[i][k][f] for i in range(3)] for k in (1, 3))
            )
            da, _ = d_ring(parts[v][2][f], halo3[v][f])
            s = strip_q[f][v] + C * (ihs * (eta * dg - dn) - (parts[v][0][f] + da))
            s = jnp.where(first & ((off == 2) | (off == 3)), jnp.where(off == 3, rl(s, -1), rl(s, -2)), s)
            s = jnp.where(last & ((off == 12) | (off == 13)), jnp.where(off == 12, rl(s, 1), rl(s, 2)), s)
            done.append(s)
        strip_s.append(done)

    def own_flux(k):
        a1, a2, a3, g = fluxes([qw[f, k] for f in range(5)], move=(hx, hz, w0))
        todo = []
        for f in range(5):
            todo += [(r, (f, k), x[f]) for r, x in ((f1w, a1), (f2w, a2), (gw, g))]
            todo += [(f3, (f, k, slice(16, 24)), a3[f])]
        return todo

    def eta_of(l):
        return ((base + l).astype(F32) + 0.5) / LAYERS


    def halo_flux(k):
        a2, a3, g = fluxes([zw[f, k] for f in range(5)], (2, 3), move=(hxz, hzz, w0z))
        todo = []
        for f in range(5):
            todo += [(r, (f, k), x[f]) for r, x in ((f2zw, a2), (gzw, g))] + put_halo(f3, f, k + 2, a3[f])
        return todo

    together(4, (0, 4, own_flux), (0, 3, halo_flux))

    def normal_own(f, k, eta):
        return ih * (eta * d_normal(plane_at(gw, f), k) - d_normal(plane_at(f2w, f), k))

    def ghost_layer(m):
        upper = (m >= 2).astype(jnp.int32)
        k, l, todo = 2 + m + 8 * upper, m - 2 + 16 * upper, []
        for f in range(5):
            dx = patched(d_lane(f1w[f, k]), pltpu.roll(pt[f, 2], patch_shift(l), 1))
            s = qw[f, k] + C * (normal_own(f, k, eta_of(l)) - (dx + d_around(f3, f, k)))
            todo.append((sx, (f, l + 2), s))
        return todo

    def outer(m):
        upper = (m >= 2).astype(jnp.int32)
        k, kz, l, todo = 4 + m + 4 * upper, 2 + m + 4 * upper, m + 12 * upper, []
        eta, half, shift = eta_of(l), l >> 3, patch_shift(l)
        for f in range(5):
            todo.append((sx, (f, l + 2), tx[f, l] + C * normal_own(f, k, eta)))
            dn, dg = d_normal(plane_at(f2zw, f), kz), d_normal(plane_at(gzw, f), kz)
            edge = edges(pltpu.roll(ptz[f, half], shift, 1))
            todo.append((sz, (f, l), tz[f, l] + C * (ihz * (eta * dg - dn) - edge)))
        return todo

    def inner(l):
        half, shift, todo = l >> 3, patch_shift(l), []
        for f in range(5):
            todo.append((sx, (f, l + 2), tx[f, l] + w0 * bx[f, l]))
            edge = edges(pltpu.roll(ptz[f, half], shift, 1))
            todo.append((sz, (f, l), (tz[f, l] + w0z * bz[f, l]) + (hxz * ez[f, l] - C * edge)))
        return todo

    together(2, (0, 2, ghost_layer), (0, 2, outer), (2, 6, inner))
    for f in range(5):
        for k in range(2):
            sx[f, k] = jnp.where(bottom, MIRROR[f] * sx[f, 3 - k], sx[f, k])
            sx[f, 18 + k] = jnp.where(top, b[f], sx[f, 18 + k])

    h1, h1z, h1s = h0 + STEP * w0, h0z + STEP * w0z, h0s + STEP * w0s
    hx1 = SCALE * d_ends(h1, rl(strip_ends(h1s), -12))
    hz1 = SCALE * d_ring(h1, h1z)[0]
    ih1 = 1.0 / h1
    h_out[...] = 0.5 * (h0 + h1 + STEP * w1)
    h_copy = pltpu.make_async_copy(h_out, h_hbm, sems.at[4])
    h_copy.start()
    for v in range(2):
        (a1,) = fluxes(strip_s[v], (1,))
        for f in range(5):
            pt[f, v] = strip_ends(a1[f])

    def own_flux_two(l):
        a1, a2, a3, g = fluxes([sx[f, l + 2] for f in range(5)], move=(hx1, hz1, w1))
        todo = []
        for f in range(5):
            todo += [(r, (f, l + 2), x[f]) for r, x in ((f1x, a1), (f2x, a2), (gx, g))]
            todo += [(f3, (f, l + 2, slice(16, 24)), a3[f])]
        return todo

    def halo_flux_two(l):
        (a3,) = fluxes([sz[f, l] for f in range(5)], (3,))
        return [x for f in range(5) for x in put_halo(f3, f, l + 2, a3[f])]

    def final(l):
        eta, shift, todo = eta_of(l), patch_shift(l), []
        for f in range(5):
            dx = d_ends(f1x[f, l + 2], pltpu.roll(pt[f, l >> 3], shift, 1))
            da = d_around(f3, f, l + 2)
            dn, dg = d_normal(plane_at(f2x, f), l + 2), d_normal(plane_at(gx, f), l + 2)
            rate = ih1 * (eta * dg - dn) - (dx + da)
            todo.append((out, (f, l), 0.5 * (q[f, l] + sx[f, l + 2] + C * rate)))
        return todo

    together(4, (-2, 5, own_flux_two), (0, 4, halo_flux_two))

    def out_copy(i):
        part = (slice(None), pl.ds(4 * i, 4))
        return pltpu.make_async_copy(out.at[part], out_hbm.at[part], sems.at[i])

    together(4, (0, 4, final), after=lambda i: out_copy(i).start())
    for i in range(4):
        out_copy(i).wait()
    h_copy.wait()


def call(body, ins, outs, scratch=(), sems=0, space=VM, out_space=VM):
    shapes = tuple(jax.ShapeDtypeStruct(s, F32) for s in outs)
    return pl.pallas_call(
        body,
        out_shape=shapes,
        in_specs=[space] * len(ins),
        out_specs=tuple([out_space] * len(shapes)),
        scratch_shapes=[pltpu.VMEM(s, F32) for s in scratch] + [pltpu.SemaphoreType.DMA((sems,))] * (sems > 0),
        compiler_params=pltpu.CompilerParams(vmem_limit_bytes=40 * 1024 * 1024),
    )(*ins)


def where_am_i():
    return lax.axis_index("sx"), lax.axis_size("sx")


def stage_rows(*refs):
    pack_rows(lax.axis_index("az") % 2 == 1, *refs)


def stage_own(*refs):
    own_parts(*refs)


def stage_columns(*refs):
    pack_columns(lax.axis_index("sx") % 2 == 0, *refs)


def stage_corners(*refs):
    pack_corners(lax.axis_index("sx") % 2 == 0, *refs)


def stage_second(*refs):
    pack_second(lax.axis_index("az") % 2 == 1, lax.axis_index("wn"), *where_am_i(), *refs)


def stage_far(*refs):
    pack_far(lax.axis_index("wn"), *refs)


def stage_prepare(*refs):
    prepare(lax.axis_index("wn"), *refs)


def stage_advance(*refs):
    advance(lax.axis_index("wn"), *where_am_i(), *refs)


def swaps(size, start, wrap):
    pairs = [(i, (i + 1) % size) for i in range(start, size if wrap else size - 1, 2)]
    return pairs + [(j, i) for i, j in pairs]


def per_device(fields, height, behind):
    around = lax.axis_size("az")
    tiles = lax.axis_size("sx")
    plane = (8, 128)
    *own, one, two = call(
        stage_rows,
        [pltpu.with_memory_space_constraint(x, pltpu.HBM) for x in (fields, height, behind)],
        [fields.shape, height.shape, behind.shape] + [(HALF, *plane)] * 2,
        sems=3,
        space=HBM,
    )
    a2 = lax.ppermute(two, "az", swaps(around, 1, True))
    a1 = lax.ppermute(one, "az", swaps(around, 0, True))
    right, left, one, two = call(stage_columns, own, [(3, *plane)] * 4)
    s2 = lax.ppermute(two, "sx", swaps(tiles, 1, False))
    s1 = lax.ppermute(one, "sx", swaps(tiles, 0, False))
    parts = call(stage_own, (own[0], right), [(5, NL, *plane)] * 5, [(5, NL, *plane)])
    halo, strips, w, near, far, slope = call(
        stage_second,
        (*own, a1, a2, right, left, s1, s2, parts[3]),
        [(NP, *plane), (UNITS, *plane), (4, *plane), (31, *plane), (27, *plane), (3, *plane)],
        [(27, *plane)] * 2,
    )
    z_right, z_left, one, two = call(stage_corners, (halo,), [(3, *plane)] * 2 + [(31, *plane)] * 2)
    near = lax.ppermute(near, "wn", [(0, 1), (1, 0), (2, 3), (3, 2)])
    s2 = lax.ppermute(two, "sx", swaps(tiles, 1, False))
    s1 = lax.ppermute(one, "sx", swaps(tiles, 0, False))
    (far,) = call(stage_far, (far, w, near, two), [(31, *plane)])
    parts = call(
        stage_prepare,
        (own[0], own[1], halo, strips, slope, *parts, far),
        [(5, NL, *plane)] * 5 + [(5, *plane)],
        [(5, NL, *plane)] * 4 + [(5, NL, 40, 128), (5, 2, *plane)],
    )
    far = lax.ppermute(far, "wn", [(1, 2), (2, 1), (3, 0)])
    return call(
        stage_advance,
        (*own, halo, strips, w, near, far, z_right, z_left, s1, s2, slope, *parts),
        [(5, NL, *plane), plane],
        [(5, 16, *plane), (5, 12, *plane)]
        + [(5, 16, *plane)] * 3
        + [(5, 12, *plane)] * 2
        + [(5, 20, *plane)] * 3
        + [(5, 20, 40, 128)]
        + [(5, 20, *plane), (5, NL, *plane), (5, 3, *plane), (5, 2, *plane), (UNITS, *plane), (5, NL, *plane), plane],
        sems=5,
        out_space=HBM,
    )


def solution(mesh):
    in_specs = (P(None, "wn", "az", "sx"), P("az", "sx"), P(None, "az", "sx"))
    out_specs = (P(None, "wn", "az", "sx"), P("az", "sx"))
    return jax.shard_map(
        per_device, mesh=mesh, in_specs=in_specs, out_specs=out_specs, check_vma=False
    )
```

```python
import functools

import jax
import jax.numpy as jnp
from jax import lax
from jax.experimental import pallas as pl
from jax.experimental.pallas import tpu as pltpu
from jax.sharding import PartitionSpec as P

GAMMA = 1.4
CFL_STEP = 0.08
LAYERS = 64
NL = 16
NP = 86
HALF = 43
UNITS = 12
SCALE = LAYERS / 12.0
STEP = CFL_STEP / LAYERS
C = CFL_STEP / 12.0
VM = pl.BlockSpec(memory_space=pltpu.VMEM)
HBM = pl.BlockSpec(memory_space=pltpu.HBM)
F32 = jnp.float32
MIRROR = (1.0, -1.0, -1.0, -1.0, 1.0)


def lane():
    return lax.broadcasted_iota(jnp.int32, (8, 128), 1)


def row():
    return lax.broadcasted_iota(jnp.int32, (8, 128), 0)


def rl(x, shift):
    return pltpu.roll(x, shift % 128, 1) if shift % 128 else x


def rs(x, shift):
    return pltpu.roll(x, shift % 8, 0) if shift % 8 else x


def d_lane(x):
    return (rl(x, 2) - rl(x, -2)) + 8.0 * (rl(x, -1) - rl(x, 1))


def strip_patch(d):
    off = lane() & 15
    return jnp.where((off == 12) | (off == 13), rl(d, 8), d)


def strip_ends(x):
    off = lane() & 15
    return jnp.where((off == 10) | (off == 11), rl(x, 8), x)


def d_ends(x, e):
    ln = lane()
    p1 = rl(jnp.where(ln < 1, e, x), -1)
    p2 = rl(jnp.where(ln < 2, e, x), -2)
    m1 = rl(jnp.where(ln >= 127, e, x), 1)
    m2 = rl(jnp.where(ln >= 126, e, x), 2)
    return (m2 - p2) + 8.0 * (p1 - m1)


def patched(d, patch):
    ln = lane()
    return jnp.where((ln < 2) | (ln >= 126), patch, d)


def ring(x, z, shift):
    keep = row() >= shift if shift > 0 else row() < 8 + shift
    a, b = rs(x, shift), rs(z, shift)
    return jnp.where(keep, a, b), jnp.where(keep, b, a)


def d_ring(x, z):
    m2, m1, p1, p2 = ring(x, z, 2), ring(x, z, 1), ring(x, z, -1), ring(x, z, -2)
    return tuple((m2[i] - p2[i]) + 8.0 * (p1[i] - m1[i]) for i in (0, 1))


def spread(x, group):
    ln = lane()
    x = rl(x, -16 * group)
    x = jnp.where(ln < 16, x, rl(x, 16))
    x = jnp.where(ln < 32, x, rl(x, 32))
    return jnp.where(ln < 64, x, rl(x, 64))


def pressure(q):
    kinetic = (q[1] * q[1] + q[2] * q[2] + q[3] * q[3]) / q[0]
    return (GAMMA - 1.0) * (q[4] - 0.5 * kinetic)


def speed(q, b):
    behind = pressure(b)
    return (pressure(q) - behind) / jnp.sqrt(GAMMA * behind * b[0])


def fluxes(q, want=(1, 2, 3), move=None):
    inv = 1.0 / q[0]
    v1, v2, v3 = q[1] * inv, q[2] * inv, q[3] * inv
    q11, q22, q33 = q[1] * v1, q[2] * v2, q[3] * v3
    p = (GAMMA - 1.0) * (q[4] - 0.5 * (q11 + q22 + q33))
    e = q[4] + p
    q12, q13, q23 = q[1] * v2, q[1] * v3, q[2] * v3
    out = []
    if 1 in want:
        out.append([q[1], q11 + p, q12, q13, e * v1])
    if 2 in want:
        out.append([q[2], q12, q22 + p, q23, e * v2])
    if 3 in want:
        out.append([q[3], q13, q23, q33 + p, e * v3])
    if move is not None:
        hx, hz, w = move
        s = hx * v1 + hz * v3
        t = s + w
        out.append([q[0] * t, q[1] * t + p * hx, q[2] * t, q[3] * t + p * hz, q[4] * t + p * s])
    return out


def plane_of(q, h, b):
    def get(i):
        if i < 80:
            return q[i // NL, i % NL]
        return h[...] if i == 80 else b[i - 81]

    return get


def unit_planes(u):
    return [8 * u + j for j in range(8)] if u < 10 else [80] * 8 if u == 11 else [80 + j for j in range(6)]


def columns(get, right, left):
    ln = lane()
    for v in range(3):
        r_acc = jnp.zeros((8, 128), F32)
        l_acc = jnp.zeros((8, 128), F32)
        for u in range(4 * v, min(4 * v + 4, UNITS)):
            for j, i in enumerate(unit_planes(u)):
                at = 16 * j + 4 * (u - 4 * v)
                x = rl(get(i), at + 4)
                r_acc = jnp.where((ln >= at) & (ln < at + 4), x, r_acc)
                at = (at + 4) % 128
                l_acc = jnp.where((ln >= at) & (ln < at + 4), x, l_acc)
        right[v] = r_acc
        left[v] = rl(l_acc, -4)


def to_pairs(even, right, left, one, two):
    for v in range(3):
        one[v] = jnp.where(even, right[v], left[v])
        two[v] = jnp.where(even, left[v], right[v])


def build_strips(tile, tiles, right, left, one, two, put):
    m = lane() & 3
    quad = (lane() >> 2) & 3
    even = tile % 2 == 0
    for v in range(3):
        lm, rm = left[v], right[v]
        end_l = jnp.where(m == 0, lm, jnp.where(m == 1, rl(lm, 1), jnp.where(m == 2, rl(lm, 2), rl(lm, 3))))
        end_r = jnp.where(m == 3, rm, jnp.where(m == 2, rl(rm, -1), jnp.where(m == 1, rl(rm, -2), rl(rm, -3))))
        lh = jnp.where(tile == 0, end_l, jnp.where(even, two[v], one[v]))
        rh = jnp.where(tile == tiles - 1, end_r, jnp.where(even, one[v], two[v]))
        for t in range(min(4, UNITS - 4 * v)):
            a, b, c, d = (rl(x, 4 * (i - t)) for i, x in enumerate((lh, lm, rm, rh)))
            put(4 * v + t, jnp.where(quad < 2, jnp.where(quad == 0, a, b), jnp.where(quad == 2, c, d)))


def pack_rows(odd, q_hbm, h_hbm, b_hbm, q, h, b, one, two, sems):
    copies = [
        pltpu.make_async_copy(x, y, sems.at[i]) for i, (x, y) in enumerate(((q_hbm, q), (h_hbm, h), (b_hbm, b)))
    ]
    for c in copies:
        c.start()
    for c in copies:
        c.wait()
    get = plane_of(q, h, b)
    mask = (row() >= 4) ^ odd
    for i in range(HALF):
        x, y = get(i), rs(get(i + HALF), 4)
        one[i] = jnp.where(mask, x, y)
        two[i] = jnp.where(mask, y, x)


def pack_columns(even, q, h, b, right, left, one, two):
    columns(plane_of(q, h, b), right, left)
    to_pairs(even, right, left, one, two)


def pack_corners(even, z, right, left, one, two):
    columns(lambda i: z[i], right, left)
    to_pairs(even, right, left, one, two)


def pack_second(odd, wn, tile, tiles, q, h, b, a1, a2, right, left, s1, s2, _parts, *outs):
    z, strips, w, near, far, slope, hi, lo = outs
    ln, rw = lane(), row()
    mask = (rw >= 4) ^ odd
    for i in range(HALF):
        x, y = a2[i], a1[i]
        z[i] = jnp.where(mask, x, y)
        z[i + HALF] = rs(jnp.where(mask, y, x), 4)

    def put(u, x):
        strips[u] = x

    build_strips(tile, tiles, right, left, s1, s2, put)
    surf = strips[10]
    own, bq = [q[f, 15] for f in range(5)], [b[f] for f in range(5)]
    zq, bz = [z[f * NL + 15] for f in range(5)], [z[81 + f] for f in range(5)]
    sq = [strips[2 * f + 1] for f in range(5)]
    w0 = speed(own, bq)
    w0z = speed(zq, bz)
    w0s = spread(speed(sq, [rl(surf, 16 * (6 - f)) for f in range(5)]), 7)
    hx = slope[0] = SCALE * patched(d_lane(h[...]), rl(strip_patch(d_lane(strips[11])), -12))
    hz, hzz = (SCALE * x for x in d_ring(h[...], z[80]))
    slope[1], slope[2] = hz, hzz
    (f1s,) = fluxes(sq, (1,))
    (f3z,) = fluxes(zq, (3,))
    levels = []
    for x in ([q[f, 13] for f in range(5)], [q[f, 14] for f in range(5)], own, bq):
        levels.append(fluxes(x, move=(hx, hz, w0)))
    eta = (LAYERS - 0.5) / LAYERS
    ih = 1.0 / h[...]
    top = []
    for f in range(5):
        dx = patched(d_lane(levels[2][0][f]), rl(strip_patch(d_lane(f1s[f])), -124))
        da, _ = d_ring(levels[2][2][f], f3z[f])
        dn, dg = ((levels[0][k][f] - 8.0 * levels[1][k][f]) + 7.0 * levels[3][k][f] for k in (1, 3))
        top.append(own[f] + C * (ih * (eta * dg - dn) - (dx + da)))
    speeds = (w0, w0z, w0s, speed(top, bq))
    for k in range(4):
        w[k] = speeds[k]
        near[27 + k] = speeds[k]
    near_rows = (rw < 2) | (rw >= 6)
    hi_s = hi[26] = strips[9]
    lo_s = lo[26] = strips[8]
    for f in range(5):
        for k in range(4):
            hi[4 * f + k] = q[f, 12 + k]
            lo[4 * f + k] = q[f, k]
        hi[20 + f] = jnp.where(near_rows, z[f * NL + 14], rs(z[f * NL + 15], 4))
        lo[20 + f] = jnp.where(near_rows, z[f * NL], rs(z[f * NL + 1], 4))
        if f < 4:
            inside = (ln >= 32 * f) & (ln < 32 * f + 32)
            hi_s = jnp.where(inside, rl(strips[2 * f + 1], 32 * f + 32), hi_s)
            lo_s = jnp.where(inside, rl(strips[2 * f], 32 * f), lo_s)
    hi[25] = hi_s
    lo[25] = lo_s
    for i in range(27):
        near[i] = jnp.where(wn % 2 == 0, hi[i], lo[i])
        far[i] = jnp.where(wn == 1, hi[i], lo[i])


def pack_far(wn, far, w, near, _corners, out):
    for i in range(27):
        out[i] = far[i]
    for k in range(4):
        out[27 + k] = jnp.where(wn == 2, near[27 + k], w[k])


def d_rows(f3, f, l, at):
    m2, m1, p1, p2 = (f3[f, l, pl.ds(at + k, 8)] for k in (-2, -1, 1, 2))
    return (m2 - p2) + 8.0 * (p1 - m1)


def d_around(f3, f, l):
    return d_rows(f3, f, l, 16)


def d_around_halo(f3, f, l):
    return jnp.where(row() < 4, d_rows(f3, f, l, 24), d_rows(f3, f, l, 8))


def put_halo(f3, f, l, x):
    return [(f3, (f, l, slice(24, 32)), x), (f3, (f, l, slice(8, 16)), x)]


def d_normal(get, l):
    return (get(l - 2) - get(l + 2)) + 8.0 * (get(l + 1) - get(l - 1))


def plane_at(ref, f):
    return lambda l: ref[f, l]


def patch_shift(l):
    return 116 - 16 * (l & 7)


def edges(patch):
    return patched(jnp.zeros_like(patch), patch)


def together(count, *parts, after=None):
    def step(i, _):
        todo = []
        for first, size, body in parts:
            for k in range(size):
                todo += body(first + i * size + k)
        for ref, at, x in todo:
            ref[at] = x
        if after is not None:
            after(i)
        return 0

    lax.fori_loop(0, count, step, 0)


def own_parts(q, _right, f1, f3, d1, dn, dq, f2):
    def flux(l):
        a1, a2, a3 = fluxes([q[f, l] for f in range(5)])
        return [(r, (f, l), x[f]) for f in range(5) for r, x in ((f1, a1), (f2, a2), (f3, a3), (d1, [d_lane(y) for y in a1]))]

    def inner(l):
        return [
            (r, (f, l), d_normal(plane_at(x, f), l)) for f in range(5) for r, x in ((dn, f2), (dq, q))
        ]

    together(4, (0, 4, flux))
    together(3, (2, 4, inner))


def prepare(wn, q, h, z, strips, slope, f1x, f3x, d1x, dnx, dqx, _far, tx, bx, tz, bz, ez, ghost, gx, f1z, f2z, gz, f3, pt):
    h0, h0z = h[...], z[80]
    hx, hz, hzz = (slope[k] for k in range(3))
    ih, ihz = C / h0, C / h0z
    base = wn * NL
    ln = lane()
    for f in range(5):
        s_lo = strips[2 * f]
        mirrored = MIRROR[f] * jnp.where(ln >= 112, rl(s_lo, -16), rl(s_lo, 80))
        ghost[f] = jnp.where(ln < 64, spread(strips[10], 1 + f), mirrored)
    for v in range(2):
        (a1,) = fluxes([strips[2 * f + v] for f in range(5)], (1,))
        for f in range(5):
            pt[f, v] = strip_patch(d_lane(a1[f]))

    def own_moving(l):
        todo = []
        for f in range(5):
            a = f3x[f, l]
            todo += [(gx, (f, l), hx * f1x[f, l] + hz * a), (f3, (f, l, slice(16, 24)), a)]
        return todo

    def halo_flux(l):
        a1, a2, a3 = fluxes([z[f * NL + l] for f in range(5)])
        todo = []
        for f in range(5):
            todo += [(r, (f, l), x) for r, x in ((f1z, a1[f]), (f2z, a2[f]), (gz, hzz * a3[f]))]
            todo += put_halo(f3, f, l, a3[f])
        return todo

    together(4, (0, 4, own_moving), (0, 4, halo_flux))

    def own_surface(f, l):
        dx = patched(d1x[f, l], pltpu.roll(pt[f, l >> 3], patch_shift(l), 1))
        return q[f, l] - C * (dx + d_around(f3, f, l))

    def halo_surface(f, l):
        dx = jnp.where((ln < 2) | (ln >= 126), 0.0, d_lane(f1z[f, l]))
        return z[f * NL + l] - C * (dx + d_around_halo(f3, f, l))

    def own_inner(l):
        k, todo = ih * (((base + l).astype(F32) + 0.5) / LAYERS), []
        for f in range(5):
            t = own_surface(f, l) + (k * d_normal(plane_at(gx, f), l) - ih * dnx[f, l])
            todo += [(tx, (f, l), t), (bx, (f, l), k * dqx[f, l])]
        return todo

    def halo_inner(l):
        k, todo = ihz * (((base + l).astype(F32) + 0.5) / LAYERS), []
        for f in range(5):
            t = halo_surface(f, l) + (k * d_normal(plane_at(gz, f), l) - ihz * d_normal(plane_at(f2z, f), l))
            todo += [(tz, (f, l), t), (bz, (f, l), k * d_normal(lambda i, f=f: z[f * NL + i], l))]
            todo += [(ez, (f, l), k * d_normal(plane_at(f1z, f), l))]
        return todo

    def outer(m):
        l = m + 12 * (m >= 2).astype(jnp.int32)
        return [(tx, (f, l), own_surface(f, l)) for f in range(5)] + [
            (tz, (f, l), halo_surface(f, l)) for f in range(5)
        ]

    together(4, (2, 3, own_inner), (2, 3, halo_inner), (0, 1, outer))


def advance_own(wn, q, h, b, z, strips, w, near, far, slope, tx, bx, ghost, *rest):
    sx, f1x, f2x, gx, f3x, qw, f1w, f2w, gw, f3, pt = rest
    ln = lane()
    bottom, top = wn == 0, wn == 3
    odd = wn % 2 == 1

    def below(i):
        return jnp.where(odd, near[i], far[i])

    def above(i):
        return jnp.where(odd, far[i], near[i])

    speeds = [jnp.where(top, w[k], jnp.where(wn == 2, near[27 + k], far[27 + k])) for k in range(4)]
    w0, w0z, w0s, w1 = speeds

    h0, h0z, h0s = h[...], z[80], strips[11]
    hx, hz, _ = (slope[k] for k in range(3))
    ih = 1.0 / h0
    base = wn * NL
    side = []
    for f in range(5):
        sign, bq, bz = MIRROR[f], b[f], z[81 + f]
        for k in range(4):
            qw[f, k] = jnp.where(bottom, sign * q[f, 3 - k], below(4 * f + k))
            qw[f, 4 + k] = q[f, k]
            qw[f, 8 + k] = q[f, 12 + k]
            qw[f, 12 + k] = jnp.where(top, bq, above(4 * f + k))
        zb, za = below(20 + f), above(20 + f)
        side.append(
            (
                jnp.where(bottom, sign * z[f * NL + 1], zb),
                jnp.where(bottom, sign * z[f * NL], rs(zb, 4)),
                jnp.where(top, bz, za),
                jnp.where(top, bz, rs(za, 4)),
            )
        )
    for i, k in enumerate((2, 3, 12, 13)):
        (a3,) = fluxes([side[f][i] for f in range(5)], (3,))
        for f in range(5):
            for ref, at, x in put_halo(f3, f, k, a3[f]):
                ref[at] = x
    strip_q = []
    for f in range(5):
        if f < 4:
            sb, sa = rl(below(25), 96 - 32 * f), rl(above(25), -32 * f)
        else:
            sb, sa = below(26), above(26)
        sb, sa = jnp.where(bottom, ghost[f], sb), jnp.where(top, ghost[f], sa)
        strip_q.append(jnp.where(ln < 64, sa, sb))
    (a1,) = fluxes(strip_q, (1,))
    for f in range(5):
        pt[f] = strip_patch(d_lane(a1[f]))

    def own_flux(k):
        a1, a2, a3, g = fluxes([qw[f, k] for f in range(5)], move=(hx, hz, w0))
        todo = []
        for f in range(5):
            todo += [(r, (f, k), x[f]) for r, x in ((f1w, a1), (f2w, a2), (gw, g))]
            todo += [(f3, (f, k, slice(16, 24)), a3[f])]
        return todo

    def eta_of(l):
        return ((base + l).astype(F32) + 0.5) / LAYERS


    def normal_own(f, k, eta):
        return ih * (eta * d_normal(plane_at(gw, f), k) - d_normal(plane_at(f2w, f), k))

    def ghost_layer(m):
        upper = (m >= 2).astype(jnp.int32)
        k, l, todo = 2 + m + 8 * upper, m - 2 + 16 * upper, []
        for f in range(5):
            dx = patched(d_lane(f1w[f, k]), pltpu.roll(pt[f], patch_shift(l), 1))
            s = qw[f, k] + C * (normal_own(f, k, eta_of(l)) - (dx + d_around(f3, f, k)))
            todo.append((sx, (f, l + 2), s))
        return todo

    def outer(m):
        upper = (m >= 2).astype(jnp.int32)
        k, l = 4 + m + 4 * upper, m + 12 * upper
        return [(sx, (f, l + 2), tx[f, l] + C * normal_own(f, k, eta_of(l))) for f in range(5)]

    def inner(l):
        return [(sx, (f, l + 2), tx[f, l] + w0 * bx[f, l]) for f in range(5)]

    together(4, (0, 4, own_flux))
    together(2, (0, 2, ghost_layer), (0, 2, outer), (2, 6, inner))
    for f in range(5):
        for k in range(2):
            sx[f, k] = jnp.where(bottom, MIRROR[f] * sx[f, 3 - k], sx[f, k])
            sx[f, 18 + k] = jnp.where(top, b[f], sx[f, 18 + k])

    h1, h1z, h1s = h0 + STEP * w0, h0z + STEP * w0z, h0s + STEP * w0s
    hx1 = SCALE * d_ends(h1, rl(strip_ends(h1s), -12))
    hz1 = SCALE * d_ring(h1, h1z)[0]

    def own_flux_two(l):
        a1, a2, a3, g = fluxes([sx[f, l + 2] for f in range(5)], move=(hx1, hz1, w1))
        todo = []
        for f in range(5):
            todo += [(r, (f, l + 2), x[f]) for r, x in ((f1x, a1), (f2x, a2), (gx, g))]
            todo += [(f3x, (f, l + 2), a3[f])]
        return todo

    together(4, (-2, 5, own_flux_two))


def advance(wn, tile, tiles, q, h, b, z, strips, w, near, far, z_right, z_left, z_one, z_two, slope, tz, bz, ez, ghost, sx, f1x, f2x, gx, f3x, *rest):
    out_hbm, h_hbm, zw, f2zw, gzw, f3, sz, pt, ptz, zst, out, h_out, sems = rest
    first, last = tile == 0, tile == tiles - 1

    def put_strip(u, x):
        zst[u] = x

    build_strips(tile, tiles, z_right, z_left, z_one, z_two, put_strip)
    odd = wn % 2 == 1

    def below(i):
        return jnp.where(odd, near[i], far[i])

    def above(i):
        return jnp.where(odd, far[i], near[i])

    ln, rw = lane(), row()
    group, off = ln >> 4, ln & 15
    bottom, top = wn == 0, wn == 3
    near_rows = (rw < 2) | (rw >= 6)

    speeds = [jnp.where(top, w[k], jnp.where(wn == 2, near[27 + k], far[27 + k])) for k in range(4)]
    w0, w0z, w0s, w1 = speeds

    strip_q = []
    for f in range(5):
        sign = MIRROR[f]
        bq, bz_ = b[f], z[81 + f]
        for k in range(4):
            zw[f, 2 + k] = z[f * NL + k]
            zw[f, 6 + k] = z[f * NL + 12 + k]
        zb, za = below(20 + f), above(20 + f)
        zw[f, 0] = jnp.where(bottom, sign * z[f * NL + 1], zb)
        zw[f, 1] = jnp.where(bottom, sign * z[f * NL], rs(zb, 4))
        zw[f, 10] = jnp.where(top, bz_, za)
        zw[f, 11] = jnp.where(top, bz_, rs(za, 4))
        s_lo, s_hi = strips[2 * f], strips[2 * f + 1]
        if f < 4:
            sb, sa = rl(below(25), 96 - 32 * f), rl(above(25), -32 * f)
        else:
            sb, sa = below(26), above(26)
        sb = jnp.where(bottom, ghost[f], sb)
        sa = jnp.where(top, ghost[f], sa)
        strip_q.append((s_lo, s_hi, jnp.where(ln < 64, sa, sb)))

    h0, h0z = h[...], z[80]
    h0s, h0sz = strips[11], zst[11]
    hx, hz, hzz = (slope[k] for k in range(3))
    hxz = SCALE * patched(d_lane(h0z), rl(strip_patch(d_lane(h0sz)), -12))
    hxs, hzs = SCALE * d_lane(h0s), SCALE * d_ring(h0s, h0sz)[0]
    ih, ihz, ihs = 1.0 / h0, 1.0 / h0z, 1.0 / h0s
    base = wn * NL

    parts = []
    for v in range(3):
        x = [strip_q[f][v] for f in range(5)]
        a1, a2, a3, g = fluxes(x, move=(hxs, hzs, w0s))
        d1 = [d_lane(a1[f]) for f in range(5)]
        for f in range(5):
            pt[f, v] = strip_patch(d1[f])
        parts.append((d1, a2, a3, g))
    halo3 = []
    for v in range(2):
        x = [zst[2 * f + v] for f in range(5)]
        z1, z3 = fluxes(x, (1, 3))
        for f in range(5):
            ptz[f, v] = strip_patch(d_lane(z1[f]))
        halo3.append(z3)

    def layer_shift(x, v, k):
        a = rl(x[v], -16 * k)
        c = rl(x[(v + (1 if k > 0 else -1)) % 3], -16 * k)
        return jnp.where(ln < 128 - 16 * k if k > 0 else ln >= -16 * k, a, c)

    strip_s = []
    for v in range(2):
        eta = ((base + 8 * v + group).astype(F32) + 0.5) / LAYERS
        done = []
        for f in range(5):
            dn, dg = (
                (layer_shift(x, v, -2) - layer_shift(x, v, 2)) + 8.0 * (layer_shift(x, v, 1) - layer_shift(x, v, -1))
                for x in ([parts[i][k][f] for i in range(3)] for k in (1, 3))
            )
            da, _ = d_ring(parts[v][2][f], halo3[v][f])
            s = strip_q[f][v] + C * (ihs * (eta * dg - dn) - (parts[v][0][f] + da))
            s = jnp.where(first & ((off == 2) | (off == 3)), jnp.where(off == 3, rl(s, -1), rl(s, -2)), s)
            s = jnp.where(last & ((off == 12) | (off == 13)), jnp.where(off == 12, rl(s, 1), rl(s, 2)), s)
            done.append(s)
        strip_s.append(done)

    def eta_of(l):
        return ((base + l).astype(F32) + 0.5) / LAYERS


    def halo_flux(k):
        a2, a3, g = fluxes([zw[f, k] for f in range(5)], (2, 3), move=(hxz, hzz, w0z))
        todo = []
        for f in range(5):
            todo += [(r, (f, k), x[f]) for r, x in ((f2zw, a2), (gzw, g))] + put_halo(f3, f, k + 2, a3[f])
        return todo

    together(3, (0, 4, halo_flux))

    def outer(m):
        upper = (m >= 2).astype(jnp.int32)
        kz, l, todo = 2 + m + 4 * upper, m + 12 * upper, []
        eta, half, shift = eta_of(l), l >> 3, patch_shift(l)
        for f in range(5):
            dn, dg = d_normal(plane_at(f2zw, f), kz), d_normal(plane_at(gzw, f), kz)
            edge = edges(pltpu.roll(ptz[f, half], shift, 1))
            todo.append((sz, (f, l), tz[f, l] + C * (ihz * (eta * dg - dn) - edge)))
        return todo

    def inner(l):
        half, shift, todo = l >> 3, patch_shift(l), []
        for f in range(5):
            edge = edges(pltpu.roll(ptz[f, half], shift, 1))
            todo.append((sz, (f, l), (tz[f, l] + w0z * bz[f, l]) + (hxz * ez[f, l] - C * edge)))
        return todo

    together(2, (0, 2, outer), (2, 6, inner))
    h1, h1z, h1s = h0 + STEP * w0, h0z + STEP * w0z, h0s + STEP * w0s
    hx1 = SCALE * d_ends(h1, rl(strip_ends(h1s), -12))
    hz1 = SCALE * d_ring(h1, h1z)[0]
    ih1 = 1.0 / h1
    h_out[...] = 0.5 * (h0 + h1 + STEP * w1)
    h_copy = pltpu.make_async_copy(h_out, h_hbm, sems.at[4])
    h_copy.start()
    for v in range(2):
        (a1,) = fluxes(strip_s[v], (1,))
        for f in range(5):
            pt[f, v] = strip_ends(a1[f])

    def halo_flux_two(l):
        (a3,) = fluxes([sz[f, l] for f in range(5)], (3,))
        todo = [(f3, (f, l + 2, slice(16, 24)), f3x[f, l + 2]) for f in range(5)]
        return todo + [x for f in range(5) for x in put_halo(f3, f, l + 2, a3[f])]

    def final(l):
        eta, shift, todo = eta_of(l), patch_shift(l), []
        for f in range(5):
            dx = d_ends(f1x[f, l + 2], pltpu.roll(pt[f, l >> 3], shift, 1))
            da = d_around(f3, f, l + 2)
            dn, dg = d_normal(plane_at(f2x, f), l + 2), d_normal(plane_at(gx, f), l + 2)
            rate = ih1 * (eta * dg - dn) - (dx + da)
            todo.append((out, (f, l), 0.5 * (q[f, l] + sx[f, l + 2] + C * rate)))
        return todo

    together(4, (0, 4, halo_flux_two))

    def out_copy(i):
        part = (slice(None), pl.ds(4 * i, 4))
        return pltpu.make_async_copy(out.at[part], out_hbm.at[part], sems.at[i])

    together(4, (0, 4, final), after=lambda i: out_copy(i).start())
    for i in range(4):
        out_copy(i).wait()
    h_copy.wait()


def call(body, ins, outs, scratch=(), sems=0, space=VM, out_space=VM):
    shapes = tuple(jax.ShapeDtypeStruct(s, F32) for s in outs)
    return pl.pallas_call(
        body,
        out_shape=shapes,
        in_specs=[space] * len(ins),
        out_specs=tuple([out_space] * len(shapes)),
        scratch_shapes=[pltpu.VMEM(s, F32) for s in scratch] + [pltpu.SemaphoreType.DMA((sems,))] * (sems > 0),
        compiler_params=pltpu.CompilerParams(vmem_limit_bytes=40 * 1024 * 1024),
    )(*ins)


def where_am_i():
    return lax.axis_index("sx"), lax.axis_size("sx")


def stage_rows(*refs):
    pack_rows(lax.axis_index("az") % 2 == 1, *refs)


def stage_own(*refs):
    own_parts(*refs)


def stage_columns(*refs):
    pack_columns(lax.axis_index("sx") % 2 == 0, *refs)


def stage_corners(*refs):
    pack_corners(lax.axis_index("sx") % 2 == 0, *refs)


def stage_second(*refs):
    pack_second(lax.axis_index("az") % 2 == 1, lax.axis_index("wn"), *where_am_i(), *refs)


def stage_far(*refs):
    pack_far(lax.axis_index("wn"), *refs)


def stage_prepare(*refs):
    prepare(lax.axis_index("wn"), *refs)


def stage_own_section(*refs):
    advance_own(lax.axis_index("wn"), *refs)


def stage_advance(*refs):
    advance(lax.axis_index("wn"), *where_am_i(), *refs)


def swaps(size, start, wrap):
    pairs = [(i, (i + 1) % size) for i in range(start, size if wrap else size - 1, 2)]
    return pairs + [(j, i) for i, j in pairs]


def per_device(fields, height, behind):
    around = lax.axis_size("az")
    tiles = lax.axis_size("sx")
    plane = (8, 128)
    *own, one, two = call(
        stage_rows,
        [pltpu.with_memory_space_constraint(x, pltpu.HBM) for x in (fields, height, behind)],
        [fields.shape, height.shape, behind.shape] + [(HALF, *plane)] * 2,
        sems=3,
        space=HBM,
    )
    a2 = lax.ppermute(two, "az", swaps(around, 1, True))
    a1 = lax.ppermute(one, "az", swaps(around, 0, True))
    right, left, one, two = call(stage_columns, own, [(3, *plane)] * 4)
    s2 = lax.ppermute(two, "sx", swaps(tiles, 1, False))
    s1 = lax.ppermute(one, "sx", swaps(tiles, 0, False))
    parts = call(stage_own, (own[0], right), [(5, NL, *plane)] * 5, [(5, NL, *plane)])
    halo, strips, w, near, far, slope = call(
        stage_second,
        (*own, a1, a2, right, left, s1, s2, parts[3]),
        [(NP, *plane), (UNITS, *plane), (4, *plane), (31, *plane), (27, *plane), (3, *plane)],
        [(27, *plane)] * 2,
    )
    z_right, z_left, one, two = call(stage_corners, (halo,), [(3, *plane)] * 4)
    near = lax.ppermute(near, "wn", [(0, 1), (1, 0), (2, 3), (3, 2)])
    s2 = lax.ppermute(two, "sx", swaps(tiles, 1, False))
    s1 = lax.ppermute(one, "sx", swaps(tiles, 0, False))
    (far,) = call(stage_far, (far, w, near, two), [(31, *plane)])
    parts = call(
        stage_prepare,
        (own[0], own[1], halo, strips, slope, *parts, far),
        [(5, NL, *plane)] * 5 + [(5, *plane)],
        [(5, NL, *plane)] * 4 + [(5, NL, 40, 128), (5, 2, *plane)],
    )
    far = lax.ppermute(far, "wn", [(1, 2), (2, 1), (3, 0)])
    tx, bx, tz, bz, ez, ghost = parts
    section = call(
        stage_own_section,
        (*own, halo, strips, w, near, far, slope, tx, bx, ghost),
        [(5, 20, *plane)] * 5,
        [(5, 16, *plane)] * 4 + [(5, 16, 40, 128), (5, *plane)],
    )
    return call(
        stage_advance,
        (*own, halo, strips, w, near, far, z_right, z_left, s1, s2, slope, tz, bz, ez, ghost, *section),
        [(5, NL, *plane), plane],
        [(5, 12, *plane)] * 3
        + [(5, 20, 40, 128)]
        + [(5, NL, *plane), (5, 3, *plane), (5, 2, *plane), (UNITS, *plane), (5, NL, *plane), plane],
        sems=5,
        out_space=HBM,
    )


def solution(mesh):
    in_specs = (P(None, "wn", "az", "sx"), P("az", "sx"), P(None, "az", "sx"))
    out_specs = (P(None, "wn", "az", "sx"), P("az", "sx"))
    return jax.shard_map(
        per_device, mesh=mesh, in_specs=in_specs, out_specs=out_specs, check_vma=False
    )
```
